32 devices in a mesh: dp: 4 (over z), ctx: 2 (over y), tensor: 4 (over x, core).
Axes of the slice: x: 2, y: 2, z: 4, core: 2. Of those that a mesh axis runs over, the one named last changes fastest.
Arguments:
- tokens: bfloat16 [16384, 2048], P(('dp', 'ctx')), may hold values from -6 to 6
- cotangent: bfloat16 [16384, 2048], P(('dp', 'ctx')), may hold values from -6 to 6
- lengths: int32 [4, 6], P('dp'), may hold values from 1 to 2048, as said below
- offsets: int32 [4, 32], P('dp'), may hold values from 0 to 3968, as said below
- ln1_gain: bfloat16 [2048], replicated, may hold values from 0.5 to 1.5
- ln1_bias: bfloat16 [2048], replicated, may hold values from -1 to 1
- w_qkv: bfloat16 [2048, 3, 2048], P(('dp', 'ctx'), None, 'tensor'), may hold values from -0.125 to 0.125
- b_qkv: bfloat16 [3, 2048], P(None, 'tensor'), may hold values from -2.5 to 2.5
- w_out: bfloat16 [2048, 2048], P('tensor', ('dp', 'ctx')), may hold values from -2 to 2
- ln2_gain: bfloat16 [2048], replicated, may hold values from 0.5 to 1.5
- ln2_bias: bfloat16 [2048], replicated, may hold values from -1 to 1
- w_gate_up: bfloat16 [2048, 2, 5632], P(('dp', 'ctx'), None, 'tensor'), may hold values from -0.125 to 0.125
- w_down: bfloat16 [5632, 2048], P('tensor', ('dp', 'ctx')), may hold values from -0.4375 to 0.4375
Outputs:
- output: bfloat16 [16384, 2048], P(('dp', 'ctx'))
- grad_tokens: bfloat16 [16384, 2048], P(('dp', 'ctx'))
- grad_ln1_gain: float32 [2048], replicated
- grad_ln1_bias: float32 [2048], replicated
- grad_w_qkv: float32 [2048, 3, 2048], P(('dp', 'ctx'), None, 'tensor')
- grad_b_qkv: float32 [3, 2048], P(None, 'tensor')
- grad_w_out: float32 [2048, 2048], P('tensor', ('dp', 'ctx'))
- grad_ln2_gain: float32 [2048], replicated
- grad_ln2_bias: float32 [2048], replicated
- grad_w_gate_up: float32 [2048, 2, 5632], P(('dp', 'ctx'), None, 'tensor')
- grad_w_down: float32 [5632, 2048], P('tensor', ('dp', 'ctx'))
The draws below stay inside these ranges and needn't reach their ends.
Inputs may be any that keep to these rules, and one draw needn't show every extreme that they name: Each row lists one group's sequence lengths in stream order; they sum to 4096, and the first is 2048, the longest of the row. `offsets`: each row is 128 times a permutation of 0 to 31.
All inputs are finite; a program needn't handle non-finite values.
Results may differ from the reference program's by a relative error of at most 0.025.
Values may be sent and summed in bfloat16 or wider, within the bound.
A program may use at most 768 MiB of HBM per device.

```python
import math
from functools import partial
import jax
import jax.numpy as jnp
from jax import lax

D = 2048
H = 32
HD = 64
ROT = 16
FF = 5632
TILE = 128
SEQS = 6
LONG = 2048
STREAM = 4096
NT = 32
TD = 16
TOKENS = 16384
N_DP = 4


def draw_lengths(key, part):
    key = jax.random.fold_in(key, 11)
    shares = jax.random.randint(key, (N_DP, SEQS - 1), 1, 9).astype(jnp.int32)
    running = jnp.cumsum(shares, axis=1).astype(jnp.int32)
    bounds = (LONG * running // running[:, -1:]).astype(jnp.int32)
    earlier = jnp.concatenate([jnp.zeros((N_DP, 1), jnp.int32), bounds[:, :-1]], axis=1)
    longest = jnp.full((N_DP, 1), LONG, jnp.int32)
    return jnp.concatenate([longest, bounds - earlier], axis=1).astype(jnp.int32)


def draw_offsets(key, part):
    key = jax.random.fold_in(key, 23)
    half_tiles = NT // 2
    tile_devices = NT // TD

    def one_group(group_key):
        lead_key, rest_key = jax.random.split(group_key)
        long_tiles = jax.random.permutation(lead_key, jnp.arange(half_tiles, dtype=jnp.int32))
        others = jnp.concatenate([long_tiles[tile_devices:], jnp.arange(half_tiles, NT, dtype=jnp.int32)])
        others = jax.random.permutation(rest_key, others)
        slots = jnp.concatenate([long_tiles[:tile_devices, None], others.reshape(tile_devices, TD - 1)], axis=1)
        return slots.reshape(NT) * TILE
    return jax.vmap(one_group)(jax.random.split(key, N_DP)).astype(jnp.int32)


def block_levels(key, dims, cuts, low, top_value):
    level = 1.0
    for dim, blocks in cuts:
        draws = jax.random.uniform(jax.random.fold_in(jax.random.fold_in(key, 6), dim), (blocks,), jnp.float32, low / len(cuts), top_value / len(cuts))
        level = level * jnp.repeat(jnp.exp(draws), dims[dim] // blocks).reshape((-1,) + (1,) * (len(dims) - 1 - dim))
    return level


def bell_draw(stream_key, extent, scale, limit, cuts=(), kind=jnp.bfloat16):
    level = block_levels(stream_key, extent, cuts, -0.22, 0.18) if cuts else 1.0
    values = jax.random.normal(stream_key, extent, jnp.float32) * scale * level
    return jnp.minimum(jnp.maximum(values, -limit), limit).astype(kind)


def setup_inputs(seed: int = 0) -> dict:
    splits = jax.random.split(jax.random.key(seed), 14)
    return {
        "tokens": bell_draw(splits[0], (TOKENS, D), 1.0, 6.0, ((0, 8),)),
        "cotangent": bell_draw(splits[1], (TOKENS, D), 1.0, 6.0, ((0, 8),)),
        "lengths": draw_lengths(jax.random.fold_in(splits[13], 71), 0),
        "offsets": draw_offsets(jax.random.fold_in(splits[13], 71), 0),
        "ln1_gain": jnp.clip(1.0 + 0.1 * jax.random.normal(splits[4], (D,), jnp.float32), 0.5, 1.5).astype(jnp.bfloat16),
        "ln1_bias": bell_draw(splits[5], (D,), 0.2, 1.0),
        "w_qkv": bell_draw(splits[6], (D, 3, D), D ** -0.5, 0.125, ((0, 8), (2, 4))),
        "b_qkv": bell_draw(splits[7], (3, D), 0.5, 2.5, ((1, 4),)),
        "w_out": bell_draw(splits[8], (D, D), (max(D // 256, 1)) ** -0.5, 2.0, ((0, 4), (1, 8))),
        "ln2_gain": jnp.clip(1.0 + 0.1 * jax.random.normal(splits[9], (D,), jnp.float32), 0.5, 1.5).astype(jnp.bfloat16),
        "ln2_bias": bell_draw(splits[10], (D,), 0.2, 1.0),
        "w_gate_up": bell_draw(splits[11], (D, 2, FF), D ** -0.5, 0.125, ((0, 8), (2, 4))),
        "w_down": bell_draw(splits[12], (FF, D), (max(FF // 32, 1)) ** -0.5, 0.4375, ((0, 4), (1, 8))),
    }


highest = lax.Precision.HIGHEST

@jax.custom_vjp
def low(v):
    return lax.optimization_barrier(v.astype(jnp.bfloat16)).astype(jnp.float32)

@jax.custom_vjp
def low_back(v):
    return v

def low_keep(v):
    return (low(v), None)

def low_pass(kept, grad):
    return (grad,)

def back_keep(v):
    return (v, None)

def back_low(kept, grad):
    return (low(grad),)
low.defvjp(low_keep, low_pass)
low_back.defvjp(back_keep, back_low)

def layer_norm(values, norm_gain, norm_shift):
    row_mean = lax.optimization_barrier(jnp.mean(values, axis=-1, keepdims=True))
    centred = values - row_mean
    spread = lax.optimization_barrier(jnp.mean(centred * centred, axis=-1, keepdims=True))
    return centred * lax.rsqrt(spread + 1e-05) * norm_gain + norm_shift

def rotate(values, cosine, sine_table):
    half_rot = ROT // 2
    first_half = values[..., :half_rot]
    second_half = values[..., half_rot:ROT]
    return jnp.concatenate([first_half * cosine - second_half * sine_table, second_half * cosine + first_half * sine_table, values[..., ROT:]], axis=-1)

def rotary_tables(relative):
    half_rot = ROT // 2
    frequency = jnp.exp(jnp.arange(half_rot, dtype=jnp.float32) * (-2.0 * math.log(10000.0) / ROT))
    angles = relative.astype(jnp.float32)[..., None] * frequency
    return (jnp.cos(angles), jnp.sin(angles))

def group_attention(query, key, value, places, begins):
    block_rows = min(512, STREAM)
    block_count = STREAM // block_rows

    def one_block(bundle):
        query_block, query_place, query_begin = bundle
        raw = low_back(jnp.einsum('qhd,khd->hqk', query_block, key, precision=highest))
        scores = raw * HD ** (-0.5)
        visible = (places[None, :] <= query_place[:, None]) & (places[None, :] >= query_begin[:, None])
        masked = jnp.where(visible[None], scores, -1e+30)
        running_top = lax.optimization_barrier(jnp.max(masked, axis=-1, keepdims=True))
        expw = jnp.where(visible[None], jnp.exp(masked - running_top), 0.0)
        row_total = lax.optimization_barrier(jnp.sum(expw, axis=-1, keepdims=True))
        chances = low(expw / row_total)
        return jnp.einsum('hqk,khd->qhd', chances, value, precision=highest)
    mixed = lax.map(jax.checkpoint(one_block), (query.reshape(block_count, block_rows, H, HD), places.reshape(block_count, block_rows), begins.reshape(block_count, block_rows)))
    return mixed.reshape(STREAM, H, HD)

def forward(places, begins, cosine, sine_table, tokens, ln1_gain, ln1_bias, w_qkv, b_qkv, w_out, ln2_gain, ln2_bias, w_gate_up, w_down):
    normed1 = low(layer_norm(tokens, ln1_gain, ln1_bias))
    projected = low_back(jnp.einsum('td,dkf->tkf', normed1, w_qkv, precision=highest) + b_qkv[None])
    query = low(rotate(projected[:, 0].reshape(TOKENS, H, HD), cosine, sine_table))
    key = low(rotate(projected[:, 1].reshape(TOKENS, H, HD), cosine, sine_table))
    value = low(projected[:, 2].reshape(TOKENS, H, HD))

    def one_group(bundle):
        return group_attention(*bundle)
    attended = lax.map(one_group, (query.reshape(N_DP, STREAM, H, HD), key.reshape(N_DP, STREAM, H, HD), value.reshape(N_DP, STREAM, H, HD), places, begins))
    attended = low(low_back(attended.reshape(TOKENS, D)))
    branch = low_back(jnp.dot(attended, w_out, precision=highest))
    middle = tokens + branch
    normed2 = low(layer_norm(middle, ln2_gain, ln2_bias))
    gate_up = low_back(jnp.einsum('td,dkf->tkf', normed2, w_gate_up, precision=highest))
    hidden = low(jax.nn.silu(gate_up[:, 0]) * gate_up[:, 1])
    return middle + jnp.dot(hidden, w_down, precision=highest)

def reference(tokens, cotangent, lengths, offsets, ln1_gain, ln1_bias, w_qkv, b_qkv, w_out, ln2_gain, ln2_bias, w_gate_up, w_down):
    places = (offsets[:, :, None] + jnp.arange(TILE, dtype=jnp.int32)[None, None, :]).reshape(N_DP, STREAM).astype(jnp.int32)
    sequence_end = jnp.cumsum(lengths, axis=1).astype(jnp.int32)
    begins = lax.optimization_barrier(jnp.sum(jnp.where(places[:, :, None] >= sequence_end[:, None, :], lengths[:, None, :], 0), axis=2)).astype(jnp.int32)
    cosine, sine_table = rotary_tables((places - begins).reshape(TOKENS))
    cosine = cosine[:, None, :]
    sine_table = sine_table[:, None, :]
    floats = tuple((item.astype(jnp.float32) for item in (tokens, ln1_gain, ln1_bias, w_qkv, b_qkv, w_out, ln2_gain, ln2_bias, w_gate_up, w_down)))
    output, pullback = jax.vjp(partial(forward, places, begins, cosine, sine_table), *floats)
    grads = pullback(cotangent.astype(jnp.float32))
    return (output.astype(jnp.bfloat16), grads[0].astype(jnp.bfloat16), grads[1], grads[2], grads[3], grads[4], grads[5], grads[6], grads[7], grads[8], grads[9])
```

```python
import functools
import math

import jax
import jax.numpy as jnp
from jax import lax
from jax.experimental import pallas as pl
from jax.experimental.pallas import tpu as pltpu
from jax.sharding import PartitionSpec as P

HD = 64
ROT = 16
TILE = 128
VMEM_LIMIT = 60 * 1024 * 1024
LOW_SCORE = -1e30
START_TOP = -1e20


def layer_norm(values, norm_gain, norm_shift):
    row_mean = jnp.mean(values, axis=-1, keepdims=True)
    centred = values - row_mean
    spread = jnp.mean(centred * centred, axis=-1, keepdims=True)
    return centred * lax.rsqrt(spread + 1e-05) * norm_gain + norm_shift


def dot_f32(left, right, left_dim, right_dim):
    return lax.dot_general(
        left, right, (((left_dim,), (right_dim,)), ((), ())), preferred_element_type=jnp.float32
    )


def spin(values, cosine, sine, lanes):
    if lanes % 128 == 0:
        ahead = pltpu.roll(values, lanes - ROT // 2, 1)
        behind = pltpu.roll(values, ROT // 2, 1)
    else:
        half_rot = ROT // 2
        ahead = jnp.concatenate([values[:, half_rot:], values[:, :half_rot]], axis=1)
        behind = jnp.concatenate([values[:, -half_rot:], values[:, :-half_rot]], axis=1)
    lane = lax.broadcasted_iota(jnp.int32, values.shape, 1) % HD
    return values * cosine + jnp.where(lane < ROT // 2, ahead, behind) * sine


def begin_of(places, len_ref, seqs):
    begin = jnp.zeros_like(places)
    end = jnp.int32(0)
    for index in range(seqs):
        end = end + len_ref[index]
        begin = jnp.where(places >= end, end, begin)
    return begin


def begin_scalar(place, len_ref, seqs):
    begin = jnp.int32(0)
    end = jnp.int32(0)
    for index in range(seqs):
        end = end + len_ref[index]
        begin = jnp.where(place >= end, end, begin)
    return begin


def finish_scalar(place, len_ref, seqs):
    finish = jnp.int32(0)
    end = jnp.int32(0)
    for index in range(seqs):
        finish = jnp.where(place >= end, end + len_ref[index], finish)
        end = end + len_ref[index]
    return finish


def fold_rows(values):
    return jnp.sum(values.reshape(-1, 8, values.shape[1]), axis=0)


def head_masks(rows, lanes, heads):
    lane = lax.broadcasted_iota(jnp.int32, (rows, lanes), 1)
    return [(lane // HD) == index for index in range(heads)]


def attend_kernel(parts, tiles, width, stream, seqs, block, slot_ref, len_ref, *refs):
    qkv_ref, cos_ref, sin_ref = refs[:3]
    out_parts = refs[3 : parts + 3]
    sorted_ref, mixed_ref, lse_ref = refs[parts + 3 : parts + 6]
    loaded, value_aug, load_sem, store_sem = refs[parts + 6 :]
    lanes = min(128, width)
    per_group = lanes // HD
    groups = width // lanes

    @pl.loop(0, parts * tiles)
    def _(tile):
        place = pl.multiple_of(slot_ref[tile] * TILE, TILE)
        row = pl.multiple_of(tile * TILE, TILE)
        pltpu.make_async_copy(
            qkv_ref.at[pl.ds(row, TILE)], loaded.at[pl.ds(place, TILE)], load_sem
        ).start()

    pltpu.make_async_copy(loaded, loaded, load_sem).wait()

    @pl.loop(0, stream // 256)
    def _(step):
        rows = pl.ds(pl.multiple_of(step * 256, 256), 256)
        cosine, sine = cos_ref[rows, :], sin_ref[rows, :]
        masks = head_masks(256, lanes, per_group)
        for group in range(groups):
            cols = slice(group * lanes, (group + 1) * lanes)
            query = spin(loaded[rows, cols].astype(jnp.float32), cosine, sine, lanes)
            query = query.astype(jnp.bfloat16) * jnp.bfloat16(HD**-0.5)
            sorted_ref[rows, cols] = query
            cols = slice(width + group * lanes, width + (group + 1) * lanes)
            key = spin(loaded[rows, cols].astype(jnp.float32), cosine, sine, lanes)
            sorted_ref[rows, cols] = key.astype(jnp.bfloat16)
            cols = slice(2 * width + group * lanes, 2 * width + (group + 1) * lanes)
            value = loaded[rows, cols]
            sorted_ref[rows, cols] = value
            ones = jnp.ones((256, lanes), jnp.bfloat16)
            for index in range(per_group):
                head = group * per_group + index
                if per_group == 2:
                    value_aug[rows, head * 128 : (head + 1) * 128] = jnp.where(
                        masks[index], value, ones
                    )
                else:
                    value_aug[rows, head * 128 : head * 128 + HD] = value
                    value_aug[rows, head * 128 + HD : (head + 1) * 128] = ones

    for group in range(groups):
        cols = slice(group * lanes, (group + 1) * lanes)
        key_cols = slice(width + group * lanes, width + (group + 1) * lanes)

        @pl.loop(0, stream // block)
        def _(index):
            first = index * block
            rows = pl.ds(pl.multiple_of(first, block), block)
            query = sorted_ref[rows, cols]
            masks = head_masks(block, lanes, per_group)
            query_heads = [jnp.where(mask, query, jnp.bfloat16(0)) for mask in masks]
            place = first + lax.broadcasted_iota(jnp.int32, (block, 1), 0)
            begin = begin_of(place, len_ref, seqs)
            begin_low = begin_scalar(first, len_ref, seqs)
            begin_high = begin_scalar(first + block - 1, len_ref, seqs)

            def step(number, carry, masked):
                start = number * block
                key_rows = pl.ds(pl.multiple_of(start, block), block)
                key = sorted_ref[key_rows, key_cols]
                out = []
                for which in range(per_group):
                    top, total = carry[which]
                    head = group * per_group + which
                    scores = dot_f32(query_heads[which], key, 1, 1)
                    if masked:
                        key_place = start + lax.broadcasted_iota(jnp.int32, (1, block), 1)
                        visible = (key_place <= place) & (key_place >= begin)
                        scores = jnp.where(visible, scores, LOW_SCORE)
                    new_top = jnp.maximum(top, jnp.max(scores, axis=1, keepdims=True))
                    expw = jnp.exp(scores - new_top).astype(jnp.bfloat16)
                    shrink = jnp.exp(top - new_top)
                    mixed = dot_f32(
                        expw, value_aug[key_rows, head * 128 : (head + 1) * 128], 1, 0
                    )
                    out.append((new_top, total * shrink + mixed))
                return tuple(out)

            carry = tuple(
                (jnp.full((block, 1), START_TOP, jnp.float32), jnp.zeros((block, 128), jnp.float32))
                for _ in range(per_group)
            )
            first_block = begin_low // block
            inner = jnp.minimum((begin_high + block - 1) // block, index)
            carry = lax.fori_loop(
                first_block, inner, functools.partial(step, masked=True), carry
            )
            carry = lax.fori_loop(inner, index, functools.partial(step, masked=False), carry)
            carry = step(index, carry, True)
            lane = lax.broadcasted_iota(jnp.int32, (block, 128), 1)
            mixed, logs = [], []
            for which in range(per_group):
                top, total = carry[which]
                swapped = pltpu.roll(total, HD, 1)
                own = (lane // HD) == which
                sums = jnp.where(own, swapped, total)
                mixed.append(total / sums)
                logs.append(top + jnp.log(sums))
            if per_group == 2:
                both = jnp.where(lane < HD, mixed[0], mixed[1])
                log_both = jnp.where(lane < HD, logs[0], logs[1])
            else:
                both = mixed[0][:, :HD]
                log_both = logs[0]
            mixed_ref[rows, cols] = both.astype(jnp.bfloat16)
            turned = jnp.transpose(log_both)
            for which in range(per_group):
                head = group * per_group + which
                lse_ref[head : head + 1, rows] = turned[which * HD : which * HD + 1, :]

    for part in range(parts):

        @pl.loop(0, tiles)
        def _(tile, part=part):
            place = pl.multiple_of(slot_ref[part * tiles + tile] * TILE, TILE)
            row = pl.multiple_of(tile * TILE, TILE)
            pltpu.make_async_copy(
                mixed_ref.at[pl.ds(place, TILE)], out_parts[part].at[pl.ds(row, TILE)], store_sem
            ).start()

    pltpu.make_async_copy(mixed_ref, mixed_ref, store_sem).wait()


def attend(slots, lengths, projected, tables, count):
    stream, triple = projected.shape
    rows = stream // count
    width = triple // 3
    heads = width // HD
    block = min(512, stream)
    anywhere = pl.BlockSpec(memory_space=pl.ANY)
    whole = pl.BlockSpec(memory_space=pltpu.VMEM)
    kernel = functools.partial(
        attend_kernel, count, rows // TILE, width, stream, lengths.shape[0], block
    )
    pairs = stream * stream // 3 * heads
    outs = pl.pallas_call(
        kernel,
        name="attention_forward",
        out_shape=[jax.ShapeDtypeStruct((rows, width), jnp.bfloat16)] * count
        + [
            jax.ShapeDtypeStruct((stream, triple), jnp.bfloat16),
            jax.ShapeDtypeStruct((stream, width), jnp.bfloat16),
            jax.ShapeDtypeStruct((max(heads, 8), stream), jnp.float32),
        ],
        in_specs=[pl.BlockSpec(memory_space=pltpu.SMEM)] * 2 + [anywhere, whole, whole],
        out_specs=[anywhere] * count + [whole] * 3,
        scratch_shapes=[
            pltpu.VMEM((stream, triple), jnp.bfloat16),
            pltpu.VMEM((stream, heads * 128), jnp.bfloat16),
            pltpu.SemaphoreType.DMA,
            pltpu.SemaphoreType.DMA,
        ],
        compiler_params=pltpu.CompilerParams(vmem_limit_bytes=VMEM_LIMIT),
        cost_estimate=pl.CostEstimate(
            flops=pairs * 4 * 256, bytes_accessed=stream * width * 20, transcendentals=pairs
        ),
    )(slots, lengths, projected, *tables)
    return outs[:count], outs[count], outs[count + 1], outs[count + 2]


def attend_back_kernel(
    given, column, width, stream, seqs, block, slot_ref, len_ref, *refs
):
    back_parts = refs[:given]
    sorted_ref, mixed_ref, lse_ref, cos_ref, sin_ref, out_ref, sums_ref = refs[given : given + 7]
    back, grads, query_grad, delta, load_sem, store_sem = refs[given + 7 :]
    given_tiles = stream // TILE // given
    lanes = min(128, width)
    per_group = lanes // HD
    groups = width // lanes
    for part in range(given):

        @pl.loop(0, given_tiles)
        def _(tile, part=part):
            place = pl.multiple_of(slot_ref[part * given_tiles + tile] * TILE, TILE)
            row = pl.multiple_of(tile * TILE, TILE)
            pltpu.make_async_copy(
                back_parts[part].at[pl.ds(row, TILE), pl.ds(column, width)],
                back.at[pl.ds(place, TILE)],
                load_sem,
            ).start()

    pltpu.make_async_copy(back, back, load_sem).wait()

    for group in range(groups):
        cols = slice(group * lanes, (group + 1) * lanes)
        key_cols = slice(width + group * lanes, width + (group + 1) * lanes)
        value_cols = slice(2 * width + group * lanes, 2 * width + (group + 1) * lanes)
        query_grad[...] = jnp.zeros_like(query_grad)
        sums_ref[...] = jnp.zeros_like(sums_ref)

        @pl.loop(0, stream // block)
        def _(index):
            rows = pl.ds(pl.multiple_of(index * block, block), block)
            product = back[rows, cols].astype(jnp.float32) * mixed_ref[rows, cols].astype(
                jnp.float32
            )
            pick = (
                lax.broadcasted_iota(jnp.int32, (8, lanes), 1) // HD
                == lax.broadcasted_iota(jnp.int32, (8, lanes), 0)
            ).astype(jnp.float32)
            delta[:, rows] = lax.dot_general(
                pick,
                product,
                (((1,), (1,)), ((), ())),
                precision=lax.Precision.HIGHEST,
                preferred_element_type=jnp.float32,
            )

        @pl.loop(0, stream // block)
        def _(index):
            first = index * block
            key_rows = pl.ds(pl.multiple_of(first, block), block)
            key = sorted_ref[key_rows, key_cols]
            value = sorted_ref[key_rows, value_cols]
            masks = head_masks(block, lanes, per_group)
            key_heads = [jnp.where(mask, key, jnp.bfloat16(0)) for mask in masks]
            key_place = first + lax.broadcasted_iota(jnp.int32, (block, 1), 0)
            finish_low = finish_scalar(first, len_ref, seqs)
            finish_high = finish_scalar(first + block - 1, len_ref, seqs)

            def step(number, carry, masked):
                key_grad, value_grad = carry
                start = number * block
                rows = pl.ds(pl.multiple_of(start, block), block)
                query = sorted_ref[rows, cols]
                upstream = back[rows, cols]
                query_add = None
                if masked:
                    place = start + lax.broadcasted_iota(jnp.int32, (1, block), 1)
                    begin = begin_of(place, len_ref, seqs)
                    visible = (key_place <= place) & (key_place >= begin)
                for which in range(per_group):
                    head = group * per_group + which
                    query_head = jnp.where(masks[which], query, jnp.bfloat16(0))
                    back_head = jnp.where(masks[which], upstream, jnp.bfloat16(0))
                    scores = dot_f32(key, query_head, 1, 1)
                    if masked:
                        scores = jnp.where(visible, scores, LOW_SCORE)
                    chances = jnp.exp(scores - lse_ref[head : head + 1, rows])
                    d_chances = dot_f32(value, back_head, 1, 1)
                    d_raw = (chances * (d_chances - delta[which : which + 1, rows])).astype(
                        jnp.bfloat16
                    )
                    value_grad = value_grad + dot_f32(
                        chances.astype(jnp.bfloat16), back_head, 1, 0
                    )
                    key_grad = key_grad + dot_f32(d_raw, query_head, 1, 0)
                    part_add = dot_f32(d_raw, key_heads[which], 0, 0)
                    query_add = part_add if query_add is None else query_add + part_add
                query_grad[rows, :] += query_add
                return (key_grad, value_grad)

            zeros = jnp.zeros((block, lanes), jnp.float32)
            carry = step(index, (zeros, zeros), True)
            inner = jnp.maximum(finish_low // block, index + 1)
            last = jnp.maximum((finish_high + block - 1) // block, inner)
            carry = lax.fori_loop(
                index + 1, inner, functools.partial(step, masked=False), carry
            )
            carry = lax.fori_loop(inner, last, functools.partial(step, masked=True), carry)
            key_grad = spin(carry[0], cos_ref[key_rows, :], -sin_ref[key_rows, :], lanes)
            grads[key_rows, key_cols] = key_grad.astype(jnp.bfloat16)
            grads[key_rows, value_cols] = carry[1].astype(jnp.bfloat16)
            sums_ref[:, key_cols] += fold_rows(key_grad)
            sums_ref[:, value_cols] += fold_rows(carry[1])

        @pl.loop(0, stream // 256)
        def _(step):
            rows = pl.ds(pl.multiple_of(step * 256, 256), 256)
            turned = spin(query_grad[rows, :], cos_ref[rows, :], -sin_ref[rows, :], lanes)
            turned = turned * (HD**-0.5)
            grads[rows, cols] = turned.astype(jnp.bfloat16)
            sums_ref[:, cols] += fold_rows(turned)

    @pl.loop(0, stream // TILE)
    def _(tile):
        place = pl.multiple_of(slot_ref[tile] * TILE, TILE)
        row = pl.multiple_of(tile * TILE, TILE)
        pltpu.make_async_copy(
            grads.at[pl.ds(place, TILE)], out_ref.at[pl.ds(row, TILE)], store_sem
        ).start()

    pltpu.make_async_copy(grads, grads, store_sem).wait()


def attend_back(slots, lengths, parts, column, kept, mixed, lse, tables):
    stream, width = mixed.shape
    heads = width // HD
    block = min(512, stream)
    lanes = min(128, width)
    anywhere = pl.BlockSpec(memory_space=pl.ANY)
    whole = pl.BlockSpec(memory_space=pltpu.VMEM)
    kernel = functools.partial(
        attend_back_kernel, len(parts), column, width, stream, lengths.shape[0], block
    )
    pairs = stream * stream // 3 * heads
    return pl.pallas_call(
        kernel,
        name="attention_backward",
        out_shape=[
            jax.ShapeDtypeStruct((stream, 3 * width), jnp.bfloat16),
            jax.ShapeDtypeStruct((8, 3 * width), jnp.float32),
        ],
        in_specs=[pl.BlockSpec(memory_space=pltpu.SMEM)] * 2
        + [anywhere] * len(parts)
        + [whole] * 5,
        out_specs=[anywhere, whole],
        scratch_shapes=[
            pltpu.VMEM((stream, width), jnp.bfloat16),
            pltpu.VMEM((stream, 3 * width), jnp.bfloat16),
            pltpu.VMEM((stream, lanes), jnp.float32),
            pltpu.VMEM((8, stream), jnp.float32),
            pltpu.SemaphoreType.DMA,
            pltpu.SemaphoreType.DMA,
        ],
        compiler_params=pltpu.CompilerParams(vmem_limit_bytes=VMEM_LIMIT),
        cost_estimate=pl.CostEstimate(
            flops=pairs * 10 * 256, bytes_accessed=stream * width * 20, transcendentals=pairs
        ),
    )(slots, lengths, *parts, kept, mixed, lse, *tables)


def rotary_kernel(lanes, table_ref, cos_ref, sin_ref):
    half_rot = ROT // 2
    lane = lax.broadcasted_iota(jnp.int32, (half_rot, lanes), 1) % HD
    entry = lax.broadcasted_iota(jnp.int32, (half_rot, lanes), 0)
    first, second = lane == entry, lane == entry + half_rot
    pick_cos = (first | second).astype(jnp.float32)
    pick_sin = second.astype(jnp.float32) - first.astype(jnp.float32)

    def spread(values, pick):
        return lax.dot_general(
            values,
            pick,
            (((0,), (0,)), ((), ())),
            precision=lax.Precision.HIGHEST,
            preferred_element_type=jnp.float32,
        )

    still = (lax.broadcasted_iota(jnp.int32, (1, lanes), 1) % HD >= ROT).astype(jnp.float32)
    cos_ref[...] = spread(table_ref[:half_rot, :], pick_cos) + still
    sin_ref[...] = spread(table_ref[half_rot:, :], pick_sin)


def rotary_tables(table, lanes):
    stream = table.shape[1]
    block = min(512, stream)
    return pl.pallas_call(
        functools.partial(rotary_kernel, lanes),
        name="rotary_tables",
        grid=(stream // block,),
        in_specs=[pl.BlockSpec((ROT, block), lambda step: (0, step))],
        out_specs=[pl.BlockSpec((block, lanes), lambda step: (step, 0))] * 2,
        out_shape=[jax.ShapeDtypeStruct((stream, lanes), jnp.float32)] * 2,
        cost_estimate=pl.CostEstimate(
            flops=stream * lanes * 100, bytes_accessed=stream * lanes * 8, transcendentals=0
        ),
    )(table)


def project_kernel(sources, groups, slab, map_ref, *refs):
    inputs = refs[:sources]
    gain_ref, shift_ref, weight_ref, bias_ref = refs[sources : sources + 4]
    outs = refs[len(refs) - groups - 1 :]

    def run(source):
        values = source[...].astype(jnp.float32)
        normed = layer_norm(values, gain_ref[...], shift_ref[...]).astype(jnp.bfloat16)
        outs[0][...] = normed
        result = dot_f32(normed, weight_ref[...], 1, 0) + bias_ref[...]
        for group in range(groups):
            outs[1 + group][...] = result[:, group * slab : (group + 1) * slab].astype(
                jnp.bfloat16
            )

    if sources == 1:
        run(inputs[0])
    else:
        for index in range(sources):

            @pl.when(pl.program_id(0) == index)
            def _(index=index):
                run(inputs[index])


def project(blocks, sources, gain, shift, weight, bias, groups, rows, first, kept):
    features, triple = weight.shape
    slab = triple // groups
    count = len(sources)
    steps = blocks.shape[0] if count == 1 else count
    size = math.gcd(256, sources[0].shape[0])
    kept = [] if kept is None else kept
    fixed = lambda step, order: (0, 0)
    placed = lambda step, order: (first + step, 0)
    if count == 1:
        specs = [pl.BlockSpec((size, features), lambda step, order: (order[step], 0))]
    else:
        specs = [pl.BlockSpec((size, features), fixed)] * count
    specs += [
        pl.BlockSpec((1, features), fixed),
        pl.BlockSpec((1, features), fixed),
        pl.BlockSpec((features, triple), fixed),
        pl.BlockSpec((1, triple), fixed),
    ]
    specs += [pl.BlockSpec(memory_space=pl.ANY)] * len(kept)
    work = steps * size
    return pl.pallas_call(
        functools.partial(project_kernel, count, groups, slab),
        name="norm_project",
        grid_spec=pltpu.PrefetchScalarGridSpec(
            num_scalar_prefetch=1,
            grid=(steps,),
            in_specs=specs,
            out_specs=[pl.BlockSpec((size, features), placed)]
            + [pl.BlockSpec((size, slab), placed)] * groups,
        ),
        out_shape=[jax.ShapeDtypeStruct((rows, features), jnp.bfloat16)]
        + [jax.ShapeDtypeStruct((rows, slab), jnp.bfloat16)] * groups,
        input_output_aliases={count + 5 + index: index for index in range(len(kept))},
        compiler_params=pltpu.CompilerParams(vmem_limit_bytes=VMEM_LIMIT),
        cost_estimate=pl.CostEstimate(
            flops=2 * work * features * triple,
            bytes_accessed=work * features * 4 + features * triple * 2,
            transcendentals=0,
        ),
    )(blocks, *sources, gain, shift, weight, bias, *kept)


def place_kernel(count, at_ref, *refs):
    for index in range(count):

        @pl.when(pl.program_id(0) == index)
        def _(index=index):
            refs[count][...] = refs[index][...]


def place_rows(at, pieces):
    size, features = pieces[0].shape
    count = len(pieces)
    return pl.pallas_call(
        functools.partial(place_kernel, count),
        name="place_rows",
        grid_spec=pltpu.PrefetchScalarGridSpec(
            num_scalar_prefetch=1,
            grid=(count,),
            in_specs=[once((size, features))] * count,
            out_specs=pl.BlockSpec((size, features), lambda step, order: (order[step], 0)),
        ),
        out_shape=jax.ShapeDtypeStruct((size * count, features), pieces[0].dtype),
        compiler_params=pltpu.CompilerParams(vmem_limit_bytes=VMEM_LIMIT),
        cost_estimate=pl.CostEstimate(
            flops=0, bytes_accessed=size * count * features * 4, transcendentals=0
        ),
    )(at, *pieces)


def once(shape):
    return pl.BlockSpec(shape, lambda *_: (0, 0), pipeline_mode=pl.Buffered(1))


def column_tiles(columns):
    return [(start, min(512, columns - start)) for start in range(0, columns, 512)]


def store_half(step, keep_ref, send_ref, cols, values):
    values = values.astype(jnp.bfloat16)

    @pl.when(step == 0)
    def _():
        send_ref[:, cols] = values

    @pl.when(step == 1)
    def _():
        keep_ref[:, cols] = values


def matmul_call(kernel, name, half, in_specs, out_specs, out_shape, scratch, flops, args):
    bytes_moved = sum(a.size * a.dtype.itemsize for a in args)
    bytes_moved += sum(math.prod(o.shape) * o.dtype.itemsize for o in out_shape)
    return pl.pallas_call(
        kernel,
        name=name,
        grid=(2,),
        in_specs=in_specs,
        out_specs=out_specs,
        out_shape=out_shape,
        scratch_shapes=scratch,
        compiler_params=pltpu.CompilerParams(vmem_limit_bytes=VMEM_LIMIT),
        cost_estimate=pl.CostEstimate(flops=flops, bytes_accessed=bytes_moved, transcendentals=0),
    )(*args)


def low_shape(*shape):
    return jax.ShapeDtypeStruct(shape, jnp.bfloat16)


def out_kernel(count, groups, lanes, holder_ref, *refs):
    parts = refs[: count * groups]
    weight_ref, keep_ref, send_ref, attended_ref = refs[count * groups :]
    step = pl.program_id(0)
    for s in range(count):
        for c in range(count):

            @pl.when(holder_ref[s] == c)
            def _(s=s, c=c):
                for group in range(groups):
                    first = (c * groups + group) * lanes
                    attended_ref[:, first : first + lanes] = parts[s * groups + group][...]

    for start, size in column_tiles(weight_ref.shape[1]):
        cols = slice(start, start + size)
        result = dot_f32(attended_ref[...], weight_ref[:, cols], 1, 0)
        store_half(step, keep_ref, send_ref, cols, result)


def project_out(holders, parts, count, groups, weight, chunk, half):
    width, features = weight.shape
    lanes = parts[0].shape[1]
    part_spec = pl.BlockSpec((half, lanes), lambda step: (chunk * 2 + 1 - step, 0))
    return matmul_call(
        functools.partial(out_kernel, count, groups, lanes),
        "project_out",
        half,
        [pl.BlockSpec(memory_space=pltpu.SMEM)]
        + [part_spec] * len(parts)
        + [once((width, features))],
        [
            pl.BlockSpec((half, features), lambda step: (0, 0)),
            pl.BlockSpec((half, features), lambda step: (0, 0)),
            pl.BlockSpec((half, width), lambda step: (1 - step, 0)),
        ],
        [low_shape(half, features), low_shape(half, features), low_shape(2 * half, width)],
        [],
        4 * half * features * width,
        (holders, *parts, weight),
    )


def collect(step, pieces, out_ref, first_step):
    half = len(pieces) // 2
    size = pieces[0].shape[0]
    for number in range(2):

        @pl.when(step == number)
        def _(number=number):
            chosen = pieces[half:] if number == first_step else pieces[:half]
            for index, piece in enumerate(chosen):
                out_ref[index * size : (index + 1) * size, :] = piece[...]


def feed_kernel(count, hidden, *refs):
    pieces = refs[:count]
    d_hidden_ref, weight_ref = refs[count : count + 2]
    normed_ref, hidden_ref, grad_ref, keep_ref, send_ref = refs[count + 2 : count + 7]
    weight, weight_sems, piece_sems = refs[count + 7 :]
    step = pl.program_id(0)
    size = pieces[0].shape[0]
    half = count // 2

    def piece_copy(index, number):
        row = index * size
        return pltpu.make_async_copy(
            pieces[half * (1 - number) + index],
            normed_ref.at[pl.ds(row, size)],
            piece_sems.at[index],
        )

    columns = [
        (first, width)
        for start, width in column_tiles(hidden)
        for first in (start, hidden + start)
    ]
    copies = [
        pltpu.make_async_copy(
            weight_ref.at[:, pl.ds(start, width)],
            weight.at[:, pl.ds(start, width)],
            weight_sems.at[number],
        )
        for number, (start, width) in enumerate(columns)
    ]

    @pl.when(step == 0)
    def _():
        for index in range(half):
            piece_copy(index, 0).start()
        for copy in copies:
            copy.start()
        for index in range(half):
            piece_copy(index, 0).wait()

    @pl.when(step == 1)
    def _():
        for index in range(half):
            piece_copy(index, 1).start()
        for index in range(half):
            piece_copy(index, 1).wait()

    for number, (start, width) in enumerate(column_tiles(hidden)):

        @pl.when(step == 0)
        def _(number=number):
            copies[2 * number].wait()
            copies[2 * number + 1].wait()

        gate_cols = slice(start, start + width)
        up_cols = slice(hidden + start, hidden + start + width)
        gate = dot_f32(normed_ref[...], weight[:, gate_cols], 1, 0)
        up = dot_f32(normed_ref[...], weight[:, up_cols], 1, 0)
        sigmoid = 1.0 / (1.0 + jnp.exp(-gate))
        silu = gate * sigmoid
        d_hidden = d_hidden_ref[:, gate_cols]
        hidden_ref[:, gate_cols] = (silu * up).astype(jnp.bfloat16)
        d_gate = d_hidden * up * sigmoid * (1.0 + gate * (1.0 - sigmoid))
        grad_ref[:, gate_cols] = d_gate.astype(jnp.bfloat16)
        grad_ref[:, up_cols] = (d_hidden * silu).astype(jnp.bfloat16)

    for start, width in column_tiles(weight.shape[0]):
        cols = slice(start, start + width)
        result = dot_f32(grad_ref[...], weight[cols, :], 1, 1)
        store_half(step, keep_ref, send_ref, cols, result)


def feed_forward(pieces, d_hidden, weight):
    share, features = pieces[0].shape
    half = share * len(pieces) // 2
    hidden = d_hidden.shape[1]
    placed = lambda step: (1 - step, 0)
    anywhere = pl.BlockSpec(memory_space=pl.ANY)
    copies = 2 * len(column_tiles(hidden))
    return matmul_call(
        functools.partial(feed_kernel, len(pieces), hidden),
        "feed_forward",
        half,
        [anywhere] * len(pieces) + [pl.BlockSpec((half, hidden), placed), anywhere],
        [
            pl.BlockSpec((half, features), placed),
            pl.BlockSpec((half, hidden), placed),
            pl.BlockSpec((half, 2 * hidden), placed),
            pl.BlockSpec((half, features), lambda step: (0, 0)),
            pl.BlockSpec((half, features), lambda step: (0, 0)),
        ],
        [
            low_shape(2 * half, features),
            low_shape(2 * half, hidden),
            low_shape(2 * half, 2 * hidden),
            low_shape(half, features),
            low_shape(half, features),
        ],
        [
            pltpu.VMEM((features, 2 * hidden), jnp.bfloat16),
            pltpu.SemaphoreType.DMA((copies,)),
            pltpu.SemaphoreType.DMA((len(pieces) // 2,)),
        ],
        16 * half * features * hidden,
        (*pieces, d_hidden, weight),
    )


def out_back_kernel(count, pieces, width, holder_ref, *refs):
    sources = refs[:pieces]
    weight_ref, gathered_ref = refs[pieces : pieces + 2]
    outs = refs[pieces + 2 : pieces + 2 + count]
    step = pl.program_id(0)
    collect(step, sources, gathered_ref, 0)
    result = dot_f32(gathered_ref[...], weight_ref[...], 1, 0).astype(jnp.bfloat16)
    for s in range(count):
        for c in range(count):

            @pl.when(holder_ref[s] == c)
            def _(s=s, c=c):
                outs[s][...] = result[:, c * width : (c + 1) * width]


def project_out_back(holders, pieces, weight, count):
    share, features = pieces[0].shape
    half = share * len(pieces) // 2
    total = weight.shape[1]
    width = total // count
    placed = lambda step: (1 - step, 0)
    outs = matmul_call(
        functools.partial(out_back_kernel, count, len(pieces), width),
        "project_out_back",
        half,
        [pl.BlockSpec(memory_space=pltpu.SMEM)]
        + [once((share, features))] * len(pieces)
        + [once((features, total))],
        [pl.BlockSpec((half, features), placed)] + [pl.BlockSpec((half, width), placed)] * count,
        [low_shape(2 * half, features)] + [low_shape(2 * half, width)] * count,
        [],
        4 * half * features * total,
        (holders, *pieces, weight),
    )
    return outs[0], list(outs[1:])


def norm_back_kernel(count, groups, slab, *refs):
    parts = refs[: count * groups]
    weights = refs[count * groups : count * groups + count]
    keep_ref, send_ref, joined = refs[count * groups + count :]
    step = pl.program_id(0)
    if groups > 1:
        for index, part in enumerate(parts):
            joined[:, index * slab : (index + 1) * slab] = part[...]

    for start, size in column_tiles(weights[0].shape[1]):
        cols = slice(start, start + size)
        total = None
        for s in range(count):
            if groups > 1:
                left = joined[:, s * groups * slab : (s + 1) * groups * slab]
            else:
                left = parts[s][...]
            product = dot_f32(left, weights[s][:, cols], 1, 0)
            total = product if total is None else total + product
        store_half(step, keep_ref, send_ref, cols, total)


def project_back(parts, weights, groups, chunk, half):
    wide, features = weights[0].shape
    count = len(weights)
    slab = wide // groups

    def spec(first):
        return pl.BlockSpec(
            (half, slab), lambda step: (first // half + chunk * 2 + 1 - step, 0)
        )

    return matmul_call(
        functools.partial(norm_back_kernel, count, groups, slab),
        "project_back",
        half,
        [spec(first) for _, first in parts] + [once((wide, features))] * count,
        [pl.BlockSpec((half, features), lambda step: (0, 0))] * 2,
        [low_shape(half, features)] * 2,
        [pltpu.VMEM((half, count * wide), jnp.bfloat16)],
        4 * half * features * wide * count,
        (*(array for array, _ in parts), *weights),
    )


def swap_bit(values, axis, bit):
    size = lax.axis_size(axis)
    return lax.ppermute(values, axis, [(i, i ^ (1 << bit)) for i in range(size)])


def sum_over_tensor(keep, send, bits):
    return sum_further(sum_first(keep, send), bits)


def sum_first(keep, send):
    return keep.astype(jnp.float32) + swap_bit(send, "tensor", 0).astype(jnp.float32)


def sum_further(total, bits):
    for bit in range(1, bits):
        half = total.shape[0] // 2
        arrived = swap_bit(total[half:].astype(jnp.bfloat16), "tensor", bit)
        total = total[:half] + arrived.astype(jnp.float32)
    return total


def gather_pieces(own, bits):
    return gather_rest(gather_first(own, bits), bits)


def gather_first(own, bits):
    return [own, swap_bit(own, "tensor", bits - 1)]


def gather_rest(pieces, bits):
    for bit in reversed(range(bits - 1)):
        pieces = pieces + [swap_bit(piece, "tensor", bit) for piece in pieces]
    return pieces


def butterfly(values):
    for axis in ("tensor", "ctx", "dp"):
        for bit in reversed(range(lax.axis_size(axis).bit_length() - 1)):
            values = values + swap_bit(values, axis, bit)
    return values


def shift_over(values, axis, shift):
    size = lax.axis_size(axis)
    return lax.ppermute(values, axis, [(i, (i - shift) % size) for i in range(size)])


def exchange(pieces):
    count = len(pieces)
    arrived = [pieces[0]] + [None] * (count - 1)
    for shift in range(1, count):
        arrived[count - shift] = shift_over(pieces[shift], "ctx", shift)
    return arrived


def take_block(values, index, size, axis):
    return lax.dynamic_slice_in_dim(values, index * size, size, axis=axis)


def body(
    tokens,
    cotangent,
    lengths,
    offsets,
    ln1_gain,
    ln1_bias,
    w_qkv,
    b_qkv,
    w_out,
    ln2_gain,
    ln2_bias,
    w_gate_up,
    w_down,
):
    f32, low = jnp.float32, jnp.bfloat16
    split = ("dp", "ctx")
    n_dp, n_ctx, n_tensor = (lax.axis_size(name) for name in ("dp", "ctx", "tensor"))
    my_dp, me, mine = (lax.axis_index(name) for name in ("dp", "ctx", "tensor"))
    bits = n_tensor.bit_length() - 1
    rows, features = tokens.shape
    quarter = rows // n_tensor
    chunks = 2 if quarter % (2 * TILE) == 0 else 1
    share = quarter // chunks
    block = rows // chunks
    heads_width = w_qkv.shape[2]
    width = heads_width // n_ctx
    lanes = min(128, width)
    groups = width // lanes
    slab = 3 * lanes
    hidden_width = w_down.shape[0]
    stream = rows * n_ctx
    tiles = rows // TILE
    order = [int(format(p, f"0{bits}b")[::-1], 2) for p in range(n_tensor)]
    quarters = [mine ^ item for item in order]
    holders = [(me - s) % n_ctx for s in range(n_ctx)]

    def own_share(values, chunk):
        return lax.dynamic_slice_in_dim(values, mine * quarter + chunk * share, share, axis=0)

    def rotated_chunk(values, chunk):
        return jnp.concatenate(
            [
                lax.dynamic_slice_in_dim(values, q * quarter + chunk * share, share, axis=0)
                for q in quarters
            ],
            axis=0,
        )

    share_at = jnp.stack(
        [quarters[p] * chunks + chunk for chunk in range(chunks) for p in range(n_tensor)]
    ).astype(jnp.int32)

    def unrotate(columns):
        return place_rows(share_at, [piece for pieces in columns for piece in pieces])

    qkv_local = (
        w_qkv.reshape(-1, 3, n_ctx, groups, lanes)
        .transpose(0, 2, 3, 1, 4)
        .reshape(-1, n_ctx, groups * slab)
    )
    depth = qkv_local.shape[0]
    from_ctx = exchange(
        [lax.dynamic_index_in_dim(qkv_local, c, 1, keepdims=False) for c in holders]
    )

    peer_pieces = [[None] * chunks for _ in range(n_ctx)]
    for chunk in range(chunks):
        own = own_share(tokens, chunk)
        for shift in range(1, n_ctx):
            arrived = shift_over(own, "ctx", shift)
            arrived, _ = lax.optimization_barrier((arrived, from_ctx))
            peer_pieces[n_ctx - shift][chunk] = gather_pieces(arrived, bits)

    piece_at = jnp.stack(
        [(my_dp + shift) % n_dp * n_ctx + c for c in holders for shift in range(n_dp)]
    ).astype(jnp.int32)

    def gather_rows(arrived, after=()):
        pieces = []
        for item in arrived:
            pieces.append(item)
            for _ in range(1, n_dp):
                item = shift_over(item, "dp", 1)
                pieces.append(item)
        pieces, _ = lax.optimization_barrier((pieces, after))
        return place_rows(piece_at, pieces)

    def scatter_first(partial, axis):
        bit = lax.axis_size(axis).bit_length() - 2
        half = partial.shape[0] // 2
        side = (lax.axis_index(axis) >> bit) & 1
        arrived = swap_bit(take_block(partial, 1 - side, half, 0).astype(low), axis, bit)
        return take_block(partial, side, half, 0), arrived

    def scatter_rest(halves, axis):
        partial = halves[0].astype(f32) + halves[1].astype(f32)
        for bit in reversed(range(lax.axis_size(axis).bit_length() - 2)):
            half = partial.shape[0] // 2
            side = (lax.axis_index(axis) >> bit) & 1
            arrived = swap_bit(take_block(partial, 1 - side, half, 0).astype(low), axis, bit)
            partial = take_block(partial, side, half, 0) + arrived.astype(f32)
        return partial

    lengths_row = lengths[0]
    offsets_row = offsets[0].reshape(n_ctx, n_tensor, chunks, share // TILE)
    rotated_offsets = jnp.stack(
        [lax.dynamic_index_in_dim(offsets_row, q, 1, keepdims=False) for q in quarters], axis=2
    ).reshape(n_ctx, tiles)
    slots = (
        jnp.concatenate([take_block(rotated_offsets, c, 1, 0) for c in holders], axis=0).reshape(-1)
        // TILE
    )
    place = jnp.arange(stream, dtype=jnp.int32)
    ends = jnp.cumsum(lengths_row)
    begin = jnp.sum(jnp.where(place[None, :] >= ends[:, None], lengths_row[:, None], 0), axis=0)
    half_rot = ROT // 2
    frequency = jnp.exp(jnp.arange(half_rot, dtype=f32) * (-2.0 * math.log(10000.0) / ROT))
    angles = frequency[:, None] * (place - begin).astype(f32)[None, :]
    table = rotary_tables(jnp.concatenate([jnp.cos(angles), jnp.sin(angles)], axis=0), lanes)

    tokens_own = [own_share(tokens, chunk) for chunk in range(chunks)]
    cotangents = [rotated_chunk(cotangent, chunk) for chunk in range(chunks)]
    gate_up_local = w_gate_up.reshape(-1, 2 * hidden_width)
    peers_half = [item[: n_tensor // 2] for items in peer_pieces[1:] for item in items]
    qkv_mine = gather_rows(
        from_ctx, (peers_half, table, slots, tokens_own, cotangents, gate_up_local)
    )
    out_full = lax.all_gather(w_out.T, split, axis=0, tiled=True)
    down_local, _ = lax.optimization_barrier((w_down.T, qkv_mine))
    down_full = lax.all_gather(down_local, split, axis=0, tiled=True)

    gain_one, shift_one = ln1_gain.astype(f32), ln1_bias.astype(f32)
    gain_two, shift_two = ln2_gain.astype(f32), ln2_bias.astype(f32)
    bias_mine = (
        take_block(b_qkv.reshape(3, n_ctx, groups, lanes), me, 1, 1)
        .transpose(1, 2, 0, 3)
        .reshape(1, -1)
        .astype(f32)
    )
    project_args = (gain_one[None], shift_one[None], qkv_mine, bias_mine, groups, stream)
    size = math.gcd(256, rows)
    if share >= size:
        own_blocks = jnp.stack(
            [share_at * (share // size) + i for i in range(share // size)], axis=1
        ).reshape(-1)
        projected = project(own_blocks, [tokens], *project_args, 0, None)
    else:
        own_rows = jnp.concatenate([rotated_chunk(tokens, c) for c in range(chunks)], axis=0)
        projected = project(
            jnp.arange(rows // size, dtype=jnp.int32), [own_rows], *project_args, 0, None
        )
    nothing = jnp.zeros((1,), jnp.int32)
    for s in range(1, n_ctx):
        for chunk in range(chunks):
            first = (s * rows + chunk * block) // share
            projected = project(nothing, peer_pieces[s][chunk], *project_args, first, projected)
    normed1 = projected[0]

    gate_up_local, _ = lax.optimization_barrier((gate_up_local, projected))
    gate_up_full = lax.all_gather(gate_up_local, split, axis=0, tiled=True)

    qkv_all = [qkv_mine] + [None] * (n_ctx - 1)
    for shift in range(1, n_ctx):
        qkv_all[n_ctx - shift] = shift_over(
            lax.optimization_barrier((qkv_mine, projected))[0], "ctx", shift
        )

    kept_attention, arrived_mixed = [], []
    for group in range(groups):
        mixed_parts, *kept = attend(slots, lengths_row, projected[1 + group], table, n_ctx)
        kept_attention.append(kept)
        arrived_mixed.append(exchange(mixed_parts))
    arrived_mixed, _ = lax.optimization_barrier((arrived_mixed, down_full))
    holders_at = jnp.stack(holders).astype(jnp.int32)
    mixed_parts = [arrived_mixed[group][s] for s in range(n_ctx) for group in range(groups)]

    def over_rows(lefts, rights):
        total = None
        for left, right in zip(lefts, rights):
            product = dot_f32(left, right, 0, 0)
            total = product if total is None else total + product
        return total.astype(low)

    tokens_own = [item.astype(f32) for item in tokens_own]
    middle, normed2, hidden, d_gate_up, d_middle, d_middle_low = ([] for _ in range(6))
    attended, arrived_normed2, arrived_middle, d_attended = [], [], [], []
    d_gain_two, d_shift_two = 0.0, 0.0
    out_turned = out_full.T
    d_hidden = [dot_f32(cotangents[chunk], down_full, 1, 0) for chunk in range(chunks)]
    for chunk in range(chunks):
        keep, send, joined = project_out(
            holders_at, mixed_parts, n_ctx, groups, out_turned, chunk, block // 2
        )
        attended.append(joined)
        total = tokens_own[chunk] + sum_over_tensor(keep, send, bits)
        total, _ = lax.optimization_barrier((total, (d_hidden, qkv_all)))
        middle.append(total)
        own = layer_norm(middle[chunk], gain_two, shift_two).astype(low)
        arrived_normed2.append(gather_pieces(own, bits))
    d_normed2_all = []
    for chunk in range(chunks):
        joined, hidden_chunk, grad_chunk, keep, send = feed_forward(
            arrived_normed2[chunk], d_hidden[chunk], gate_up_full
        )
        normed2.append(joined)
        hidden.append(hidden_chunk)
        d_gate_up.append(grad_chunk)
        send, _ = lax.optimization_barrier((send, d_normed2_all))
        total = sum_first(keep, send)
        if chunk + 1 < chunks:
            arrived_normed2[chunk + 1], _ = lax.optimization_barrier(
                (arrived_normed2[chunk + 1], total)
            )
        d_normed2_all.append(sum_further(total, bits))
    ready, _ = lax.optimization_barrier(((normed2[0], d_gate_up[0], hidden), total))
    grad_gate_up = dot_f32(ready[0], ready[1], 0, 0)
    grad_down = over_rows(cotangents, ready[2])
    for chunk in range(chunks):
        d_normed2 = d_normed2_all[chunk]
        if chunk:
            d_normed2, _ = lax.optimization_barrier(
                (d_normed2, (grad_gate_up, grad_down, arrived_middle))
            )
        _, norm_two_back = jax.vjp(layer_norm, middle[chunk], gain_two, shift_two)
        d_middle_norm, d_gain, d_shift = norm_two_back(d_normed2)
        d_gain_two, d_shift_two = d_gain_two + d_gain, d_shift_two + d_shift
        d_middle.append(cotangents[chunk][:share].astype(f32) + d_middle_norm)
        own = d_middle[chunk].astype(low)
        arrived_middle.append(gather_first(own, bits))
    later, _ = lax.optimization_barrier(((normed2[1:], d_gate_up[1:]), own))
    for left, right in zip(*later):
        grad_gate_up = grad_gate_up + dot_f32(left, right, 0, 0)
    grad_gate_up = grad_gate_up.astype(low)
    arrived_middle[-1], _ = lax.optimization_barrier((arrived_middle[-1], grad_gate_up))
    arrived_middle = [gather_rest(item, bits) for item in arrived_middle]
    for chunk in range(chunks):
        joined, sent = project_out_back(holders_at, arrived_middle[chunk], out_full, n_ctx)
        d_middle_low.append(joined)
        d_attended.append(sent)
    arrived_back = [exchange(sent) for sent in d_attended]
    back_parts = [arrived_back[chunk][s] for s in range(n_ctx) for chunk in range(chunks)]

    grad_down = lax.psum_scatter(grad_down, split, scatter_dimension=0, tiled=True)
    grad_gate_up = lax.psum_scatter(grad_gate_up, split, scatter_dimension=0, tiled=True)

    grad_out = scatter_first(over_rows(d_middle_low, attended), "dp")

    later, _ = lax.optimization_barrier((hidden, arrived_back[0]))
    feed_partial = [dot_f32(item, down_full, 1, 1).astype(low) for item in later]
    kept_feed, arrived_feed = [], []
    for chunk in range(chunks):
        partial = feed_partial[chunk]
        kept_feed.append(partial[: block // 2])
        send, _ = lax.optimization_barrier((partial[block // 2 :], d_attended))
        arrived_feed.append(sum_first(kept_feed[chunk], send))
    back_parts, arrived_feed = lax.optimization_barrier((back_parts, arrived_feed))
    output_shares = [
        (middle[chunk] + sum_further(arrived_feed[chunk], bits)).astype(low)
        for chunk in range(chunks)
    ]

    d_parts, partials, bias_sums = [], [], []
    for group in range(groups):
        d_group, sums = attend_back(
            slots, lengths_row, back_parts, group * lanes, *kept_attention[group], table
        )
        sent = [d_group[s * rows : (s + 1) * rows] for s in range(n_ctx)]
        sent, _ = lax.optimization_barrier((sent, d_parts))
        d_parts.append([d_group] + exchange(sent)[1:])
        bias_sums.append(jnp.sum(sums, axis=0))
        partials.append(dot_f32(normed1, d_group, 0, 0).astype(low))
        if group == 0:
            output_shares, _ = lax.optimization_barrier((output_shares, d_group))
            back_parts, output_shares = lax.optimization_barrier((back_parts, output_shares))
    output_pieces = gather_first(jnp.concatenate(output_shares, axis=0), bits)
    output_pieces, _ = lax.optimization_barrier((output_pieces, d_group))
    output_pieces = gather_rest(output_pieces, bits)
    output = place_rows(jnp.stack(quarters).astype(jnp.int32), output_pieces)
    qkv_turned = [item.T for item in qkv_all]
    if groups > 1:
        partials, qkv_turned, _ = lax.optimization_barrier(
            (partials, qkv_turned, (output, grad_out))
        )
    grad_qkv = scatter_first(jnp.concatenate(partials, axis=1), "dp")
    d_projected = [(d_parts[group][s], 0) for s in range(n_ctx) for group in range(groups)]
    d_normed1_all = []
    for chunk in range(chunks):
        keep, send = project_back(d_projected, qkv_turned, groups, chunk, block // 2)
        send, _ = lax.optimization_barrier((send, d_normed1_all))
        total = sum_first(keep, send)
        if chunk + 1 < chunks:
            qkv_turned, _ = lax.optimization_barrier((qkv_turned, total))
        d_normed1_all.append(sum_further(total, bits))
    token_pieces = []
    d_gain_one, d_shift_one = 0.0, 0.0
    for chunk in range(chunks):
        d_normed1 = d_normed1_all[chunk]
        _, norm_one_back = jax.vjp(layer_norm, tokens_own[chunk], gain_one, shift_one)
        d_input, d_gain, d_shift = norm_one_back(d_normed1)
        d_gain_one, d_shift_one = d_gain_one + d_gain, d_shift_one + d_shift
        token_pieces.append(gather_pieces((d_middle[chunk] + d_input).astype(low), bits))
    grad_out, grad_qkv, _ = lax.optimization_barrier(
        (grad_out, grad_qkv, [items[: n_tensor // 2] for items in token_pieces])
    )
    grad_down = grad_down.astype(f32).T
    grad_gate_up = grad_gate_up.astype(f32).reshape(-1, 2, hidden_width)
    token_pieces[-1], _ = lax.optimization_barrier((token_pieces[-1], (grad_down, grad_gate_up)))
    grad_tokens = unrotate(token_pieces)

    grad_out = scatter_rest(scatter_first(scatter_rest(grad_out, "dp"), "ctx"), "ctx")
    grad_qkv = scatter_rest(grad_qkv, "dp").astype(low)
    grad_qkv = exchange([take_block(grad_qkv, c, depth, 0) for c in holders])
    grad_qkv = jnp.stack(grad_qkv)[(me - jnp.arange(n_ctx)) % n_ctx]
    grad_qkv = (
        grad_qkv.reshape(n_ctx, depth, groups, 3, lanes)
        .transpose(1, 3, 0, 2, 4)
        .reshape(depth, 3, heads_width)
        .astype(f32)
    )

    bias_slots = jnp.zeros((n_tensor, n_ctx, groups * slab), f32)
    bias_slots = lax.dynamic_update_slice(
        bias_slots, jnp.concatenate(bias_sums)[None, None], (mine, me, 0)
    )
    small = [d_gain_one, d_shift_one, d_gain_two, d_shift_two, bias_slots.reshape(-1)]
    small = butterfly(jnp.concatenate(small).reshape(-1, 128)).reshape(-1)
    norms = [small[index * features : (index + 1) * features] for index in range(4)]
    bias_sum = take_block(small[4 * features :].reshape(n_tensor, -1), mine, 1, 0)
    bias_sum = (
        bias_sum.reshape(n_ctx, groups, 3, lanes).transpose(2, 0, 1, 3).reshape(3, heads_width)
    )
    return (
        output,
        grad_tokens,
        norms[0],
        norms[1],
        grad_qkv,
        bias_sum,
        grad_out.T,
        norms[2],
        norms[3],
        grad_gate_up,
        grad_down,
    )


def solution(mesh):
    placed = (
        P(("dp", "ctx"), None),
        P(("dp", "ctx"), None),
        P("dp", None),
        P("dp", None),
        P(),
        P(),
        P(("dp", "ctx"), None, "tensor"),
        P(None, "tensor"),
        P("tensor", ("dp", "ctx")),
        P(),
        P(),
        P(("dp", "ctx"), None, "tensor"),
        P("tensor", ("dp", "ctx")),
    )
    return jax.shard_map(
        body,
        mesh=mesh,
        in_specs=placed,
        out_specs=(
            P(("dp", "ctx"), None),
            P(("dp", "ctx"), None),
            P(),
            P(),
            P(("dp", "ctx"), None, "tensor"),
            P(None, "tensor"),
            P("tensor", ("dp", "ctx")),
            P(),
            P(),
            P(("dp", "ctx"), None, "tensor"),
            P("tensor", ("dp", "ctx")),
        ),
        check_vma=False,
    )
```

```python
import functools
import math

import jax
import jax.numpy as jnp
from jax import lax
from jax.experimental import pallas as pl
from jax.experimental.pallas import tpu as pltpu
from jax.sharding import PartitionSpec as P

HD = 64
ROT = 16
TILE = 128
VMEM_LIMIT = 60 * 1024 * 1024
LOW_SCORE = -1e30
START_TOP = -1e20


def layer_norm(values, norm_gain, norm_shift):
    row_mean = jnp.mean(values, axis=-1, keepdims=True)
    centred = values - row_mean
    spread = jnp.mean(centred * centred, axis=-1, keepdims=True)
    return centred * lax.rsqrt(spread + 1e-05) * norm_gain + norm_shift


def dot_f32(left, right, left_dim, right_dim):
    return lax.dot_general(
        left, right, (((left_dim,), (right_dim,)), ((), ())), preferred_element_type=jnp.float32
    )


def spin(values, cosine, sine, lanes):
    if lanes % 128 == 0:
        ahead = pltpu.roll(values, lanes - ROT // 2, 1)
        behind = pltpu.roll(values, ROT // 2, 1)
    else:
        half_rot = ROT // 2
        ahead = jnp.concatenate([values[:, half_rot:], values[:, :half_rot]], axis=1)
        behind = jnp.concatenate([values[:, -half_rot:], values[:, :-half_rot]], axis=1)
    lane = lax.broadcasted_iota(jnp.int32, values.shape, 1) % HD
    return values * cosine + jnp.where(lane < ROT // 2, ahead, behind) * sine


def begin_of(places, len_ref, seqs):
    begin = jnp.zeros_like(places)
    end = jnp.int32(0)
    for index in range(seqs):
        end = end + len_ref[index]
        begin = jnp.where(places >= end, end, begin)
    return begin


def begin_scalar(place, len_ref, seqs):
    begin = jnp.int32(0)
    end = jnp.int32(0)
    for index in range(seqs):
        end = end + len_ref[index]
        begin = jnp.where(place >= end, end, begin)
    return begin


def finish_scalar(place, len_ref, seqs):
    finish = jnp.int32(0)
    end = jnp.int32(0)
    for index in range(seqs):
        finish = jnp.where(place >= end, end + len_ref[index], finish)
        end = end + len_ref[index]
    return finish


def fold_rows(values):
    return jnp.sum(values.reshape(-1, 8, values.shape[1]), axis=0)


def head_masks(rows, lanes, heads):
    lane = lax.broadcasted_iota(jnp.int32, (rows, lanes), 1)
    return [(lane // HD) == index for index in range(heads)]


def attend_kernel(parts, tiles, width, stream, seqs, block, slot_ref, len_ref, *refs):
    qkv_ref, cos_ref, sin_ref = refs[:3]
    out_parts = refs[3 : parts + 3]
    sorted_ref, mixed_ref, lse_ref = refs[parts + 3 : parts + 6]
    loaded, value_aug, load_sem, store_sem = refs[parts + 6 :]
    lanes = min(128, width)
    per_group = lanes // HD
    groups = width // lanes

    @pl.loop(0, parts * tiles)
    def _(tile):
        place = pl.multiple_of(slot_ref[tile] * TILE, TILE)
        row = pl.multiple_of(tile * TILE, TILE)
        pltpu.make_async_copy(
            qkv_ref.at[pl.ds(row, TILE)], loaded.at[pl.ds(place, TILE)], load_sem
        ).start()

    pltpu.make_async_copy(loaded, loaded, load_sem).wait()

    @pl.loop(0, stream // 256)
    def _(step):
        rows = pl.ds(pl.multiple_of(step * 256, 256), 256)
        cosine, sine = cos_ref[rows, :], sin_ref[rows, :]
        masks = head_masks(256, lanes, per_group)
        for group in range(groups):
            cols = slice(group * lanes, (group + 1) * lanes)
            query = spin(loaded[rows, cols].astype(jnp.float32), cosine, sine, lanes)
            query = query.astype(jnp.bfloat16) * jnp.bfloat16(HD**-0.5)
            sorted_ref[rows, cols] = query
            cols = slice(width + group * lanes, width + (group + 1) * lanes)
            key = spin(loaded[rows, cols].astype(jnp.float32), cosine, sine, lanes)
            sorted_ref[rows, cols] = key.astype(jnp.bfloat16)
            cols = slice(2 * width + group * lanes, 2 * width + (group + 1) * lanes)
            value = loaded[rows, cols]
            sorted_ref[rows, cols] = value
            ones = jnp.ones((256, lanes), jnp.bfloat16)
            for index in range(per_group):
                head = group * per_group + index
                if per_group == 2:
                    value_aug[rows, head * 128 : (head + 1) * 128] = jnp.where(
                        masks[index], value, ones
                    )
                else:
                    value_aug[rows, head * 128 : head * 128 + HD] = value
                    value_aug[rows, head * 128 + HD : (head + 1) * 128] = ones

    for group in range(groups):
        cols = slice(group * lanes, (group + 1) * lanes)
        key_cols = slice(width + group * lanes, width + (group + 1) * lanes)

        @pl.loop(0, stream // block)
        def _(index):
            first = index * block
            rows = pl.ds(pl.multiple_of(first, block), block)
            query = sorted_ref[rows, cols]
            masks = head_masks(block, lanes, per_group)
            query_heads = [jnp.where(mask, query, jnp.bfloat16(0)) for mask in masks]
            place = first + lax.broadcasted_iota(jnp.int32, (block, 1), 0)
            begin = begin_of(place, len_ref, seqs)
            begin_low = begin_scalar(first, len_ref, seqs)
            begin_high = begin_scalar(first + block - 1, len_ref, seqs)

            def step(number, carry, masked):
                start = number * block
                key_rows = pl.ds(pl.multiple_of(start, block), block)
                key = sorted_ref[key_rows, key_cols]
                out = []
                for which in range(per_group):
                    top, total = carry[which]
                    head = group * per_group + which
                    scores = dot_f32(query_heads[which], key, 1, 1)
                    if masked:
                        key_place = start + lax.broadcasted_iota(jnp.int32, (1, block), 1)
                        visible = (key_place <= place) & (key_place >= begin)
                        scores = jnp.where(visible, scores, LOW_SCORE)
                    new_top = jnp.maximum(top, jnp.max(scores, axis=1, keepdims=True))
                    expw = jnp.exp(scores - new_top).astype(jnp.bfloat16)
                    shrink = jnp.exp(top - new_top)
                    mixed = dot_f32(
                        expw, value_aug[key_rows, head * 128 : (head + 1) * 128], 1, 0
                    )
                    out.append((new_top, total * shrink + mixed))
                return tuple(out)

            carry = tuple(
                (jnp.full((block, 1), START_TOP, jnp.float32), jnp.zeros((block, 128), jnp.float32))
                for _ in range(per_group)
            )
            first_block = begin_low // block
            inner = jnp.minimum((begin_high + block - 1) // block, index)
            carry = lax.fori_loop(
                first_block, inner, functools.partial(step, masked=True), carry
            )
            carry = lax.fori_loop(inner, index, functools.partial(step, masked=False), carry)
            carry = step(index, carry, True)
            lane = lax.broadcasted_iota(jnp.int32, (block, 128), 1)
            mixed, logs = [], []
            for which in range(per_group):
                top, total = carry[which]
                swapped = pltpu.roll(total, HD, 1)
                own = (lane // HD) == which
                sums = jnp.where(own, swapped, total)
                mixed.append(total / sums)
                logs.append(top + jnp.log(sums))
            if per_group == 2:
                both = jnp.where(lane < HD, mixed[0], mixed[1])
                log_both = jnp.where(lane < HD, logs[0], logs[1])
            else:
                both = mixed[0][:, :HD]
                log_both = logs[0]
            mixed_ref[rows, cols] = both.astype(jnp.bfloat16)
            turned = jnp.transpose(log_both)
            for which in range(per_group):
                head = group * per_group + which
                lse_ref[head : head + 1, rows] = turned[which * HD : which * HD + 1, :]

    for part in range(parts):

        @pl.loop(0, tiles)
        def _(tile, part=part):
            place = pl.multiple_of(slot_ref[part * tiles + tile] * TILE, TILE)
            row = pl.multiple_of(tile * TILE, TILE)
            pltpu.make_async_copy(
                mixed_ref.at[pl.ds(place, TILE)], out_parts[part].at[pl.ds(row, TILE)], store_sem
            ).start()

    pltpu.make_async_copy(mixed_ref, mixed_ref, store_sem).wait()


def attend(slots, lengths, projected, tables, count):
    stream, triple = projected.shape
    rows = stream // count
    width = triple // 3
    heads = width // HD
    block = min(512, stream)
    anywhere = pl.BlockSpec(memory_space=pl.ANY)
    whole = pl.BlockSpec(memory_space=pltpu.VMEM)
    kernel = functools.partial(
        attend_kernel, count, rows // TILE, width, stream, lengths.shape[0], block
    )
    pairs = stream * stream // 3 * heads
    outs = pl.pallas_call(
        kernel,
        name="attention_forward",
        out_shape=[jax.ShapeDtypeStruct((rows, width), jnp.bfloat16)] * count
        + [
            jax.ShapeDtypeStruct((stream, triple), jnp.bfloat16),
            jax.ShapeDtypeStruct((stream, width), jnp.bfloat16),
            jax.ShapeDtypeStruct((max(heads, 8), stream), jnp.float32),
        ],
        in_specs=[pl.BlockSpec(memory_space=pltpu.SMEM)] * 2 + [anywhere, whole, whole],
        out_specs=[anywhere] * count + [whole] * 3,
        scratch_shapes=[
            pltpu.VMEM((stream, triple), jnp.bfloat16),
            pltpu.VMEM((stream, heads * 128), jnp.bfloat16),
            pltpu.SemaphoreType.DMA,
            pltpu.SemaphoreType.DMA,
        ],
        compiler_params=pltpu.CompilerParams(vmem_limit_bytes=VMEM_LIMIT),
        cost_estimate=pl.CostEstimate(
            flops=pairs * 4 * 256, bytes_accessed=stream * width * 20, transcendentals=pairs
        ),
    )(slots, lengths, projected, *tables)
    return outs[:count], outs[count], outs[count + 1], outs[count + 2]


def attend_back_kernel(
    given, column, width, stream, seqs, block, slot_ref, len_ref, *refs
):
    back_parts = refs[:given]
    sorted_ref, mixed_ref, lse_ref, cos_ref, sin_ref, out_ref, sums_ref = refs[given : given + 7]
    back, grads, query_grad, delta, load_sem, store_sem = refs[given + 7 :]
    given_tiles = stream // TILE // given
    lanes = min(128, width)
    per_group = lanes // HD
    groups = width // lanes
    for part in range(given):

        @pl.loop(0, given_tiles)
        def _(tile, part=part):
            place = pl.multiple_of(slot_ref[part * given_tiles + tile] * TILE, TILE)
            row = pl.multiple_of(tile * TILE, TILE)
            pltpu.make_async_copy(
                back_parts[part].at[pl.ds(row, TILE), pl.ds(column, width)],
                back.at[pl.ds(place, TILE)],
                load_sem,
            ).start()

    pltpu.make_async_copy(back, back, load_sem).wait()

    for group in range(groups):
        cols = slice(group * lanes, (group + 1) * lanes)
        key_cols = slice(width + group * lanes, width + (group + 1) * lanes)
        value_cols = slice(2 * width + group * lanes, 2 * width + (group + 1) * lanes)
        query_grad[...] = jnp.zeros_like(query_grad)
        sums_ref[...] = jnp.zeros_like(sums_ref)

        @pl.loop(0, stream // block)
        def _(index):
            rows = pl.ds(pl.multiple_of(index * block, block), block)
            product = back[rows, cols].astype(jnp.float32) * mixed_ref[rows, cols].astype(
                jnp.float32
            )
            pick = (
                lax.broadcasted_iota(jnp.int32, (8, lanes), 1) // HD
                == lax.broadcasted_iota(jnp.int32, (8, lanes), 0)
            ).astype(jnp.float32)
            delta[:, rows] = lax.dot_general(
                pick,
                product,
                (((1,), (1,)), ((), ())),
                precision=lax.Precision.HIGHEST,
                preferred_element_type=jnp.float32,
            )

        @pl.loop(0, stream // block)
        def _(index):
            first = index * block
            key_rows = pl.ds(pl.multiple_of(first, block), block)
            key = sorted_ref[key_rows, key_cols]
            value = sorted_ref[key_rows, value_cols]
            masks = head_masks(block, lanes, per_group)
            key_heads = [jnp.where(mask, key, jnp.bfloat16(0)) for mask in masks]
            key_place = first + lax.broadcasted_iota(jnp.int32, (block, 1), 0)
            finish_low = finish_scalar(first, len_ref, seqs)
            finish_high = finish_scalar(first + block - 1, len_ref, seqs)

            def step(number, carry, masked):
                key_grad, value_grad = carry
                start = number * block
                rows = pl.ds(pl.multiple_of(start, block), block)
                query = sorted_ref[rows, cols]
                upstream = back[rows, cols]
                query_add = None
                if masked:
                    place = start + lax.broadcasted_iota(jnp.int32, (1, block), 1)
                    begin = begin_of(place, len_ref, seqs)
                    visible = (key_place <= place) & (key_place >= begin)
                for which in range(per_group):
                    head = group * per_group + which
                    query_head = jnp.where(masks[which], query, jnp.bfloat16(0))
                    back_head = jnp.where(masks[which], upstream, jnp.bfloat16(0))
                    scores = dot_f32(key, query_head, 1, 1)
                    if masked:
                        scores = jnp.where(visible, scores, LOW_SCORE)
                    chances = jnp.exp(scores - lse_ref[head : head + 1, rows])
                    d_chances = dot_f32(value, back_head, 1, 1)
                    d_raw = (chances * (d_chances - delta[which : which + 1, rows])).astype(
                        jnp.bfloat16
                    )
                    value_grad = value_grad + dot_f32(
                        chances.astype(jnp.bfloat16), back_head, 1, 0
                    )
                    key_grad = key_grad + dot_f32(d_raw, query_head, 1, 0)
                    part_add = dot_f32(d_raw, key_heads[which], 0, 0)
                    query_add = part_add if query_add is None else query_add + part_add
                query_grad[rows, :] += query_add
                return (key_grad, value_grad)

            zeros = jnp.zeros((block, lanes), jnp.float32)
            carry = step(index, (zeros, zeros), True)
            inner = jnp.maximum(finish_low // block, index + 1)
            last = jnp.maximum((finish_high + block - 1) // block, inner)
            carry = lax.fori_loop(
                index + 1, inner, functools.partial(step, masked=False), carry
            )
            carry = lax.fori_loop(inner, last, functools.partial(step, masked=True), carry)
            key_grad = spin(carry[0], cos_ref[key_rows, :], -sin_ref[key_rows, :], lanes)
            grads[key_rows, key_cols] = key_grad.astype(jnp.bfloat16)
            grads[key_rows, value_cols] = carry[1].astype(jnp.bfloat16)
            sums_ref[:, key_cols] += fold_rows(key_grad)
            sums_ref[:, value_cols] += fold_rows(carry[1])

        @pl.loop(0, stream // 256)
        def _(step):
            rows = pl.ds(pl.multiple_of(step * 256, 256), 256)
            turned = spin(query_grad[rows, :], cos_ref[rows, :], -sin_ref[rows, :], lanes)
            turned = turned * (HD**-0.5)
            grads[rows, cols] = turned.astype(jnp.bfloat16)
            sums_ref[:, cols] += fold_rows(turned)

    @pl.loop(0, stream // TILE)
    def _(tile):
        place = pl.multiple_of(slot_ref[tile] * TILE, TILE)
        row = pl.multiple_of(tile * TILE, TILE)
        pltpu.make_async_copy(
            grads.at[pl.ds(place, TILE)], out_ref.at[pl.ds(row, TILE)], store_sem
        ).start()

    pltpu.make_async_copy(grads, grads, store_sem).wait()


def attend_back(slots, lengths, parts, column, kept, mixed, lse, tables):
    stream, width = mixed.shape
    heads = width // HD
    block = min(512, stream)
    lanes = min(128, width)
    anywhere = pl.BlockSpec(memory_space=pl.ANY)
    whole = pl.BlockSpec(memory_space=pltpu.VMEM)
    kernel = functools.partial(
        attend_back_kernel, len(parts), column, width, stream, lengths.shape[0], block
    )
    pairs = stream * stream // 3 * heads
    return pl.pallas_call(
        kernel,
        name="attention_backward",
        out_shape=[
            jax.ShapeDtypeStruct((stream, 3 * width), jnp.bfloat16),
            jax.ShapeDtypeStruct((8, 3 * width), jnp.float32),
        ],
        in_specs=[pl.BlockSpec(memory_space=pltpu.SMEM)] * 2
        + [anywhere] * len(parts)
        + [whole] * 5,
        out_specs=[anywhere, whole],
        scratch_shapes=[
            pltpu.VMEM((stream, width), jnp.bfloat16),
            pltpu.VMEM((stream, 3 * width), jnp.bfloat16),
            pltpu.VMEM((stream, lanes), jnp.float32),
            pltpu.VMEM((8, stream), jnp.float32),
            pltpu.SemaphoreType.DMA,
            pltpu.SemaphoreType.DMA,
        ],
        compiler_params=pltpu.CompilerParams(vmem_limit_bytes=VMEM_LIMIT),
        cost_estimate=pl.CostEstimate(
            flops=pairs * 10 * 256, bytes_accessed=stream * width * 20, transcendentals=pairs
        ),
    )(slots, lengths, *parts, kept, mixed, lse, *tables)


def rotary_kernel(lanes, table_ref, cos_ref, sin_ref):
    half_rot = ROT // 2
    lane = lax.broadcasted_iota(jnp.int32, (half_rot, lanes), 1) % HD
    entry = lax.broadcasted_iota(jnp.int32, (half_rot, lanes), 0)
    first, second = lane == entry, lane == entry + half_rot
    pick_cos = (first | second).astype(jnp.float32)
    pick_sin = second.astype(jnp.float32) - first.astype(jnp.float32)

    def spread(values, pick):
        return lax.dot_general(
            values,
            pick,
            (((0,), (0,)), ((), ())),
            precision=lax.Precision.HIGHEST,
            preferred_element_type=jnp.float32,
        )

    still = (lax.broadcasted_iota(jnp.int32, (1, lanes), 1) % HD >= ROT).astype(jnp.float32)
    cos_ref[...] = spread(table_ref[:half_rot, :], pick_cos) + still
    sin_ref[...] = spread(table_ref[half_rot:, :], pick_sin)


def rotary_tables(table, lanes):
    stream = table.shape[1]
    block = min(512, stream)
    return pl.pallas_call(
        functools.partial(rotary_kernel, lanes),
        name="rotary_tables",
        grid=(stream // block,),
        in_specs=[pl.BlockSpec((ROT, block), lambda step: (0, step))],
        out_specs=[pl.BlockSpec((block, lanes), lambda step: (step, 0))] * 2,
        out_shape=[jax.ShapeDtypeStruct((stream, lanes), jnp.float32)] * 2,
        cost_estimate=pl.CostEstimate(
            flops=stream * lanes * 100, bytes_accessed=stream * lanes * 8, transcendentals=0
        ),
    )(table)


def project_kernel(sources, groups, slab, map_ref, *refs):
    inputs = refs[:sources]
    gain_ref, shift_ref, weight_ref, bias_ref = refs[sources : sources + 4]
    outs = refs[len(refs) - groups - 1 :]

    def run(source):
        values = source[...].astype(jnp.float32)
        normed = layer_norm(values, gain_ref[...], shift_ref[...]).astype(jnp.bfloat16)
        outs[0][...] = normed
        result = dot_f32(normed, weight_ref[...], 1, 0) + bias_ref[...]
        for group in range(groups):
            outs[1 + group][...] = result[:, group * slab : (group + 1) * slab].astype(
                jnp.bfloat16
            )

    if sources == 1:
        run(inputs[0])
    else:
        for index in range(sources):

            @pl.when(pl.program_id(0) == index)
            def _(index=index):
                run(inputs[index])


def project(blocks, sources, gain, shift, weight, bias, groups, rows, first, kept):
    features, triple = weight.shape
    slab = triple // groups
    count = len(sources)
    steps = blocks.shape[0] if count == 1 else count
    size = math.gcd(256, sources[0].shape[0])
    kept = [] if kept is None else kept
    fixed = lambda step, order: (0, 0)
    placed = lambda step, order: (first + step, 0)
    if count == 1:
        specs = [pl.BlockSpec((size, features), lambda step, order: (order[step], 0))]
    else:
        specs = [pl.BlockSpec((size, features), fixed)] * count
    specs += [
        pl.BlockSpec((1, features), fixed),
        pl.BlockSpec((1, features), fixed),
        pl.BlockSpec((features, triple), fixed),
        pl.BlockSpec((1, triple), fixed),
    ]
    specs += [pl.BlockSpec(memory_space=pl.ANY)] * len(kept)
    work = steps * size
    return pl.pallas_call(
        functools.partial(project_kernel, count, groups, slab),
        name="norm_project",
        grid_spec=pltpu.PrefetchScalarGridSpec(
            num_scalar_prefetch=1,
            grid=(steps,),
            in_specs=specs,
            out_specs=[pl.BlockSpec((size, features), placed)]
            + [pl.BlockSpec((size, slab), placed)] * groups,
        ),
        out_shape=[jax.ShapeDtypeStruct((rows, features), jnp.bfloat16)]
        + [jax.ShapeDtypeStruct((rows, slab), jnp.bfloat16)] * groups,
        input_output_aliases={count + 5 + index: index for index in range(len(kept))},
        compiler_params=pltpu.CompilerParams(vmem_limit_bytes=VMEM_LIMIT),
        cost_estimate=pl.CostEstimate(
            flops=2 * work * features * triple,
            bytes_accessed=work * features * 4 + features * triple * 2,
            transcendentals=0,
        ),
    )(blocks, *sources, gain, shift, weight, bias, *kept)


def place_kernel(count, at_ref, *refs):
    for index in range(count):

        @pl.when(pl.program_id(0) == index)
        def _(index=index):
            refs[count][...] = refs[index][...]


def place_rows(at, pieces):
    size, features = pieces[0].shape
    count = len(pieces)
    return pl.pallas_call(
        functools.partial(place_kernel, count),
        name="place_rows",
        grid_spec=pltpu.PrefetchScalarGridSpec(
            num_scalar_prefetch=1,
            grid=(count,),
            in_specs=[once((size, features))] * count,
            out_specs=pl.BlockSpec((size, features), lambda step, order: (order[step], 0)),
        ),
        out_shape=jax.ShapeDtypeStruct((size * count, features), pieces[0].dtype),
        compiler_params=pltpu.CompilerParams(vmem_limit_bytes=VMEM_LIMIT),
        cost_estimate=pl.CostEstimate(
            flops=0, bytes_accessed=size * count * features * 4, transcendentals=0
        ),
    )(at, *pieces)


def pick_kernel(at_ref, source, out):
    out[...] = source[...]


def pick_rows(at, values, size):
    rows, features = values.shape
    return pl.pallas_call(
        pick_kernel,
        name="pick_rows",
        grid_spec=pltpu.PrefetchScalarGridSpec(
            num_scalar_prefetch=1,
            grid=(rows // size,),
            in_specs=[pl.BlockSpec((size, features), lambda step, order: (order[step], 0))],
            out_specs=pl.BlockSpec((size, features), lambda step, order: (step, 0)),
        ),
        out_shape=jax.ShapeDtypeStruct((rows, features), values.dtype),
        cost_estimate=pl.CostEstimate(
            flops=0, bytes_accessed=rows * features * 4, transcendentals=0
        ),
    )(at, values)


def once(shape):
    return pl.BlockSpec(shape, lambda *_: (0, 0), pipeline_mode=pl.Buffered(1))


def column_tiles(columns):
    return [(start, min(512, columns - start)) for start in range(0, columns, 512)]


def store_half(step, keep_ref, send_ref, cols, values):
    values = values.astype(jnp.bfloat16)

    @pl.when(step == 0)
    def _():
        send_ref[:, cols] = values

    @pl.when(step == 1)
    def _():
        keep_ref[:, cols] = values


def matmul_call(
    kernel, name, half, in_specs, out_specs, out_shape, scratch, flops, args, aliases=None
):
    bytes_moved = sum(a.size * a.dtype.itemsize for a in args)
    bytes_moved += sum(math.prod(o.shape) * o.dtype.itemsize for o in out_shape)
    return pl.pallas_call(
        kernel,
        name=name,
        grid=(2,),
        in_specs=in_specs,
        out_specs=out_specs,
        out_shape=out_shape,
        scratch_shapes=scratch,
        input_output_aliases=aliases or {},
        compiler_params=pltpu.CompilerParams(vmem_limit_bytes=VMEM_LIMIT),
        cost_estimate=pl.CostEstimate(flops=flops, bytes_accessed=bytes_moved, transcendentals=0),
    )(*args)


def low_shape(*shape):
    return jax.ShapeDtypeStruct(shape, jnp.bfloat16)


def out_kernel(count, groups, lanes, holder_ref, *refs):
    parts = refs[: count * groups]
    weight_ref, keep_ref, send_ref, attended_ref = refs[count * groups :]
    step = pl.program_id(0)
    for s in range(count):
        for c in range(count):

            @pl.when(holder_ref[s] == c)
            def _(s=s, c=c):
                for group in range(groups):
                    first = (c * groups + group) * lanes
                    attended_ref[:, first : first + lanes] = parts[s * groups + group][...]

    for start, size in column_tiles(weight_ref.shape[1]):
        cols = slice(start, start + size)
        result = dot_f32(attended_ref[...], weight_ref[:, cols], 1, 0)
        store_half(step, keep_ref, send_ref, cols, result)


def project_out(holders, parts, count, groups, weight, chunk, half):
    width, features = weight.shape
    lanes = parts[0].shape[1]
    part_spec = pl.BlockSpec((half, lanes), lambda step: (chunk * 2 + 1 - step, 0))
    return matmul_call(
        functools.partial(out_kernel, count, groups, lanes),
        "project_out",
        half,
        [pl.BlockSpec(memory_space=pltpu.SMEM)]
        + [part_spec] * len(parts)
        + [once((width, features))],
        [
            pl.BlockSpec((half, features), lambda step: (0, 0)),
            pl.BlockSpec((half, features), lambda step: (0, 0)),
            pl.BlockSpec((half, width), lambda step: (1 - step, 0)),
        ],
        [low_shape(half, features), low_shape(half, features), low_shape(2 * half, width)],
        [],
        4 * half * features * width,
        (holders, *parts, weight),
    )


def collect(step, pieces, out_ref, first_step):
    half = len(pieces) // 2
    size = pieces[0].shape[0]
    for number in range(2):

        @pl.when(step == number)
        def _(number=number):
            chosen = pieces[half:] if number == first_step else pieces[:half]
            for index, piece in enumerate(chosen):
                out_ref[index * size : (index + 1) * size, :] = piece[...]


def feed_kernel(count, hidden, joined, *refs):
    pieces = refs[:count]
    d_hidden_ref, weight_ref = refs[count : count + 2]
    refs = refs[count + 2 + joined :]
    normed_ref, hidden_ref, grad_ref, keep_ref, send_ref = refs[:5]
    weight, weight_sems, piece_sems = refs[5:]
    step = pl.program_id(0)
    size = pieces[0].shape[0]
    half = count // 2

    def piece_copy(index, number):
        row = index * size
        return pltpu.make_async_copy(
            pieces[half * (1 - number) + index],
            normed_ref.at[pl.ds(row, size)],
            piece_sems.at[index],
        )

    columns = [
        (first, width)
        for start, width in column_tiles(hidden)
        for first in (start, hidden + start)
    ]
    copies = [
        pltpu.make_async_copy(
            weight_ref.at[:, pl.ds(start, width)],
            weight.at[:, pl.ds(start, width)],
            weight_sems.at[number],
        )
        for number, (start, width) in enumerate(columns)
    ]

    @pl.when(step == 0)
    def _():
        for index in range(half):
            piece_copy(index, 0).start()
        for copy in copies:
            copy.start()
        for index in range(half):
            piece_copy(index, 0).wait()

    @pl.when(step == 1)
    def _():
        for index in range(half):
            piece_copy(index, 1).start()
        for index in range(half):
            piece_copy(index, 1).wait()

    for number, (start, width) in enumerate(column_tiles(hidden)):

        @pl.when(step == 0)
        def _(number=number):
            copies[2 * number].wait()
            copies[2 * number + 1].wait()

        gate_cols = slice(start, start + width)
        up_cols = slice(hidden + start, hidden + start + width)
        gate = dot_f32(normed_ref[...], weight[:, gate_cols], 1, 0)
        up = dot_f32(normed_ref[...], weight[:, up_cols], 1, 0)
        sigmoid = 1.0 / (1.0 + jnp.exp(-gate))
        silu = gate * sigmoid
        d_hidden = d_hidden_ref[:, gate_cols]
        hidden_ref[:, gate_cols] = (silu * up).astype(jnp.bfloat16)
        d_gate = d_hidden * up * sigmoid * (1.0 + gate * (1.0 - sigmoid))
        grad_ref[:, gate_cols] = d_gate.astype(jnp.bfloat16)
        grad_ref[:, up_cols] = (d_hidden * silu).astype(jnp.bfloat16)

    for start, width in column_tiles(weight.shape[0]):
        cols = slice(start, start + width)
        result = dot_f32(grad_ref[...], weight[cols, :], 1, 1)
        store_half(step, keep_ref, send_ref, cols, result)


def feed_forward(pieces, d_hidden, weight, rows, chunk, joined):
    share, features = pieces[0].shape
    half = share * len(pieces) // 2
    hidden = d_hidden.shape[1]
    joined_at = lambda step: (chunk * 2 + 1 - step, 0)
    anywhere = pl.BlockSpec(memory_space=pl.ANY)
    copies = 2 * len(column_tiles(hidden))
    joined = [] if joined is None else joined
    args = (*pieces, d_hidden, weight, *joined)
    return matmul_call(
        functools.partial(feed_kernel, len(pieces), hidden, len(joined)),
        "feed_forward",
        half,
        [anywhere] * len(pieces)
        + [pl.BlockSpec((half, hidden), joined_at), anywhere]
        + [anywhere] * len(joined),
        [
            pl.BlockSpec((half, features), joined_at),
            pl.BlockSpec((half, hidden), joined_at),
            pl.BlockSpec((half, 2 * hidden), joined_at),
            pl.BlockSpec((half, features), lambda step: (0, 0)),
            pl.BlockSpec((half, features), lambda step: (0, 0)),
        ],
        [
            low_shape(rows, features),
            low_shape(rows, hidden),
            low_shape(rows, 2 * hidden),
            low_shape(half, features),
            low_shape(half, features),
        ],
        [
            pltpu.VMEM((features, 2 * hidden), jnp.bfloat16),
            pltpu.SemaphoreType.DMA((copies,)),
            pltpu.SemaphoreType.DMA((len(pieces) // 2,)),
        ],
        16 * half * features * hidden,
        args,
        {len(pieces) + 2 + index: index for index in range(len(joined))},
    )


def out_back_kernel(count, pieces, width, holder_ref, *refs):
    sources = refs[:pieces]
    weight_ref, gathered_ref = refs[pieces : pieces + 2]
    outs = refs[pieces + 2 : pieces + 2 + count]
    step = pl.program_id(0)
    collect(step, sources, gathered_ref, 0)
    result = dot_f32(gathered_ref[...], weight_ref[...], 1, 0).astype(jnp.bfloat16)
    for s in range(count):
        for c in range(count):

            @pl.when(holder_ref[s] == c)
            def _(s=s, c=c):
                outs[s][...] = result[:, c * width : (c + 1) * width]


def project_out_back(holders, pieces, weight, count):
    share, features = pieces[0].shape
    half = share * len(pieces) // 2
    total = weight.shape[1]
    width = total // count
    placed = lambda step: (1 - step, 0)
    outs = matmul_call(
        functools.partial(out_back_kernel, count, len(pieces), width),
        "project_out_back",
        half,
        [pl.BlockSpec(memory_space=pltpu.SMEM)]
        + [once((share, features))] * len(pieces)
        + [once((features, total))],
        [pl.BlockSpec((half, features), placed)] + [pl.BlockSpec((half, width), placed)] * count,
        [low_shape(2 * half, features)] + [low_shape(2 * half, width)] * count,
        [],
        4 * half * features * total,
        (holders, *pieces, weight),
    )
    return outs[0], list(outs[1:])


def norm_back_kernel(count, groups, slab, *refs):
    parts = refs[: count * groups]
    weights = refs[count * groups : count * groups + count]
    keep_ref, send_ref, joined = refs[count * groups + count :]
    step = pl.program_id(0)
    if groups > 1:
        for index, part in enumerate(parts):
            joined[:, index * slab : (index + 1) * slab] = part[...]

    for start, size in column_tiles(weights[0].shape[1]):
        cols = slice(start, start + size)
        total = None
        for s in range(count):
            if groups > 1:
                left = joined[:, s * groups * slab : (s + 1) * groups * slab]
            else:
                left = parts[s][...]
            product = dot_f32(left, weights[s][:, cols], 1, 0)
            total = product if total is None else total + product
        store_half(step, keep_ref, send_ref, cols, total)


def project_back(parts, weights, groups, half):
    wide, features = weights[0].shape
    count = len(weights)
    slab = wide // groups

    def spec(first):
        return pl.BlockSpec(
            (half, slab), lambda step: (first // half + 1 - step, 0)
        )

    return matmul_call(
        functools.partial(norm_back_kernel, count, groups, slab),
        "project_back",
        half,
        [spec(first) for _, first in parts] + [once((wide, features))] * count,
        [pl.BlockSpec((half, features), lambda step: (0, 0))] * 2,
        [low_shape(half, features)] * 2,
        [pltpu.VMEM((half, count * wide), jnp.bfloat16)],
        4 * half * features * wide * count,
        (*(array for array, _ in parts), *weights),
    )


def swap_bit(values, axis, bit):
    size = lax.axis_size(axis)
    return lax.ppermute(values, axis, [(i, i ^ (1 << bit)) for i in range(size)])


def sum_over_tensor(keep, send, bits):
    return sum_further(sum_first(keep, send), bits)


def sum_first(keep, send):
    return keep.astype(jnp.float32) + swap_bit(send, "tensor", 0).astype(jnp.float32)


def sum_further(total, bits):
    for bit in range(1, bits):
        half = total.shape[0] // 2
        arrived = swap_bit(total[half:].astype(jnp.bfloat16), "tensor", bit)
        total = total[:half] + arrived.astype(jnp.float32)
    return total


def gather_pieces(own, bits):
    return gather_rest(gather_first(own, bits), bits)


def gather_first(own, bits):
    return [own, swap_bit(own, "tensor", bits - 1)]


def gather_rest(pieces, bits):
    for bit in reversed(range(bits - 1)):
        pieces = pieces + [swap_bit(piece, "tensor", bit) for piece in pieces]
    return pieces


def butterfly(values):
    for axis in ("ctx", "dp", "tensor"):
        for bit in range(lax.axis_size(axis).bit_length() - 1):
            values = values + swap_bit(values, axis, bit)
    return values


def shift_over(values, axis, shift):
    size = lax.axis_size(axis)
    return lax.ppermute(values, axis, [(i, (i - shift) % size) for i in range(size)])


def exchange(pieces):
    count = len(pieces)
    arrived = [pieces[0]] + [None] * (count - 1)
    for shift in range(1, count):
        arrived[count - shift] = shift_over(pieces[shift], "ctx", shift)
    return arrived


def take_block(values, index, size, axis):
    return lax.dynamic_slice_in_dim(values, index * size, size, axis=axis)


def body(
    tokens,
    cotangent,
    lengths,
    offsets,
    ln1_gain,
    ln1_bias,
    w_qkv,
    b_qkv,
    w_out,
    ln2_gain,
    ln2_bias,
    w_gate_up,
    w_down,
):
    f32, low = jnp.float32, jnp.bfloat16
    split = ("dp", "ctx")
    n_dp, n_ctx, n_tensor = (lax.axis_size(name) for name in ("dp", "ctx", "tensor"))
    my_dp, me, mine = (lax.axis_index(name) for name in ("dp", "ctx", "tensor"))
    bits = n_tensor.bit_length() - 1
    rows, features = tokens.shape
    quarter = rows // n_tensor
    chunks = 2 if quarter % (2 * TILE) == 0 else 1
    share = quarter // chunks
    block = rows // chunks
    heads_width = w_qkv.shape[2]
    width = heads_width // n_ctx
    lanes = min(128, width)
    groups = width // lanes
    slab = 3 * lanes
    hidden_width = w_down.shape[0]
    stream = rows * n_ctx
    tiles = rows // TILE
    order = [int(format(p, f"0{bits}b")[::-1], 2) for p in range(n_tensor)]
    quarters = [mine ^ item for item in order]
    holders = [(me - s) % n_ctx for s in range(n_ctx)]

    def own_share(values, chunk):
        return lax.dynamic_slice_in_dim(values, mine * quarter + chunk * share, share, axis=0)

    def rotated_chunk(values, chunk):
        return jnp.concatenate(
            [
                lax.dynamic_slice_in_dim(values, q * quarter + chunk * share, share, axis=0)
                for q in quarters
            ],
            axis=0,
        )

    share_at = jnp.stack(
        [quarters[p] * chunks + chunk for chunk in range(chunks) for p in range(n_tensor)]
    ).astype(jnp.int32)

    def unrotate(columns):
        return place_rows(share_at, [piece for pieces in columns for piece in pieces])

    qkv_local = (
        w_qkv.reshape(-1, 3, n_ctx, groups, lanes)
        .transpose(0, 2, 3, 1, 4)
        .reshape(-1, n_ctx, groups * slab)
    )
    depth = qkv_local.shape[0]
    from_ctx = exchange(
        [lax.dynamic_index_in_dim(qkv_local, c, 1, keepdims=False) for c in holders]
    )

    piece_at = jnp.stack(
        [(my_dp + shift) % n_dp * n_ctx + c for c in holders for shift in range(n_dp)]
    ).astype(jnp.int32)

    def ring_rows(arrived):
        pieces = []
        for item in arrived:
            pieces.append(item)
            for _ in range(1, n_dp):
                item = shift_over(item, "dp", 1)
                pieces.append(item)
        return pieces

    qkv_pieces = ring_rows(from_ctx)

    peer_pieces = [[None] * chunks for _ in range(n_ctx)]
    for chunk in range(chunks):
        own = own_share(tokens, chunk)
        for shift in range(1, n_ctx):
            arrived = shift_over(own, "ctx", shift)
            steps = [qkv_pieces[s * n_dp + min(chunk + 1, n_dp - 1)] for s in range(n_ctx)]
            arrived, _ = lax.optimization_barrier((arrived, steps))
            peer_pieces[n_ctx - shift][chunk] = gather_pieces(arrived, bits)

    def scatter_ring(partial, axis, after=()):
        size, index = lax.axis_size(axis), lax.axis_index(axis)
        deep = partial.shape[0] // size
        totals = [take_block(partial, (index + 1) % size, deep, 0)]
        for step in range(1, size):
            arrived = shift_over(totals[-1].astype(low), axis, 1)
            if step <= len(after):
                arrived, _ = lax.optimization_barrier((arrived, after[step - 1]))
            own = take_block(partial, (index + 1 + step) % size, deep, 0)
            totals.append(own.astype(f32) + arrived.astype(f32))
        return totals

    lengths_row = lengths[0]
    offsets_row = offsets[0].reshape(n_ctx, n_tensor, chunks, share // TILE)
    rotated_offsets = jnp.stack(
        [lax.dynamic_index_in_dim(offsets_row, q, 1, keepdims=False) for q in quarters], axis=2
    ).reshape(n_ctx, tiles)
    slots = (
        jnp.concatenate([take_block(rotated_offsets, c, 1, 0) for c in holders], axis=0).reshape(-1)
        // TILE
    )
    place = jnp.arange(stream, dtype=jnp.int32)
    ends = jnp.cumsum(lengths_row)
    begin = jnp.sum(jnp.where(place[None, :] >= ends[:, None], lengths_row[:, None], 0), axis=0)
    half_rot = ROT // 2
    frequency = jnp.exp(jnp.arange(half_rot, dtype=f32) * (-2.0 * math.log(10000.0) / ROT))
    angles = frequency[:, None] * (place - begin).astype(f32)[None, :]
    table = rotary_tables(jnp.concatenate([jnp.cos(angles), jnp.sin(angles)], axis=0), lanes)

    tokens_own = [own_share(tokens, chunk) for chunk in range(chunks)]
    cotangent_rot = pick_rows(share_at, cotangent, share)
    gate_up_local = w_gate_up.reshape(-1, 2 * hidden_width)
    peers_half = [item[: n_tensor // 2] for items in peer_pieces[1:] for item in items]
    qkv_pieces, _ = lax.optimization_barrier(
        (qkv_pieces, (peers_half, table, slots, tokens_own, cotangent_rot, gate_up_local))
    )
    qkv_mine = place_rows(piece_at, qkv_pieces)
    out_full = lax.all_gather(w_out.T, split, axis=0, tiled=True)
    down_local, _ = lax.optimization_barrier((w_down.T, from_ctx))
    down_full = lax.all_gather(down_local, split, axis=0, tiled=True)
    gate_up_local, _ = lax.optimization_barrier((gate_up_local, qkv_mine))
    gate_up_full = lax.all_gather(gate_up_local, split, axis=0, tiled=True)

    gain_one, shift_one = ln1_gain.astype(f32), ln1_bias.astype(f32)
    gain_two, shift_two = ln2_gain.astype(f32), ln2_bias.astype(f32)
    bias_mine = (
        take_block(b_qkv.reshape(3, n_ctx, groups, lanes), me, 1, 1)
        .transpose(1, 2, 0, 3)
        .reshape(1, -1)
        .astype(f32)
    )
    project_args = (gain_one[None], shift_one[None], qkv_mine, bias_mine, groups, stream)
    size = math.gcd(256, rows)
    if share >= size:
        own_blocks = jnp.stack(
            [share_at * (share // size) + i for i in range(share // size)], axis=1
        ).reshape(-1)
        projected = project(own_blocks, [tokens], *project_args, 0, None)
    else:
        own_rows = jnp.concatenate([rotated_chunk(tokens, c) for c in range(chunks)], axis=0)
        projected = project(
            jnp.arange(rows // size, dtype=jnp.int32), [own_rows], *project_args, 0, None
        )
    nothing = jnp.zeros((1,), jnp.int32)
    for s in range(1, n_ctx):
        for chunk in range(chunks):
            first = (s * rows + chunk * block) // share
            projected = project(nothing, peer_pieces[s][chunk], *project_args, first, projected)
    normed1 = projected[0]

    qkv_all = [[qkv_mine]] + [None] * (n_ctx - 1)
    arrived, _ = lax.optimization_barrier((qkv_mine, projected))
    for shift in range(1, n_ctx):
        items = []
        for half in range(2):
            sent = take_block(qkv_mine, half, features // 2, 0)
            arrived = shift_over(lax.optimization_barrier((sent, arrived))[0], "ctx", shift)
            items.append(arrived)
        qkv_all[n_ctx - shift] = items

    kept_attention, arrived_mixed = [], []
    for group in range(groups):
        mixed_parts, *kept = attend(slots, lengths_row, projected[1 + group], table, n_ctx)
        kept_attention.append(kept)
        arrived_mixed.append(exchange(mixed_parts))
    arrived_mixed, _ = lax.optimization_barrier((arrived_mixed, down_full))
    holders_at = jnp.stack(holders).astype(jnp.int32)
    mixed_parts = [arrived_mixed[group][s] for s in range(n_ctx) for group in range(groups)]

    def over_rows(lefts, rights):
        total = None
        for left, right in zip(lefts, rights):
            product = dot_f32(left, right, 0, 0)
            total = product if total is None else total + product
        return total.astype(low)

    tokens_own = [item.astype(f32) for item in tokens_own]
    middle, d_middle, d_middle_low = [], [], []
    attended, arrived_normed2, arrived_middle, d_attended = [], [], [], []
    d_gain_two, d_shift_two = 0.0, 0.0
    out_turned = out_full.T
    d_hidden = dot_f32(cotangent_rot, down_full, 1, 0)
    for chunk in range(chunks):
        keep, send, joined = project_out(
            holders_at, mixed_parts, n_ctx, groups, out_turned, chunk, block // 2
        )
        attended.append(joined)
        total = tokens_own[chunk] + sum_over_tensor(keep, send, bits)
        total, _ = lax.optimization_barrier((total, d_hidden))
        middle.append(total)
        own = layer_norm(middle[chunk], gain_two, shift_two).astype(low)
        arrived_normed2.append(gather_first(own, bits))
    first_normed2 = arrived_normed2
    arrived_normed2 = [gather_rest(item, bits) for item in arrived_normed2]
    joined = None
    d_normed2_all = []
    for chunk in range(chunks):
        *joined, keep, send = feed_forward(
            arrived_normed2[chunk], d_hidden, gate_up_full, rows, chunk, joined
        )
        send, _ = lax.optimization_barrier(
            (
                send,
                (
                    d_normed2_all,
                    first_normed2[chunk + 1 : chunk + 2],
                    [items[chunk] for items in qkv_all[1:]],
                ),
            )
        )
        total = sum_first(keep, send)
        if chunk + 1 < chunks:
            arrived_normed2[chunk + 1], _ = lax.optimization_barrier(
                (arrived_normed2[chunk + 1], total)
            )
        d_normed2_all.append(sum_further(total, bits))
    normed2, hidden, d_gate_up = joined
    ready, _ = lax.optimization_barrier((hidden, total))
    grad_down = dot_f32(cotangent_rot, ready, 0, 0).astype(low)
    for chunk in range(chunks):
        d_normed2 = d_normed2_all[chunk]
        if chunk:
            d_normed2, _ = lax.optimization_barrier(
                (d_normed2, grad_down)
            )
        _, norm_two_back = jax.vjp(layer_norm, middle[chunk], gain_two, shift_two)
        d_middle_norm, d_gain, d_shift = norm_two_back(d_normed2)
        d_gain_two, d_shift_two = d_gain_two + d_gain, d_shift_two + d_shift
        upstream = cotangent_rot[chunk * block : chunk * block + share].astype(f32)
        d_middle.append(upstream + d_middle_norm)
        own = d_middle[chunk].astype(low)
        arrived_middle.append(gather_first(own, bits))
    ready, _ = lax.optimization_barrier(((hidden, d_gate_up), own))
    grad_gate_up = dot_f32(normed2, ready[1], 0, 0).astype(low)
    feed_partial = dot_f32(ready[0], down_full, 1, 1).astype(low)
    arrived_middle[-1], _ = lax.optimization_barrier(
        (arrived_middle[-1], (grad_gate_up, feed_partial, qkv_all))
    )
    arrived_middle = [gather_rest(item, bits) for item in arrived_middle]
    for chunk in range(chunks):
        joined, sent = project_out_back(holders_at, arrived_middle[chunk], out_full, n_ctx)
        d_middle_low.append(joined)
        d_attended.append(sent)
    arrived_back = [exchange(sent) for sent in d_attended]
    back_parts = [arrived_back[chunk][s] for s in range(n_ctx) for chunk in range(chunks)]

    grad_down = lax.psum_scatter(grad_down, split, scatter_dimension=0, tiled=True)
    grad_gate_up = lax.psum_scatter(grad_gate_up, split, scatter_dimension=0, tiled=True)

    late, _ = lax.optimization_barrier((d_middle_low, arrived_back[0]))
    grad_out = over_rows(late, attended)

    kept_feed, arrived_feed = [], []
    for chunk in range(chunks):
        partial = feed_partial[chunk * block : (chunk + 1) * block]
        kept_feed.append(partial[: block // 2])
        send, _ = lax.optimization_barrier((partial[block // 2 :], d_attended))
        arrived_feed.append(sum_first(kept_feed[chunk], send))
    back_parts, arrived_feed, _ = lax.optimization_barrier((back_parts, arrived_feed, grad_out))
    output_shares = [
        (middle[chunk] + sum_further(arrived_feed[chunk], bits)).astype(low)
        for chunk in range(chunks)
    ]

    d_parts, d_groups, bias_sums, output_pieces = [], [], [], []
    for group in range(groups):
        d_group, sums = attend_back(
            slots, lengths_row, back_parts, group * lanes, *kept_attention[group], table
        )
        parts = 1 if group + 1 < groups else chunks
        arrived = []
        for part in range(parts):
            size = rows // parts
            sent = [
                d_group[s * rows + part * size : s * rows + (part + 1) * size]
                for s in range(n_ctx)
            ]
            sent, _ = lax.optimization_barrier((sent, (d_parts, arrived, output_pieces)))
            arrived.append(exchange(sent)[1:])
        d_parts.append(arrived)
        bias_sums.append(jnp.sum(sums, axis=0))
        d_groups.append(d_group)
        if group == 0:
            output_shares, _ = lax.optimization_barrier((output_shares, d_group))
            back_parts, output_shares = lax.optimization_barrier((back_parts, output_shares))
            output_pieces = gather_first(jnp.concatenate(output_shares, axis=0), bits)
    output_pieces, _ = lax.optimization_barrier((output_pieces, d_group))
    output_pieces = gather_rest(output_pieces, bits)
    partials = []
    for group in range(groups):
        after = d_group if group == 0 else d_parts[-1][0]
        late, _ = lax.optimization_barrier((normed1, after))
        partials.append(dot_f32(late, d_groups[group], 0, 0).astype(low))
    qkv_turned = [jnp.concatenate([item.T for item in items], axis=1) for items in qkv_all]
    if groups > 1:
        partials, qkv_turned, _ = lax.optimization_barrier((partials, qkv_turned, d_parts[-1]))
    d_normed1_all = []
    for chunk in range(chunks):
        parts = [(d_group, chunk * block) for d_group in d_groups]
        for s in range(1, n_ctx):
            for arrived in d_parts:
                if len(arrived) == 1:
                    parts.append((arrived[0][s - 1], chunk * block))
                else:
                    parts.append((arrived[chunk][s - 1], 0))
        keep, send = project_back(parts, qkv_turned, groups, block // 2)
        send, _ = lax.optimization_barrier((send, d_normed1_all))
        total = sum_first(keep, send)
        if chunk + 1 < chunks:
            qkv_turned, _ = lax.optimization_barrier((qkv_turned, total))
        d_normed1_all.append(sum_further(total, bits))
    output_pieces, _ = lax.optimization_barrier((output_pieces, total))
    output = place_rows(jnp.stack(quarters).astype(jnp.int32), output_pieces)
    d_normed1_all[-1], _ = lax.optimization_barrier(
        (d_normed1_all[-1], output)
    )
    token_pieces, token_shares = [], []
    d_gain_one, d_shift_one = 0.0, 0.0
    for chunk in range(chunks):
        d_normed1 = d_normed1_all[chunk]
        _, norm_one_back = jax.vjp(layer_norm, tokens_own[chunk], gain_one, shift_one)
        d_input, d_gain, d_shift = norm_one_back(d_normed1)
        d_gain_one, d_shift_one = d_gain_one + d_gain, d_shift_one + d_shift
        token_shares.append((d_middle[chunk] + d_input).astype(low))
        token_pieces.append(gather_pieces(token_shares[chunk], bits))
    after = (d_normed1_all[0], d_normed1_all[-1], token_shares)
    grad_out = scatter_ring(grad_out, "dp", after)[-1]
    grad_qkv = scatter_ring(jnp.concatenate(partials, axis=1), "dp", after)[-1].astype(low)
    grad_down = grad_down.astype(f32).T
    grad_gate_up = grad_gate_up.astype(f32).reshape(-1, 2, hidden_width)
    token_pieces[-1], _ = lax.optimization_barrier((token_pieces[-1], (grad_down, grad_gate_up)))
    grad_tokens = unrotate(token_pieces)

    grad_out = scatter_ring(grad_out, "ctx")[-1]
    grad_qkv = exchange([take_block(grad_qkv, c, depth, 0) for c in holders])
    grad_qkv = jnp.stack(grad_qkv)[(me - jnp.arange(n_ctx)) % n_ctx]
    grad_qkv = (
        grad_qkv.reshape(n_ctx, depth, groups, 3, lanes)
        .transpose(1, 3, 0, 2, 4)
        .reshape(depth, 3, heads_width)
        .astype(f32)
    )

    bias_slots = jnp.zeros((n_tensor, n_ctx, groups * slab), f32)
    bias_slots = lax.dynamic_update_slice(
        bias_slots, jnp.concatenate(bias_sums)[None, None], (mine, me, 0)
    )
    small = [d_gain_one, d_shift_one, d_gain_two, d_shift_two, bias_slots.reshape(-1)]
    small, _ = lax.optimization_barrier(
        (
            jnp.concatenate(small).reshape(-1, 128),
            [items[: n_tensor // 2] for items in token_pieces],
        )
    )
    small = butterfly(small).reshape(-1)
    norms = [small[index * features : (index + 1) * features] for index in range(4)]
    bias_sum = take_block(small[4 * features :].reshape(n_tensor, -1), mine, 1, 0)
    bias_sum = (
        bias_sum.reshape(n_ctx, groups, 3, lanes).transpose(2, 0, 1, 3).reshape(3, heads_width)
    )
    return (
        output,
        grad_tokens,
        norms[0],
        norms[1],
        grad_qkv,
        bias_sum,
        grad_out.T,
        norms[2],
        norms[3],
        grad_gate_up,
        grad_down,
    )


def solution(mesh):
    placed = (
        P(("dp", "ctx"), None),
        P(("dp", "ctx"), None),
        P("dp", None),
        P("dp", None),
        P(),
        P(),
        P(("dp", "ctx"), None, "tensor"),
        P(None, "tensor"),
        P("tensor", ("dp", "ctx")),
        P(),
        P(),
        P(("dp", "ctx"), None, "tensor"),
        P("tensor", ("dp", "ctx")),
    )
    return jax.shard_map(
        body,
        mesh=mesh,
        in_specs=placed,
        out_specs=(
            P(("dp", "ctx"), None),
            P(("dp", "ctx"), None),
            P(),
            P(),
            P(("dp", "ctx"), None, "tensor"),
            P(None, "tensor"),
            P("tensor", ("dp", "ctx")),
            P(),
            P(),
            P(("dp", "ctx"), None, "tensor"),
            P("tensor", ("dp", "ctx")),
        ),
        check_vma=False,
    )
```

```python
import functools
import math

import jax
import jax.numpy as jnp
from jax import lax
from jax.experimental import pallas as pl
from jax.experimental.pallas import tpu as pltpu
from jax.sharding import PartitionSpec as P

HD = 64
ROT = 16
TILE = 128
VMEM_LIMIT = 60 * 1024 * 1024
LOW_SCORE = -1e30
START_TOP = -1e20


def layer_norm(values, norm_gain, norm_shift):
    row_mean = jnp.mean(values, axis=-1, keepdims=True)
    centred = values - row_mean
    spread = jnp.mean(centred * centred, axis=-1, keepdims=True)
    return centred * lax.rsqrt(spread + 1e-05) * norm_gain + norm_shift


def dot_f32(left, right, left_dim, right_dim):
    return lax.dot_general(
        left, right, (((left_dim,), (right_dim,)), ((), ())), preferred_element_type=jnp.float32
    )


def spin(values, cosine, sine, lanes):
    if lanes % 128 == 0:
        ahead = pltpu.roll(values, lanes - ROT // 2, 1)
        behind = pltpu.roll(values, ROT // 2, 1)
    else:
        half_rot = ROT // 2
        ahead = jnp.concatenate([values[:, half_rot:], values[:, :half_rot]], axis=1)
        behind = jnp.concatenate([values[:, -half_rot:], values[:, :-half_rot]], axis=1)
    lane = lax.broadcasted_iota(jnp.int32, values.shape, 1) % HD
    return values * cosine + jnp.where(lane < ROT // 2, ahead, behind) * sine


def begin_of(places, len_ref, seqs):
    begin = jnp.zeros_like(places)
    end = jnp.int32(0)
    for index in range(seqs):
        end = end + len_ref[index]
        begin = jnp.where(places >= end, end, begin)
    return begin


def begin_scalar(place, len_ref, seqs):
    begin = jnp.int32(0)
    end = jnp.int32(0)
    for index in range(seqs):
        end = end + len_ref[index]
        begin = jnp.where(place >= end, end, begin)
    return begin


def finish_scalar(place, len_ref, seqs):
    finish = jnp.int32(0)
    end = jnp.int32(0)
    for index in range(seqs):
        finish = jnp.where(place >= end, end + len_ref[index], finish)
        end = end + len_ref[index]
    return finish


def fold_rows(values):
    return jnp.sum(values.reshape(-1, 8, values.shape[1]), axis=0)


def head_masks(rows, lanes, heads):
    lane = lax.broadcasted_iota(jnp.int32, (rows, lanes), 1)
    return [(lane // HD) == index for index in range(heads)]


def attend_kernel(parts, tiles, width, stream, seqs, block, slot_ref, len_ref, *refs):
    qkv_ref, cos_ref, sin_ref = refs[:3]
    out_parts = refs[3 : parts + 3]
    sorted_ref, mixed_ref, lse_ref = refs[parts + 3 : parts + 6]
    loaded, value_aug, load_sem, store_sem = refs[parts + 6 :]
    lanes = min(128, width)
    per_group = lanes // HD
    groups = width // lanes

    @pl.loop(0, parts * tiles)
    def _(tile):
        place = pl.multiple_of(slot_ref[tile] * TILE, TILE)
        row = pl.multiple_of(tile * TILE, TILE)
        pltpu.make_async_copy(
            qkv_ref.at[pl.ds(row, TILE)], loaded.at[pl.ds(place, TILE)], load_sem
        ).start()

    pltpu.make_async_copy(loaded, loaded, load_sem).wait()

    @pl.loop(0, stream // 256)
    def _(step):
        rows = pl.ds(pl.multiple_of(step * 256, 256), 256)
        cosine, sine = cos_ref[rows, :], sin_ref[rows, :]
        masks = head_masks(256, lanes, per_group)
        for group in range(groups):
            cols = slice(group * lanes, (group + 1) * lanes)
            query = spin(loaded[rows, cols].astype(jnp.float32), cosine, sine, lanes)
            query = query.astype(jnp.bfloat16) * jnp.bfloat16(HD**-0.5)
            sorted_ref[rows, cols] = query
            cols = slice(width + group * lanes, width + (group + 1) * lanes)
            key = spin(loaded[rows, cols].astype(jnp.float32), cosine, sine, lanes)
            sorted_ref[rows, cols] = key.astype(jnp.bfloat16)
            cols = slice(2 * width + group * lanes, 2 * width + (group + 1) * lanes)
            value = loaded[rows, cols]
            sorted_ref[rows, cols] = value
            ones = jnp.ones((256, lanes), jnp.bfloat16)
            for index in range(per_group):
                head = group * per_group + index
                if per_group == 2:
                    value_aug[rows, head * 128 : (head + 1) * 128] = jnp.where(
                        masks[index], value, ones
                    )
                else:
                    value_aug[rows, head * 128 : head * 128 + HD] = value
                    value_aug[rows, head * 128 + HD : (head + 1) * 128] = ones

    for group in range(groups):
        cols = slice(group * lanes, (group + 1) * lanes)
        key_cols = slice(width + group * lanes, width + (group + 1) * lanes)

        @pl.loop(0, stream // block)
        def _(index):
            first = index * block
            rows = pl.ds(pl.multiple_of(first, block), block)
            query = sorted_ref[rows, cols]
            masks = head_masks(block, lanes, per_group)
            query_heads = [jnp.where(mask, query, jnp.bfloat16(0)) for mask in masks]
            place = first + lax.broadcasted_iota(jnp.int32, (block, 1), 0)
            begin = begin_of(place, len_ref, seqs)
            begin_low = begin_scalar(first, len_ref, seqs)
            begin_high = begin_scalar(first + block - 1, len_ref, seqs)

            def step(number, carry, masked):
                start = number * block
                key_rows = pl.ds(pl.multiple_of(start, block), block)
                key = sorted_ref[key_rows, key_cols]
                out = []
                for which in range(per_group):
                    top, total = carry[which]
                    head = group * per_group + which
                    scores = dot_f32(query_heads[which], key, 1, 1)
                    if masked:
                        key_place = start + lax.broadcasted_iota(jnp.int32, (1, block), 1)
                        visible = (key_place <= place) & (key_place >= begin)
                        scores = jnp.where(visible, scores, LOW_SCORE)
                    new_top = jnp.maximum(top, jnp.max(scores, axis=1, keepdims=True))
                    expw = jnp.exp(scores - new_top).astype(jnp.bfloat16)
                    shrink = jnp.exp(top - new_top)
                    mixed = dot_f32(
                        expw, value_aug[key_rows, head * 128 : (head + 1) * 128], 1, 0
                    )
                    out.append((new_top, total * shrink + mixed))
                return tuple(out)

            carry = tuple(
                (jnp.full((block, 1), START_TOP, jnp.float32), jnp.zeros((block, 128), jnp.float32))
                for _ in range(per_group)
            )
            first_block = begin_low // block
            inner = jnp.minimum((begin_high + block - 1) // block, index)
            carry = lax.fori_loop(
                first_block, inner, functools.partial(step, masked=True), carry
            )
            carry = lax.fori_loop(inner, index, functools.partial(step, masked=False), carry)
            carry = step(index, carry, True)
            lane = lax.broadcasted_iota(jnp.int32, (block, 128), 1)
            mixed, logs = [], []
            for which in range(per_group):
                top, total = carry[which]
                swapped = pltpu.roll(total, HD, 1)
                own = (lane // HD) == which
                sums = jnp.where(own, swapped, total)
                mixed.append(total / sums)
                logs.append(top + jnp.log(sums))
            if per_group == 2:
                both = jnp.where(lane < HD, mixed[0], mixed[1])
                log_both = jnp.where(lane < HD, logs[0], logs[1])
            else:
                both = mixed[0][:, :HD]
                log_both = logs[0]
            mixed_ref[rows, cols] = both.astype(jnp.bfloat16)
            turned = jnp.transpose(log_both)
            for which in range(per_group):
                head = group * per_group + which
                lse_ref[head : head + 1, rows] = turned[which * HD : which * HD + 1, :]

    for part in range(parts):

        @pl.loop(0, tiles)
        def _(tile, part=part):
            place = pl.multiple_of(slot_ref[part * tiles + tile] * TILE, TILE)
            row = pl.multiple_of(tile * TILE, TILE)
            pltpu.make_async_copy(
                mixed_ref.at[pl.ds(place, TILE)], out_parts[part].at[pl.ds(row, TILE)], store_sem
            ).start()

    pltpu.make_async_copy(mixed_ref, mixed_ref, store_sem).wait()


def attend(slots, lengths, projected, tables, count):
    stream, triple = projected.shape
    rows = stream // count
    width = triple // 3
    heads = width // HD
    block = min(512, stream)
    anywhere = pl.BlockSpec(memory_space=pl.ANY)
    whole = pl.BlockSpec(memory_space=pltpu.VMEM)
    kernel = functools.partial(
        attend_kernel, count, rows // TILE, width, stream, lengths.shape[0], block
    )
    pairs = stream * stream // 3 * heads
    outs = pl.pallas_call(
        kernel,
        name="attention_forward",
        out_shape=[jax.ShapeDtypeStruct((rows, width), jnp.bfloat16)] * count
        + [
            jax.ShapeDtypeStruct((stream, triple), jnp.bfloat16),
            jax.ShapeDtypeStruct((stream, width), jnp.bfloat16),
            jax.ShapeDtypeStruct((max(heads, 8), stream), jnp.float32),
        ],
        in_specs=[pl.BlockSpec(memory_space=pltpu.SMEM)] * 2 + [anywhere, whole, whole],
        out_specs=[anywhere] * count + [whole] * 3,
        scratch_shapes=[
            pltpu.VMEM((stream, triple), jnp.bfloat16),
            pltpu.VMEM((stream, heads * 128), jnp.bfloat16),
            pltpu.SemaphoreType.DMA,
            pltpu.SemaphoreType.DMA,
        ],
        compiler_params=pltpu.CompilerParams(vmem_limit_bytes=VMEM_LIMIT),
        cost_estimate=pl.CostEstimate(
            flops=pairs * 4 * 256, bytes_accessed=stream * width * 20, transcendentals=pairs
        ),
    )(slots, lengths, projected, *tables)
    return outs[:count], outs[count], outs[count + 1], outs[count + 2]


def attend_back_kernel(
    given, column, width, stream, seqs, block, slot_ref, len_ref, *refs
):
    back_parts = refs[:given]
    sorted_ref, mixed_ref, lse_ref, cos_ref, sin_ref, out_ref, sums_ref = refs[given : given + 7]
    back, grads, query_grad, delta, load_sem, store_sem = refs[given + 7 :]
    given_tiles = stream // TILE // given
    lanes = min(128, width)
    per_group = lanes // HD
    groups = width // lanes
    for part in range(given):

        @pl.loop(0, given_tiles)
        def _(tile, part=part):
            place = pl.multiple_of(slot_ref[part * given_tiles + tile] * TILE, TILE)
            row = pl.multiple_of(tile * TILE, TILE)
            pltpu.make_async_copy(
                back_parts[part].at[pl.ds(row, TILE), pl.ds(column, width)],
                back.at[pl.ds(place, TILE)],
                load_sem,
            ).start()

    pltpu.make_async_copy(back, back, load_sem).wait()

    for group in range(groups):
        cols = slice(group * lanes, (group + 1) * lanes)
        key_cols = slice(width + group * lanes, width + (group + 1) * lanes)
        value_cols = slice(2 * width + group * lanes, 2 * width + (group + 1) * lanes)
        query_grad[...] = jnp.zeros_like(query_grad)
        sums_ref[...] = jnp.zeros_like(sums_ref)

        @pl.loop(0, stream // block)
        def _(index):
            rows = pl.ds(pl.multiple_of(index * block, block), block)
            product = back[rows, cols].astype(jnp.float32) * mixed_ref[rows, cols].astype(
                jnp.float32
            )
            pick = (
                lax.broadcasted_iota(jnp.int32, (8, lanes), 1) // HD
                == lax.broadcasted_iota(jnp.int32, (8, lanes), 0)
            ).astype(jnp.float32)
            delta[:, rows] = lax.dot_general(
                pick,
                product,
                (((1,), (1,)), ((), ())),
                precision=lax.Precision.HIGHEST,
                preferred_element_type=jnp.float32,
            )

        @pl.loop(0, stream // block)
        def _(index):
            first = index * block
            key_rows = pl.ds(pl.multiple_of(first, block), block)
            key = sorted_ref[key_rows, key_cols]
            value = sorted_ref[key_rows, value_cols]
            masks = head_masks(block, lanes, per_group)
            key_heads = [jnp.where(mask, key, jnp.bfloat16(0)) for mask in masks]
            key_place = first + lax.broadcasted_iota(jnp.int32, (block, 1), 0)
            finish_low = finish_scalar(first, len_ref, seqs)
            finish_high = finish_scalar(first + block - 1, len_ref, seqs)

            def step(number, carry, masked):
                key_grad, value_grad = carry
                start = number * block
                rows = pl.ds(pl.multiple_of(start, block), block)
                query = sorted_ref[rows, cols]
                upstream = back[rows, cols]
                query_add = None
                if masked:
                    place = start + lax.broadcasted_iota(jnp.int32, (1, block), 1)
                    begin = begin_of(place, len_ref, seqs)
                    visible = (key_place <= place) & (key_place >= begin)
                for which in range(per_group):
                    head = group * per_group + which
                    query_head = jnp.where(masks[which], query, jnp.bfloat16(0))
                    back_head = jnp.where(masks[which], upstream, jnp.bfloat16(0))
                    scores = dot_f32(key, query_head, 1, 1)
                    if masked:
                        scores = jnp.where(visible, scores, LOW_SCORE)
                    chances = jnp.exp(scores - lse_ref[head : head + 1, rows])
                    d_chances = dot_f32(value, back_head, 1, 1)
                    d_raw = (chances * (d_chances - delta[which : which + 1, rows])).astype(
                        jnp.bfloat16
                    )
                    value_grad = value_grad + dot_f32(
                        chances.astype(jnp.bfloat16), back_head, 1, 0
                    )
                    key_grad = key_grad + dot_f32(d_raw, query_head, 1, 0)
                    part_add = dot_f32(d_raw, key_heads[which], 0, 0)
                    query_add = part_add if query_add is None else query_add + part_add
                query_grad[rows, :] += query_add
                return (key_grad, value_grad)

            zeros = jnp.zeros((block, lanes), jnp.float32)
            carry = step(index, (zeros, zeros), True)
            inner = jnp.maximum(finish_low // block, index + 1)
            last = jnp.maximum((finish_high + block - 1) // block, inner)
            carry = lax.fori_loop(
                index + 1, inner, functools.partial(step, masked=False), carry
            )
            carry = lax.fori_loop(inner, last, functools.partial(step, masked=True), carry)
            key_grad = spin(carry[0], cos_ref[key_rows, :], -sin_ref[key_rows, :], lanes)
            grads[key_rows, key_cols] = key_grad.astype(jnp.bfloat16)
            grads[key_rows, value_cols] = carry[1].astype(jnp.bfloat16)
            sums_ref[:, key_cols] += fold_rows(key_grad)
            sums_ref[:, value_cols] += fold_rows(carry[1])

        @pl.loop(0, stream // 256)
        def _(step):
            rows = pl.ds(pl.multiple_of(step * 256, 256), 256)
            turned = spin(query_grad[rows, :], cos_ref[rows, :], -sin_ref[rows, :], lanes)
            turned = turned * (HD**-0.5)
            grads[rows, cols] = turned.astype(jnp.bfloat16)
            sums_ref[:, cols] += fold_rows(turned)

    @pl.loop(0, stream // TILE)
    def _(tile):
        place = pl.multiple_of(slot_ref[tile] * TILE, TILE)
        row = pl.multiple_of(tile * TILE, TILE)
        pltpu.make_async_copy(
            grads.at[pl.ds(place, TILE)], out_ref.at[pl.ds(row, TILE)], store_sem
        ).start()

    pltpu.make_async_copy(grads, grads, store_sem).wait()


def attend_back(slots, lengths, parts, column, kept, mixed, lse, tables):
    stream, width = mixed.shape
    heads = width // HD
    block = min(512, stream)
    lanes = min(128, width)
    anywhere = pl.BlockSpec(memory_space=pl.ANY)
    whole = pl.BlockSpec(memory_space=pltpu.VMEM)
    kernel = functools.partial(
        attend_back_kernel, len(parts), column, width, stream, lengths.shape[0], block
    )
    pairs = stream * stream // 3 * heads
    return pl.pallas_call(
        kernel,
        name="attention_backward",
        out_shape=[
            jax.ShapeDtypeStruct((stream, 3 * width), jnp.bfloat16),
            jax.ShapeDtypeStruct((8, 3 * width), jnp.float32),
        ],
        in_specs=[pl.BlockSpec(memory_space=pltpu.SMEM)] * 2
        + [anywhere] * len(parts)
        + [whole] * 5,
        out_specs=[anywhere, whole],
        scratch_shapes=[
            pltpu.VMEM((stream, width), jnp.bfloat16),
            pltpu.VMEM((stream, 3 * width), jnp.bfloat16),
            pltpu.VMEM((stream, lanes), jnp.float32),
            pltpu.VMEM((8, stream), jnp.float32),
            pltpu.SemaphoreType.DMA,
            pltpu.SemaphoreType.DMA,
        ],
        compiler_params=pltpu.CompilerParams(vmem_limit_bytes=VMEM_LIMIT),
        cost_estimate=pl.CostEstimate(
            flops=pairs * 10 * 256, bytes_accessed=stream * width * 20, transcendentals=pairs
        ),
    )(slots, lengths, *parts, kept, mixed, lse, *tables)


def rotary_kernel(lanes, table_ref, cos_ref, sin_ref):
    half_rot = ROT // 2
    lane = lax.broadcasted_iota(jnp.int32, (half_rot, lanes), 1) % HD
    entry = lax.broadcasted_iota(jnp.int32, (half_rot, lanes), 0)
    first, second = lane == entry, lane == entry + half_rot
    pick_cos = (first | second).astype(jnp.float32)
    pick_sin = second.astype(jnp.float32) - first.astype(jnp.float32)

    def spread(values, pick):
        return lax.dot_general(
            values,
            pick,
            (((0,), (0,)), ((), ())),
            precision=lax.Precision.HIGHEST,
            preferred_element_type=jnp.float32,
        )

    still = (lax.broadcasted_iota(jnp.int32, (1, lanes), 1) % HD >= ROT).astype(jnp.float32)
    cos_ref[...] = spread(table_ref[:half_rot, :], pick_cos) + still
    sin_ref[...] = spread(table_ref[half_rot:, :], pick_sin)


def rotary_tables(table, lanes):
    stream = table.shape[1]
    block = min(512, stream)
    return pl.pallas_call(
        functools.partial(rotary_kernel, lanes),
        name="rotary_tables",
        grid=(stream // block,),
        in_specs=[pl.BlockSpec((ROT, block), lambda step: (0, step))],
        out_specs=[pl.BlockSpec((block, lanes), lambda step: (step, 0))] * 2,
        out_shape=[jax.ShapeDtypeStruct((stream, lanes), jnp.float32)] * 2,
        cost_estimate=pl.CostEstimate(
            flops=stream * lanes * 100, bytes_accessed=stream * lanes * 8, transcendentals=0
        ),
    )(table)


def project_kernel(sources, groups, slab, map_ref, *refs):
    inputs = refs[:sources]
    gain_ref, shift_ref, weight_ref, bias_ref = refs[sources : sources + 4]
    outs = refs[len(refs) - groups - 1 :]

    def run(source):
        values = source[...].astype(jnp.float32)
        normed = layer_norm(values, gain_ref[...], shift_ref[...]).astype(jnp.bfloat16)
        outs[0][...] = normed
        result = dot_f32(normed, weight_ref[...], 1, 0) + bias_ref[...]
        for group in range(groups):
            outs[1 + group][...] = result[:, group * slab : (group + 1) * slab].astype(
                jnp.bfloat16
            )

    if sources == 1:
        run(inputs[0])
    else:
        for index in range(sources):

            @pl.when(pl.program_id(0) == index)
            def _(index=index):
                run(inputs[index])


def project(blocks, sources, gain, shift, weight, bias, groups, rows, first, kept):
    features, triple = weight.shape
    slab = triple // groups
    count = len(sources)
    steps = blocks.shape[0] if count == 1 else count
    size = math.gcd(256, sources[0].shape[0])
    kept = [] if kept is None else kept
    fixed = lambda step, order: (0, 0)
    placed = lambda step, order: (first + step, 0)
    if count == 1:
        specs = [pl.BlockSpec((size, features), lambda step, order: (order[step], 0))]
    else:
        specs = [pl.BlockSpec((size, features), fixed)] * count
    specs += [
        pl.BlockSpec((1, features), fixed),
        pl.BlockSpec((1, features), fixed),
        pl.BlockSpec((features, triple), fixed),
        pl.BlockSpec((1, triple), fixed),
    ]
    specs += [pl.BlockSpec(memory_space=pl.ANY)] * len(kept)
    work = steps * size
    return pl.pallas_call(
        functools.partial(project_kernel, count, groups, slab),
        name="norm_project",
        grid_spec=pltpu.PrefetchScalarGridSpec(
            num_scalar_prefetch=1,
            grid=(steps,),
            in_specs=specs,
            out_specs=[pl.BlockSpec((size, features), placed)]
            + [pl.BlockSpec((size, slab), placed)] * groups,
        ),
        out_shape=[jax.ShapeDtypeStruct((rows, features), jnp.bfloat16)]
        + [jax.ShapeDtypeStruct((rows, slab), jnp.bfloat16)] * groups,
        input_output_aliases={count + 5 + index: index for index in range(len(kept))},
        compiler_params=pltpu.CompilerParams(vmem_limit_bytes=VMEM_LIMIT),
        cost_estimate=pl.CostEstimate(
            flops=2 * work * features * triple,
            bytes_accessed=work * features * 4 + features * triple * 2,
            transcendentals=0,
        ),
    )(blocks, *sources, gain, shift, weight, bias, *kept)


def place_kernel(count, at_ref, *refs):
    for index in range(count):

        @pl.when(pl.program_id(0) == index)
        def _(index=index):
            refs[count][...] = refs[index][...]


def place_rows(at, pieces):
    size, features = pieces[0].shape
    count = len(pieces)
    return pl.pallas_call(
        functools.partial(place_kernel, count),
        name="place_rows",
        grid_spec=pltpu.PrefetchScalarGridSpec(
            num_scalar_prefetch=1,
            grid=(count,),
            in_specs=[once((size, features))] * count,
            out_specs=pl.BlockSpec((size, features), lambda step, order: (order[step], 0)),
        ),
        out_shape=jax.ShapeDtypeStruct((size * count, features), pieces[0].dtype),
        compiler_params=pltpu.CompilerParams(vmem_limit_bytes=VMEM_LIMIT),
        cost_estimate=pl.CostEstimate(
            flops=0, bytes_accessed=size * count * features * 4, transcendentals=0
        ),
    )(at, *pieces)


def pick_kernel(at_ref, source, out):
    out[...] = source[...]


def pick_rows(at, values, size):
    rows, features = values.shape
    return pl.pallas_call(
        pick_kernel,
        name="pick_rows",
        grid_spec=pltpu.PrefetchScalarGridSpec(
            num_scalar_prefetch=1,
            grid=(rows // size,),
            in_specs=[pl.BlockSpec((size, features), lambda step, order: (order[step], 0))],
            out_specs=pl.BlockSpec((size, features), lambda step, order: (step, 0)),
        ),
        out_shape=jax.ShapeDtypeStruct((rows, features), values.dtype),
        cost_estimate=pl.CostEstimate(
            flops=0, bytes_accessed=rows * features * 4, transcendentals=0
        ),
    )(at, values)


def once(shape):
    return pl.BlockSpec(shape, lambda *_: (0, 0), pipeline_mode=pl.Buffered(1))


def column_tiles(columns):
    return [(start, min(512, columns - start)) for start in range(0, columns, 512)]


def store_half(step, keep_ref, send_ref, cols, values):
    values = values.astype(jnp.bfloat16)

    @pl.when(step == 0)
    def _():
        send_ref[:, cols] = values

    @pl.when(step == 1)
    def _():
        keep_ref[:, cols] = values


def matmul_call(
    kernel, name, half, in_specs, out_specs, out_shape, scratch, flops, args, aliases=None
):
    bytes_moved = sum(a.size * a.dtype.itemsize for a in args)
    bytes_moved += sum(math.prod(o.shape) * o.dtype.itemsize for o in out_shape)
    return pl.pallas_call(
        kernel,
        name=name,
        grid=(2,),
        in_specs=in_specs,
        out_specs=out_specs,
        out_shape=out_shape,
        scratch_shapes=scratch,
        input_output_aliases=aliases or {},
        compiler_params=pltpu.CompilerParams(vmem_limit_bytes=VMEM_LIMIT),
        cost_estimate=pl.CostEstimate(flops=flops, bytes_accessed=bytes_moved, transcendentals=0),
    )(*args)


def low_shape(*shape):
    return jax.ShapeDtypeStruct(shape, jnp.bfloat16)


def out_kernel(count, groups, lanes, holder_ref, *refs):
    parts = refs[: count * groups]
    weight_ref, keep_ref, send_ref, attended_ref = refs[count * groups :]
    step = pl.program_id(0)
    for s in range(count):
        for c in range(count):

            @pl.when(holder_ref[s] == c)
            def _(s=s, c=c):
                for group in range(groups):
                    first = (c * groups + group) * lanes
                    attended_ref[:, first : first + lanes] = parts[s * groups + group][...]

    for start, size in column_tiles(weight_ref.shape[1]):
        cols = slice(start, start + size)
        result = dot_f32(attended_ref[...], weight_ref[:, cols], 1, 0)
        store_half(step, keep_ref, send_ref, cols, result)


def project_out(holders, parts, count, groups, weight, chunk, half):
    width, features = weight.shape
    lanes = parts[0].shape[1]
    part_spec = pl.BlockSpec((half, lanes), lambda step: (chunk * 2 + 1 - step, 0))
    return matmul_call(
        functools.partial(out_kernel, count, groups, lanes),
        "project_out",
        half,
        [pl.BlockSpec(memory_space=pltpu.SMEM)]
        + [part_spec] * len(parts)
        + [once((width, features))],
        [
            pl.BlockSpec((half, features), lambda step: (0, 0)),
            pl.BlockSpec((half, features), lambda step: (0, 0)),
            pl.BlockSpec((half, width), lambda step: (1 - step, 0)),
        ],
        [low_shape(half, features), low_shape(half, features), low_shape(2 * half, width)],
        [],
        4 * half * features * width,
        (holders, *parts, weight),
    )


def collect(step, pieces, out_ref, first_step):
    half = len(pieces) // 2
    size = pieces[0].shape[0]
    for number in range(2):

        @pl.when(step == number)
        def _(number=number):
            chosen = pieces[half:] if number == first_step else pieces[:half]
            for index, piece in enumerate(chosen):
                out_ref[index * size : (index + 1) * size, :] = piece[...]


def feed_kernel(count, hidden, joined, *refs):
    pieces = refs[:count]
    d_hidden_ref, weight_ref = refs[count : count + 2]
    refs = refs[count + 2 + joined :]
    normed_ref, hidden_ref, grad_ref, keep_ref, send_ref = refs[:5]
    weight, weight_sems, piece_sems = refs[5:]
    step = pl.program_id(0)
    size = pieces[0].shape[0]
    half = count // 2

    def piece_copy(index, number):
        row = index * size
        return pltpu.make_async_copy(
            pieces[half * (1 - number) + index],
            normed_ref.at[pl.ds(row, size)],
            piece_sems.at[index],
        )

    columns = [
        (first, width)
        for start, width in column_tiles(hidden)
        for first in (start, hidden + start)
    ]
    copies = [
        pltpu.make_async_copy(
            weight_ref.at[:, pl.ds(start, width)],
            weight.at[:, pl.ds(start, width)],
            weight_sems.at[number],
        )
        for number, (start, width) in enumerate(columns)
    ]

    @pl.when(step == 0)
    def _():
        for index in range(half):
            piece_copy(index, 0).start()
        for copy in copies:
            copy.start()
        for index in range(half):
            piece_copy(index, 0).wait()

    @pl.when(step == 1)
    def _():
        for index in range(half):
            piece_copy(index, 1).start()
        for index in range(half):
            piece_copy(index, 1).wait()

    for number, (start, width) in enumerate(column_tiles(hidden)):

        @pl.when(step == 0)
        def _(number=number):
            copies[2 * number].wait()
            copies[2 * number + 1].wait()

        gate_cols = slice(start, start + width)
        up_cols = slice(hidden + start, hidden + start + width)
        gate = dot_f32(normed_ref[...], weight[:, gate_cols], 1, 0)
        up = dot_f32(normed_ref[...], weight[:, up_cols], 1, 0)
        sigmoid = 1.0 / (1.0 + jnp.exp(-gate))
        silu = gate * sigmoid
        d_hidden = d_hidden_ref[:, gate_cols]
        hidden_ref[:, gate_cols] = (silu * up).astype(jnp.bfloat16)
        d_gate = d_hidden * up * sigmoid * (1.0 + gate * (1.0 - sigmoid))
        grad_ref[:, gate_cols] = d_gate.astype(jnp.bfloat16)
        grad_ref[:, up_cols] = (d_hidden * silu).astype(jnp.bfloat16)

    for start, width in column_tiles(weight.shape[0]):
        cols = slice(start, start + width)
        result = dot_f32(grad_ref[...], weight[cols, :], 1, 1)
        store_half(step, keep_ref, send_ref, cols, result)


def feed_forward(pieces, d_hidden, weight, rows, chunk, joined):
    share, features = pieces[0].shape
    half = share * len(pieces) // 2
    hidden = d_hidden.shape[1]
    joined_at = lambda step: (chunk * 2 + 1 - step, 0)
    anywhere = pl.BlockSpec(memory_space=pl.ANY)
    copies = 2 * len(column_tiles(hidden))
    joined = [] if joined is None else joined
    args = (*pieces, d_hidden, weight, *joined)
    return matmul_call(
        functools.partial(feed_kernel, len(pieces), hidden, len(joined)),
        "feed_forward",
        half,
        [anywhere] * len(pieces)
        + [pl.BlockSpec((half, hidden), joined_at), anywhere]
        + [anywhere] * len(joined),
        [
            pl.BlockSpec((half, features), joined_at),
            pl.BlockSpec((half, hidden), joined_at),
            pl.BlockSpec((half, 2 * hidden), joined_at),
            pl.BlockSpec((half, features), lambda step: (0, 0)),
            pl.BlockSpec((half, features), lambda step: (0, 0)),
        ],
        [
            low_shape(rows, features),
            low_shape(rows, hidden),
            low_shape(rows, 2 * hidden),
            low_shape(half, features),
            low_shape(half, features),
        ],
        [
            pltpu.VMEM((features, 2 * hidden), jnp.bfloat16),
            pltpu.SemaphoreType.DMA((copies,)),
            pltpu.SemaphoreType.DMA((len(pieces) // 2,)),
        ],
        16 * half * features * hidden,
        args,
        {len(pieces) + 2 + index: index for index in range(len(joined))},
    )


def out_back_kernel(count, pieces, width, holder_ref, *refs):
    sources = refs[:pieces]
    weight_ref, gathered_ref = refs[pieces : pieces + 2]
    outs = refs[pieces + 2 : pieces + 2 + count]
    step = pl.program_id(0)
    collect(step, sources, gathered_ref, 0)
    result = dot_f32(gathered_ref[...], weight_ref[...], 1, 0).astype(jnp.bfloat16)
    for s in range(count):
        for c in range(count):

            @pl.when(holder_ref[s] == c)
            def _(s=s, c=c):
                outs[s][...] = result[:, c * width : (c + 1) * width]


def project_out_back(holders, pieces, weight, count):
    share, features = pieces[0].shape
    half = share * len(pieces) // 2
    total = weight.shape[1]
    width = total // count
    placed = lambda step: (1 - step, 0)
    outs = matmul_call(
        functools.partial(out_back_kernel, count, len(pieces), width),
        "project_out_back",
        half,
        [pl.BlockSpec(memory_space=pltpu.SMEM)]
        + [once((share, features))] * len(pieces)
        + [once((features, total))],
        [pl.BlockSpec((half, features), placed)] + [pl.BlockSpec((half, width), placed)] * count,
        [low_shape(2 * half, features)] + [low_shape(2 * half, width)] * count,
        [],
        4 * half * features * total,
        (holders, *pieces, weight),
    )
    return outs[0], list(outs[1:])


def norm_back_kernel(count, groups, slab, *refs):
    parts = refs[: count * groups]
    weights = refs[count * groups : count * groups + count]
    keep_ref, send_ref, joined = refs[count * groups + count :]
    step = pl.program_id(0)
    if groups > 1:
        for index, part in enumerate(parts):
            joined[:, index * slab : (index + 1) * slab] = part[...]

    for start, size in column_tiles(weights[0].shape[1]):
        cols = slice(start, start + size)
        total = None
        for s in range(count):
            if groups > 1:
                left = joined[:, s * groups * slab : (s + 1) * groups * slab]
            else:
                left = parts[s][...]
            product = dot_f32(left, weights[s][:, cols], 1, 0)
            total = product if total is None else total + product
        store_half(step, keep_ref, send_ref, cols, total)


def project_back(parts, weights, groups, half):
    wide, features = weights[0].shape
    count = len(weights)
    slab = wide // groups

    def spec(first):
        return pl.BlockSpec(
            (half, slab), lambda step: (first // half + 1 - step, 0)
        )

    return matmul_call(
        functools.partial(norm_back_kernel, count, groups, slab),
        "project_back",
        half,
        [spec(first) for _, first in parts] + [once((wide, features))] * count,
        [pl.BlockSpec((half, features), lambda step: (0, 0))] * 2,
        [low_shape(half, features)] * 2,
        [pltpu.VMEM((half, count * wide), jnp.bfloat16)],
        4 * half * features * wide * count,
        (*(array for array, _ in parts), *weights),
    )


def swap_bit(values, axis, bit):
    size = lax.axis_size(axis)
    return lax.ppermute(values, axis, [(i, i ^ (1 << bit)) for i in range(size)])


def sum_over_tensor(keep, send, bits):
    return sum_further(sum_first(keep, send), bits)


def sum_first(keep, send):
    return keep.astype(jnp.float32) + swap_bit(send, "tensor", 0).astype(jnp.float32)


def sum_further(total, bits):
    for bit in range(1, bits):
        half = total.shape[0] // 2
        arrived = swap_bit(total[half:].astype(jnp.bfloat16), "tensor", bit)
        total = total[:half] + arrived.astype(jnp.float32)
    return total


def gather_pieces(own, bits):
    return gather_rest(gather_first(own, bits), bits)


def gather_first(own, bits):
    return [own, swap_bit(own, "tensor", bits - 1)]


def gather_rest(pieces, bits):
    for bit in reversed(range(bits - 1)):
        pieces = pieces + [swap_bit(piece, "tensor", bit) for piece in pieces]
    return pieces


def butterfly(values, steps, after):
    count = 0
    for axis in ("ctx", "dp", "tensor"):
        for bit in range(lax.axis_size(axis).bit_length() - 1):
            if count == steps:
                values, _ = lax.optimization_barrier((values, after))
            values = values + swap_bit(values, axis, bit)
            count += 1
    return values


def shift_over(values, axis, shift):
    size = lax.axis_size(axis)
    return lax.ppermute(values, axis, [(i, (i - shift) % size) for i in range(size)])


def exchange(pieces):
    count = len(pieces)
    arrived = [pieces[0]] + [None] * (count - 1)
    for shift in range(1, count):
        arrived[count - shift] = shift_over(pieces[shift], "ctx", shift)
    return arrived


def take_block(values, index, size, axis):
    return lax.dynamic_slice_in_dim(values, index * size, size, axis=axis)


def body(
    tokens,
    cotangent,
    lengths,
    offsets,
    ln1_gain,
    ln1_bias,
    w_qkv,
    b_qkv,
    w_out,
    ln2_gain,
    ln2_bias,
    w_gate_up,
    w_down,
):
    f32, low = jnp.float32, jnp.bfloat16
    split = ("dp", "ctx")
    n_dp, n_ctx, n_tensor = (lax.axis_size(name) for name in ("dp", "ctx", "tensor"))
    my_dp, me, mine = (lax.axis_index(name) for name in ("dp", "ctx", "tensor"))
    bits = n_tensor.bit_length() - 1
    rows, features = tokens.shape
    quarter = rows // n_tensor
    chunks = 2 if quarter % (2 * TILE) == 0 else 1
    share = quarter // chunks
    block = rows // chunks
    heads_width = w_qkv.shape[2]
    width = heads_width // n_ctx
    lanes = min(128, width)
    groups = width // lanes
    slab = 3 * lanes
    hidden_width = w_down.shape[0]
    stream = rows * n_ctx
    tiles = rows // TILE
    order = [int(format(p, f"0{bits}b")[::-1], 2) for p in range(n_tensor)]
    quarters = [mine ^ item for item in order]
    holders = [(me - s) % n_ctx for s in range(n_ctx)]

    def own_share(values, chunk):
        return lax.dynamic_slice_in_dim(values, mine * quarter + chunk * share, share, axis=0)

    def rotated_chunk(values, chunk):
        return jnp.concatenate(
            [
                lax.dynamic_slice_in_dim(values, q * quarter + chunk * share, share, axis=0)
                for q in quarters
            ],
            axis=0,
        )

    share_at = jnp.stack(
        [quarters[p] * chunks + chunk for chunk in range(chunks) for p in range(n_tensor)]
    ).astype(jnp.int32)

    def unrotate(columns):
        return place_rows(share_at, [piece for pieces in columns for piece in pieces])

    qkv_local = (
        w_qkv.reshape(-1, 3, n_ctx, groups, lanes)
        .transpose(0, 2, 3, 1, 4)
        .reshape(-1, n_ctx, groups * slab)
    )
    depth = qkv_local.shape[0]
    from_ctx = exchange(
        [lax.dynamic_index_in_dim(qkv_local, c, 1, keepdims=False) for c in holders]
    )

    piece_at = jnp.stack(
        [(my_dp + shift) % n_dp * n_ctx + c for c in holders for shift in range(n_dp)]
    ).astype(jnp.int32)

    def ring_rows(arrived):
        pieces = []
        for item in arrived:
            pieces.append(item)
            for _ in range(1, n_dp):
                item = shift_over(item, "dp", 1)
                pieces.append(item)
        return pieces

    qkv_pieces = ring_rows(from_ctx)

    peer_pieces = [[None] * chunks for _ in range(n_ctx)]
    awaited = []
    for chunk in range(chunks):
        own = own_share(tokens, chunk)
        for shift in range(1, n_ctx):
            arrived = shift_over(own, "ctx", shift)
            last = chunk + 1 == chunks
            reached = n_dp - 1 if last else min(chunk + 2, n_dp - 1)
            steps = [qkv_pieces[s * n_dp + reached] for s in range(n_ctx)]
            arrived, _ = lax.optimization_barrier((arrived, steps))
            pieces = gather_pieces(arrived, bits)
            peer_pieces[n_ctx - shift][chunk] = pieces
            awaited.append(arrived if last else pieces[: n_tensor // 2])

    def scatter_ring(partial, axis, after=()):
        size, index = lax.axis_size(axis), lax.axis_index(axis)
        deep = partial.shape[0] // size
        totals = [take_block(partial, (index + 1) % size, deep, 0)]
        for step in range(1, size):
            arrived = shift_over(totals[-1].astype(low), axis, 1)
            if step <= len(after):
                arrived, _ = lax.optimization_barrier((arrived, after[step - 1]))
            own = take_block(partial, (index + 1 + step) % size, deep, 0)
            totals.append(own.astype(f32) + arrived.astype(f32))
        return totals

    lengths_row = lengths[0]
    offsets_row = offsets[0].reshape(n_ctx, n_tensor, chunks, share // TILE)
    rotated_offsets = jnp.stack(
        [lax.dynamic_index_in_dim(offsets_row, q, 1, keepdims=False) for q in quarters], axis=2
    ).reshape(n_ctx, tiles)
    slots = (
        jnp.concatenate([take_block(rotated_offsets, c, 1, 0) for c in holders], axis=0).reshape(-1)
        // TILE
    )
    place = jnp.arange(stream, dtype=jnp.int32)
    ends = jnp.cumsum(lengths_row)
    begin = jnp.sum(jnp.where(place[None, :] >= ends[:, None], lengths_row[:, None], 0), axis=0)
    half_rot = ROT // 2
    frequency = jnp.exp(jnp.arange(half_rot, dtype=f32) * (-2.0 * math.log(10000.0) / ROT))
    angles = frequency[:, None] * (place - begin).astype(f32)[None, :]
    table = rotary_tables(jnp.concatenate([jnp.cos(angles), jnp.sin(angles)], axis=0), lanes)

    tokens_own = [own_share(tokens, chunk) for chunk in range(chunks)]
    cotangent_rot = pick_rows(share_at, cotangent, share)
    gate_up_local = w_gate_up.reshape(-1, 2 * hidden_width)
    qkv_pieces, _ = lax.optimization_barrier(
        (qkv_pieces, (awaited, table, slots, tokens_own, cotangent_rot, gate_up_local))
    )
    qkv_mine = place_rows(piece_at, qkv_pieces)
    out_full = lax.all_gather(w_out.T, split, axis=0, tiled=True)
    down_local, _ = lax.optimization_barrier((w_down.T, from_ctx))
    down_full = lax.all_gather(down_local, split, axis=0, tiled=True)
    gate_up_local, _ = lax.optimization_barrier((gate_up_local, qkv_mine))
    gate_up_full = lax.all_gather(gate_up_local, split, axis=0, tiled=True)

    gain_one, shift_one = ln1_gain.astype(f32), ln1_bias.astype(f32)
    gain_two, shift_two = ln2_gain.astype(f32), ln2_bias.astype(f32)
    bias_mine = (
        take_block(b_qkv.reshape(3, n_ctx, groups, lanes), me, 1, 1)
        .transpose(1, 2, 0, 3)
        .reshape(1, -1)
        .astype(f32)
    )
    project_args = (gain_one[None], shift_one[None], qkv_mine, bias_mine, groups, stream)
    size = math.gcd(256, rows)
    if share >= size:
        own_blocks = jnp.stack(
            [share_at * (share // size) + i for i in range(share // size)], axis=1
        ).reshape(-1)
        projected = project(own_blocks, [tokens], *project_args, 0, None)
    else:
        own_rows = jnp.concatenate([rotated_chunk(tokens, c) for c in range(chunks)], axis=0)
        projected = project(
            jnp.arange(rows // size, dtype=jnp.int32), [own_rows], *project_args, 0, None
        )
    nothing = jnp.zeros((1,), jnp.int32)
    for s in range(1, n_ctx):
        for chunk in range(chunks):
            first = (s * rows + chunk * block) // share
            projected = project(nothing, peer_pieces[s][chunk], *project_args, first, projected)
    normed1 = projected[0]

    qkv_all = [[qkv_mine]] + [None] * (n_ctx - 1)
    arrived, _ = lax.optimization_barrier((qkv_mine, projected))
    for shift in range(1, n_ctx):
        items = []
        for half in range(2):
            sent = take_block(qkv_mine, half, features // 2, 0)
            arrived = shift_over(lax.optimization_barrier((sent, arrived))[0], "ctx", shift)
            items.append(arrived)
        qkv_all[n_ctx - shift] = items

    kept_attention, arrived_mixed = [], []
    for group in range(groups):
        mixed_parts, *kept = attend(slots, lengths_row, projected[1 + group], table, n_ctx)
        kept_attention.append(kept)
        arrived_mixed.append(exchange(mixed_parts))
    arrived_mixed, _ = lax.optimization_barrier((arrived_mixed, down_full))
    holders_at = jnp.stack(holders).astype(jnp.int32)
    mixed_parts = [arrived_mixed[group][s] for s in range(n_ctx) for group in range(groups)]

    def over_rows(lefts, rights):
        total = None
        for left, right in zip(lefts, rights):
            product = dot_f32(left, right, 0, 0)
            total = product if total is None else total + product
        return total.astype(low)

    tokens_own = [item.astype(f32) for item in tokens_own]
    middle, d_middle, d_middle_low = [], [], []
    attended, arrived_normed2, arrived_middle, d_attended = [], [], [], []
    d_gain_two, d_shift_two = 0.0, 0.0
    out_turned = out_full.T
    d_hidden = dot_f32(cotangent_rot, down_full, 1, 0)
    for chunk in range(chunks):
        keep, send, joined = project_out(
            holders_at, mixed_parts, n_ctx, groups, out_turned, chunk, block // 2
        )
        attended.append(joined)
        total = tokens_own[chunk] + sum_over_tensor(keep, send, bits)
        total, _ = lax.optimization_barrier((total, d_hidden))
        middle.append(total)
        own = layer_norm(middle[chunk], gain_two, shift_two).astype(low)
        arrived_normed2.append(gather_first(own, bits))
    first_normed2 = arrived_normed2
    arrived_normed2 = [gather_rest(item, bits) for item in arrived_normed2]
    joined = None
    d_normed2_all = []
    for chunk in range(chunks):
        *joined, keep, send = feed_forward(
            arrived_normed2[chunk], d_hidden, gate_up_full, rows, chunk, joined
        )
        send, _ = lax.optimization_barrier(
            (
                send,
                (
                    d_normed2_all,
                    first_normed2[chunk + 1 : chunk + 2],
                    [items[chunk] for items in qkv_all[1:]],
                ),
            )
        )
        total = sum_first(keep, send)
        if chunk + 1 < chunks:
            arrived_normed2[chunk + 1], _ = lax.optimization_barrier(
                (arrived_normed2[chunk + 1], total)
            )
        d_normed2_all.append(sum_further(total, bits))
    normed2, hidden, d_gate_up = joined
    ready, _ = lax.optimization_barrier((hidden, total))
    grad_down = dot_f32(cotangent_rot, ready, 0, 0).astype(low)
    for chunk in range(chunks):
        d_normed2 = d_normed2_all[chunk]
        if chunk:
            d_normed2, _ = lax.optimization_barrier(
                (d_normed2, grad_down)
            )
        _, norm_two_back = jax.vjp(layer_norm, middle[chunk], gain_two, shift_two)
        d_middle_norm, d_gain, d_shift = norm_two_back(d_normed2)
        d_gain_two, d_shift_two = d_gain_two + d_gain, d_shift_two + d_shift
        upstream = cotangent_rot[chunk * block : chunk * block + share].astype(f32)
        d_middle.append(upstream + d_middle_norm)
        own = d_middle[chunk].astype(low)
        arrived_middle.append(gather_first(own, bits))
    ready, _ = lax.optimization_barrier(((hidden, d_gate_up), own))
    grad_gate_up = [
        dot_f32(normed2, ready[1][:, part * hidden_width : (part + 1) * hidden_width], 0, 0).astype(low)
        for part in range(2)
    ]
    feed_partial = dot_f32(ready[0], down_full, 1, 1).astype(low)
    arrived_middle[-1], _ = lax.optimization_barrier(
        (arrived_middle[-1], (grad_gate_up, feed_partial, qkv_all))
    )
    arrived_middle = [gather_rest(item, bits) for item in arrived_middle]
    for chunk in range(chunks):
        joined, sent = project_out_back(holders_at, arrived_middle[chunk], out_full, n_ctx)
        d_middle_low.append(joined)
        d_attended.append(sent)
    arrived_back = [exchange(sent) for sent in d_attended]
    back_parts = [arrived_back[chunk][s] for s in range(n_ctx) for chunk in range(chunks)]

    grad_down = lax.psum_scatter(grad_down, split, scatter_dimension=0, tiled=True)
    grad_gate = lax.psum_scatter(grad_gate_up[0], split, scatter_dimension=0, tiled=True)

    late, _ = lax.optimization_barrier((d_middle_low, arrived_back[0]))
    grad_out = over_rows(late, attended)

    kept_feed, arrived_feed = [], []
    for chunk in range(chunks):
        partial = feed_partial[chunk * block : (chunk + 1) * block]
        kept_feed.append(partial[: block // 2])
        send, _ = lax.optimization_barrier((partial[block // 2 :], d_attended))
        arrived_feed.append(sum_first(kept_feed[chunk], send))
    back_parts, arrived_feed, _ = lax.optimization_barrier((back_parts, arrived_feed, grad_out))
    output_shares = [
        (middle[chunk] + sum_further(arrived_feed[chunk], bits)).astype(low)
        for chunk in range(chunks)
    ]

    d_parts, d_groups, bias_sums, output_pieces = [], [], [], []
    for group in range(groups):
        d_group, sums = attend_back(
            slots, lengths_row, back_parts, group * lanes, *kept_attention[group], table
        )
        parts = 1 if group + 1 < groups else chunks
        arrived = []
        for part in range(parts):
            size = rows // parts
            sent = [
                d_group[s * rows + part * size : s * rows + (part + 1) * size]
                for s in range(n_ctx)
            ]
            sent, _ = lax.optimization_barrier((sent, (d_parts, arrived, output_pieces)))
            arrived.append(exchange(sent)[1:])
        d_parts.append(arrived)
        bias_sums.append(jnp.sum(sums, axis=0))
        d_groups.append(d_group)
        if group == 0:
            output_shares, _ = lax.optimization_barrier((output_shares, d_group))
            back_parts, output_shares = lax.optimization_barrier((back_parts, output_shares))
            output_pieces = gather_first(jnp.concatenate(output_shares, axis=0), bits)
    output_pieces, _ = lax.optimization_barrier((output_pieces, d_group))
    output_pieces = gather_rest(output_pieces, bits)
    grad_up, _ = lax.optimization_barrier((grad_gate_up[1], d_parts[-1]))
    grad_up = lax.psum_scatter(grad_up, split, scatter_dimension=0, tiled=True)

    partials = []
    for group in range(groups):
        after = d_group if group == 0 else d_parts[-1][0]
        late, _ = lax.optimization_barrier((normed1, after))
        partials.append(dot_f32(late, d_groups[group], 0, 0).astype(low))
    qkv_turned = [jnp.concatenate([item.T for item in items], axis=1) for items in qkv_all]
    if groups > 1:
        partials, qkv_turned, _ = lax.optimization_barrier((partials, qkv_turned, d_parts[-1]))
    d_normed1_all = []
    for chunk in range(chunks):
        parts = [(d_group, chunk * block) for d_group in d_groups]
        for s in range(1, n_ctx):
            for arrived in d_parts:
                if len(arrived) == 1:
                    parts.append((arrived[0][s - 1], chunk * block))
                else:
                    parts.append((arrived[chunk][s - 1], 0))
        keep, send = project_back(parts, qkv_turned, groups, block // 2)
        send, _ = lax.optimization_barrier((send, d_normed1_all))
        total = sum_first(keep, send)
        if chunk + 1 < chunks:
            qkv_turned, _ = lax.optimization_barrier((qkv_turned, total))
        d_normed1_all.append(sum_further(total, bits))
    output_pieces, _ = lax.optimization_barrier((output_pieces, total))
    output = place_rows(jnp.stack(quarters).astype(jnp.int32), output_pieces)
    d_normed1_all[-1], _ = lax.optimization_barrier(
        (d_normed1_all[-1], output)
    )
    token_pieces, token_shares = [], []
    d_gain_one, d_shift_one = 0.0, 0.0
    for chunk in range(chunks):
        d_normed1 = d_normed1_all[chunk]
        _, norm_one_back = jax.vjp(layer_norm, tokens_own[chunk], gain_one, shift_one)
        d_input, d_gain, d_shift = norm_one_back(d_normed1)
        d_gain_one, d_shift_one = d_gain_one + d_gain, d_shift_one + d_shift
        token_shares.append((d_middle[chunk] + d_input).astype(low))
        token_pieces.append(gather_pieces(token_shares[chunk], bits))
    after = (d_normed1_all[0], d_normed1_all[-1], token_shares)
    grad_out = scatter_ring(grad_out, "dp", after)[-1]
    grad_qkv = scatter_ring(jnp.concatenate(partials, axis=1), "dp", after)[-1].astype(low)
    grad_down = grad_down.astype(f32).T
    grad_gate_up = jnp.stack([grad_gate.astype(f32), grad_up.astype(f32)], axis=1)
    token_pieces[-1], _ = lax.optimization_barrier((token_pieces[-1], (grad_down, grad_gate_up)))
    grad_tokens = unrotate(token_pieces)

    grad_out = scatter_ring(grad_out, "ctx")[-1]
    grad_qkv = exchange([take_block(grad_qkv, c, depth, 0) for c in holders])
    grad_qkv = jnp.stack(grad_qkv)[(me - jnp.arange(n_ctx)) % n_ctx]
    grad_qkv = (
        grad_qkv.reshape(n_ctx, depth, groups, 3, lanes)
        .transpose(1, 3, 0, 2, 4)
        .reshape(depth, 3, heads_width)
        .astype(f32)
    )

    bias_slots = jnp.zeros((n_tensor, n_ctx, groups * slab), f32)
    bias_slots = lax.dynamic_update_slice(
        bias_slots, jnp.concatenate(bias_sums)[None, None], (mine, me, 0)
    )
    small = [d_gain_one, d_shift_one, d_gain_two, d_shift_two, bias_slots.reshape(-1)]
    small, _ = lax.optimization_barrier(
        (jnp.concatenate(small).reshape(-1, 128), token_pieces[0][: n_tensor // 2])
    )
    small = butterfly(small, 2, token_pieces[-1][: n_tensor // 2]).reshape(-1)
    norms = [small[index * features : (index + 1) * features] for index in range(4)]
    bias_sum = take_block(small[4 * features :].reshape(n_tensor, -1), mine, 1, 0)
    bias_sum = (
        bias_sum.reshape(n_ctx, groups, 3, lanes).transpose(2, 0, 1, 3).reshape(3, heads_width)
    )
    return (
        output,
        grad_tokens,
        norms[0],
        norms[1],
        grad_qkv,
        bias_sum,
        grad_out.T,
        norms[2],
        norms[3],
        grad_gate_up,
        grad_down,
    )


def solution(mesh):
    placed = (
        P(("dp", "ctx"), None),
        P(("dp", "ctx"), None),
        P("dp", None),
        P("dp", None),
        P(),
        P(),
        P(("dp", "ctx"), None, "tensor"),
        P(None, "tensor"),
        P("tensor", ("dp", "ctx")),
        P(),
        P(),
        P(("dp", "ctx"), None, "tensor"),
        P("tensor", ("dp", "ctx")),
    )
    return jax.shard_map(
        body,
        mesh=mesh,
        in_specs=placed,
        out_specs=(
            P(("dp", "ctx"), None),
            P(("dp", "ctx"), None),
            P(),
            P(),
            P(("dp", "ctx"), None, "tensor"),
            P(None, "tensor"),
            P("tensor", ("dp", "ctx")),
            P(),
            P(),
            P(("dp", "ctx"), None, "tensor"),
            P("tensor", ("dp", "ctx")),
        ),
        check_vma=False,
    )
```

```python
import functools
import math

import jax
import jax.numpy as jnp
from jax import lax
from jax.experimental import pallas as pl
from jax.experimental.pallas import tpu as pltpu
from jax.sharding import PartitionSpec as P

HD = 64
ROT = 16
TILE = 128
VMEM_LIMIT = 60 * 1024 * 1024
LOW_SCORE = -1e30
START_TOP = -1e20


def layer_norm(values, norm_gain, norm_shift):
    row_mean = jnp.mean(values, axis=-1, keepdims=True)
    centred = values - row_mean
    spread = jnp.mean(centred * centred, axis=-1, keepdims=True)
    return centred * lax.rsqrt(spread + 1e-05) * norm_gain + norm_shift


def dot_f32(left, right, left_dim, right_dim):
    return lax.dot_general(
        left, right, (((left_dim,), (right_dim,)), ((), ())), preferred_element_type=jnp.float32
    )


def spin(values, cosine, sine, lanes):
    if lanes % 128 == 0:
        ahead = pltpu.roll(values, lanes - ROT // 2, 1)
        behind = pltpu.roll(values, ROT // 2, 1)
    else:
        half_rot = ROT // 2
        ahead = jnp.concatenate([values[:, half_rot:], values[:, :half_rot]], axis=1)
        behind = jnp.concatenate([values[:, -half_rot:], values[:, :-half_rot]], axis=1)
    lane = lax.broadcasted_iota(jnp.int32, values.shape, 1) % HD
    return values * cosine + jnp.where(lane < ROT // 2, ahead, behind) * sine


def begin_of(places, len_ref, seqs):
    begin = jnp.zeros_like(places)
    end = jnp.int32(0)
    for index in range(seqs):
        end = end + len_ref[index]
        begin = jnp.where(places >= end, end, begin)
    return begin


def begin_scalar(place, len_ref, seqs):
    begin = jnp.int32(0)
    end = jnp.int32(0)
    for index in range(seqs):
        end = end + len_ref[index]
        begin = jnp.where(place >= end, end, begin)
    return begin


def finish_scalar(place, len_ref, seqs):
    finish = jnp.int32(0)
    end = jnp.int32(0)
    for index in range(seqs):
        finish = jnp.where(place >= end, end + len_ref[index], finish)
        end = end + len_ref[index]
    return finish


def fold_rows(values):
    return jnp.sum(values.reshape(-1, 8, values.shape[1]), axis=0)


def head_masks(rows, lanes, heads):
    lane = lax.broadcasted_iota(jnp.int32, (rows, lanes), 1)
    return [(lane // HD) == index for index in range(heads)]


def attend_kernel(parts, tiles, width, stream, seqs, block, slot_ref, len_ref, *refs):
    qkv_ref, cos_ref, sin_ref = refs[:3]
    out_parts = refs[3 : parts + 3]
    sorted_ref, mixed_ref, lse_ref = refs[parts + 3 : parts + 6]
    loaded, value_aug, load_sem, store_sem = refs[parts + 6 :]
    lanes = min(128, width)
    per_group = lanes // HD
    groups = width // lanes

    @pl.loop(0, parts * tiles)
    def _(tile):
        place = pl.multiple_of(slot_ref[tile] * TILE, TILE)
        row = pl.multiple_of(tile * TILE, TILE)
        pltpu.make_async_copy(
            qkv_ref.at[pl.ds(row, TILE)], loaded.at[pl.ds(place, TILE)], load_sem
        ).start()

    pltpu.make_async_copy(loaded, loaded, load_sem).wait()

    @pl.loop(0, stream // 256)
    def _(step):
        rows = pl.ds(pl.multiple_of(step * 256, 256), 256)
        cosine, sine = cos_ref[rows, :], sin_ref[rows, :]
        masks = head_masks(256, lanes, per_group)
        for group in range(groups):
            cols = slice(group * lanes, (group + 1) * lanes)
            query = spin(loaded[rows, cols].astype(jnp.float32), cosine, sine, lanes)
            query = query.astype(jnp.bfloat16) * jnp.bfloat16(HD**-0.5)
            sorted_ref[rows, cols] = query
            cols = slice(width + group * lanes, width + (group + 1) * lanes)
            key = spin(loaded[rows, cols].astype(jnp.float32), cosine, sine, lanes)
            sorted_ref[rows, cols] = key.astype(jnp.bfloat16)
            cols = slice(2 * width + group * lanes, 2 * width + (group + 1) * lanes)
            value = loaded[rows, cols]
            sorted_ref[rows, cols] = value
            ones = jnp.ones((256, lanes), jnp.bfloat16)
            for index in range(per_group):
                head = group * per_group + index
                if per_group == 2:
                    value_aug[rows, head * 128 : (head + 1) * 128] = jnp.where(
                        masks[index], value, ones
                    )
                else:
                    value_aug[rows, head * 128 : head * 128 + HD] = value
                    value_aug[rows, head * 128 + HD : (head + 1) * 128] = ones

    for group in range(groups):
        cols = slice(group * lanes, (group + 1) * lanes)
        key_cols = slice(width + group * lanes, width + (group + 1) * lanes)

        @pl.loop(0, stream // block)
        def _(index):
            first = index * block
            rows = pl.ds(pl.multiple_of(first, block), block)
            query = sorted_ref[rows, cols]
            masks = head_masks(block, lanes, per_group)
            query_heads = [jnp.where(mask, query, jnp.bfloat16(0)) for mask in masks]
            place = first + lax.broadcasted_iota(jnp.int32, (block, 1), 0)
            begin = begin_of(place, len_ref, seqs)
            begin_low = begin_scalar(first, len_ref, seqs)
            begin_high = begin_scalar(first + block - 1, len_ref, seqs)

            def step(number, carry, masked):
                start = number * block
                key_rows = pl.ds(pl.multiple_of(start, block), block)
                key = sorted_ref[key_rows, key_cols]
                out = []
                for which in range(per_group):
                    top, total = carry[which]
                    head = group * per_group + which
                    scores = dot_f32(query_heads[which], key, 1, 1)
                    if masked:
                        key_place = start + lax.broadcasted_iota(jnp.int32, (1, block), 1)
                        visible = (key_place <= place) & (key_place >= begin)
                        scores = jnp.where(visible, scores, LOW_SCORE)
                    new_top = jnp.maximum(top, jnp.max(scores, axis=1, keepdims=True))
                    expw = jnp.exp(scores - new_top).astype(jnp.bfloat16)
                    shrink = jnp.exp(top - new_top)
                    mixed = dot_f32(
                        expw, value_aug[key_rows, head * 128 : (head + 1) * 128], 1, 0
                    )
                    out.append((new_top, total * shrink + mixed))
                return tuple(out)

            carry = tuple(
                (jnp.full((block, 1), START_TOP, jnp.float32), jnp.zeros((block, 128), jnp.float32))
                for _ in range(per_group)
            )
            first_block = begin_low // block
            inner = jnp.minimum((begin_high + block - 1) // block, index)
            carry = lax.fori_loop(
                first_block, inner, functools.partial(step, masked=True), carry
            )
            carry = lax.fori_loop(inner, index, functools.partial(step, masked=False), carry)
            carry = step(index, carry, True)
            lane = lax.broadcasted_iota(jnp.int32, (block, 128), 1)
            mixed, logs = [], []
            for which in range(per_group):
                top, total = carry[which]
                swapped = pltpu.roll(total, HD, 1)
                own = (lane // HD) == which
                sums = jnp.where(own, swapped, total)
                mixed.append(total / sums)
                logs.append(top + jnp.log(sums))
            if per_group == 2:
                both = jnp.where(lane < HD, mixed[0], mixed[1])
                log_both = jnp.where(lane < HD, logs[0], logs[1])
            else:
                both = mixed[0][:, :HD]
                log_both = logs[0]
            mixed_ref[rows, cols] = both.astype(jnp.bfloat16)
            turned = jnp.transpose(log_both)
            for which in range(per_group):
                head = group * per_group + which
                lse_ref[head : head + 1, rows] = turned[which * HD : which * HD + 1, :]

    for part in range(parts):

        @pl.loop(0, tiles)
        def _(tile, part=part):
            place = pl.multiple_of(slot_ref[part * tiles + tile] * TILE, TILE)
            row = pl.multiple_of(tile * TILE, TILE)
            pltpu.make_async_copy(
                mixed_ref.at[pl.ds(place, TILE)], out_parts[part].at[pl.ds(row, TILE)], store_sem
            ).start()

    pltpu.make_async_copy(mixed_ref, mixed_ref, store_sem).wait()


def attend(slots, lengths, projected, tables, count):
    stream, triple = projected.shape
    rows = stream // count
    width = triple // 3
    heads = width // HD
    block = min(512, stream)
    anywhere = pl.BlockSpec(memory_space=pl.ANY)
    whole = pl.BlockSpec(memory_space=pltpu.VMEM)
    kernel = functools.partial(
        attend_kernel, count, rows // TILE, width, stream, lengths.shape[0], block
    )
    pairs = stream * stream // 3 * heads
    outs = pl.pallas_call(
        kernel,
        name="attention_forward",
        out_shape=[jax.ShapeDtypeStruct((rows, width), jnp.bfloat16)] * count
        + [
            jax.ShapeDtypeStruct((stream, triple), jnp.bfloat16),
            jax.ShapeDtypeStruct((stream, width), jnp.bfloat16),
            jax.ShapeDtypeStruct((max(heads, 8), stream), jnp.float32),
        ],
        in_specs=[pl.BlockSpec(memory_space=pltpu.SMEM)] * 2 + [anywhere, whole, whole],
        out_specs=[anywhere] * count + [whole] * 3,
        scratch_shapes=[
            pltpu.VMEM((stream, triple), jnp.bfloat16),
            pltpu.VMEM((stream, heads * 128), jnp.bfloat16),
            pltpu.SemaphoreType.DMA,
            pltpu.SemaphoreType.DMA,
        ],
        compiler_params=pltpu.CompilerParams(vmem_limit_bytes=VMEM_LIMIT),
        cost_estimate=pl.CostEstimate(
            flops=pairs * 4 * 256, bytes_accessed=stream * width * 20, transcendentals=pairs
        ),
    )(slots, lengths, projected, *tables)
    return outs[:count], outs[count], outs[count + 1], outs[count + 2]


def attend_back_kernel(
    given, column, width, stream, seqs, block, slot_ref, len_ref, *refs
):
    back_parts = refs[:given]
    sorted_ref, mixed_ref, lse_ref, cos_ref, sin_ref, out_ref, sums_ref = refs[given : given + 7]
    back, grads, query_grad, delta, load_sem, store_sem = refs[given + 7 :]
    given_tiles = stream // TILE // given
    lanes = min(128, width)
    per_group = lanes // HD
    groups = width // lanes
    for part in range(given):

        @pl.loop(0, given_tiles)
        def _(tile, part=part):
            place = pl.multiple_of(slot_ref[part * given_tiles + tile] * TILE, TILE)
            row = pl.multiple_of(tile * TILE, TILE)
            pltpu.make_async_copy(
                back_parts[part].at[pl.ds(row, TILE), pl.ds(column, width)],
                back.at[pl.ds(place, TILE)],
                load_sem,
            ).start()

    pltpu.make_async_copy(back, back, load_sem).wait()

    for group in range(groups):
        cols = slice(group * lanes, (group + 1) * lanes)
        key_cols = slice(width + group * lanes, width + (group + 1) * lanes)
        value_cols = slice(2 * width + group * lanes, 2 * width + (group + 1) * lanes)
        query_grad[...] = jnp.zeros_like(query_grad)
        sums_ref[...] = jnp.zeros_like(sums_ref)

        @pl.loop(0, stream // block)
        def _(index):
            rows = pl.ds(pl.multiple_of(index * block, block), block)
            product = back[rows, cols].astype(jnp.float32) * mixed_ref[rows, cols].astype(
                jnp.float32
            )
            pick = (
                lax.broadcasted_iota(jnp.int32, (8, lanes), 1) // HD
                == lax.broadcasted_iota(jnp.int32, (8, lanes), 0)
            ).astype(jnp.float32)
            delta[:, rows] = lax.dot_general(
                pick,
                product,
                (((1,), (1,)), ((), ())),
                precision=lax.Precision.HIGHEST,
                preferred_element_type=jnp.float32,
            )

        @pl.loop(0, stream // block)
        def _(index):
            first = index * block
            key_rows = pl.ds(pl.multiple_of(first, block), block)
            key = sorted_ref[key_rows, key_cols]
            value = sorted_ref[key_rows, value_cols]
            masks = head_masks(block, lanes, per_group)
            key_heads = [jnp.where(mask, key, jnp.bfloat16(0)) for mask in masks]
            key_place = first + lax.broadcasted_iota(jnp.int32, (block, 1), 0)
            finish_low = finish_scalar(first, len_ref, seqs)
            finish_high = finish_scalar(first + block - 1, len_ref, seqs)

            def step(number, carry, masked):
                key_grad, value_grad = carry
                start = number * block
                rows = pl.ds(pl.multiple_of(start, block), block)
                query = sorted_ref[rows, cols]
                upstream = back[rows, cols]
                query_add = None
                if masked:
                    place = start + lax.broadcasted_iota(jnp.int32, (1, block), 1)
                    begin = begin_of(place, len_ref, seqs)
                    visible = (key_place <= place) & (key_place >= begin)
                for which in range(per_group):
                    head = group * per_group + which
                    query_head = jnp.where(masks[which], query, jnp.bfloat16(0))
                    back_head = jnp.where(masks[which], upstream, jnp.bfloat16(0))
                    scores = dot_f32(key, query_head, 1, 1)
                    if masked:
                        scores = jnp.where(visible, scores, LOW_SCORE)
                    chances = jnp.exp(scores - lse_ref[head : head + 1, rows])
                    d_chances = dot_f32(value, back_head, 1, 1)
                    d_raw = (chances * (d_chances - delta[which : which + 1, rows])).astype(
                        jnp.bfloat16
                    )
                    value_grad = value_grad + dot_f32(
                        chances.astype(jnp.bfloat16), back_head, 1, 0
                    )
                    key_grad = key_grad + dot_f32(d_raw, query_head, 1, 0)
                    part_add = dot_f32(d_raw, key_heads[which], 0, 0)
                    query_add = part_add if query_add is None else query_add + part_add
                query_grad[rows, :] += query_add
                return (key_grad, value_grad)

            zeros = jnp.zeros((block, lanes), jnp.float32)
            carry = step(index, (zeros, zeros), True)
            inner = jnp.maximum(finish_low // block, index + 1)
            last = jnp.maximum((finish_high + block - 1) // block, inner)
            carry = lax.fori_loop(
                index + 1, inner, functools.partial(step, masked=False), carry
            )
            carry = lax.fori_loop(inner, last, functools.partial(step, masked=True), carry)
            key_grad = spin(carry[0], cos_ref[key_rows, :], -sin_ref[key_rows, :], lanes)
            grads[key_rows, key_cols] = key_grad.astype(jnp.bfloat16)
            grads[key_rows, value_cols] = carry[1].astype(jnp.bfloat16)
            sums_ref[:, key_cols] += fold_rows(key_grad)
            sums_ref[:, value_cols] += fold_rows(carry[1])

        @pl.loop(0, stream // 256)
        def _(step):
            rows = pl.ds(pl.multiple_of(step * 256, 256), 256)
            turned = spin(query_grad[rows, :], cos_ref[rows, :], -sin_ref[rows, :], lanes)
            turned = turned * (HD**-0.5)
            grads[rows, cols] = turned.astype(jnp.bfloat16)
            sums_ref[:, cols] += fold_rows(turned)

    @pl.loop(0, stream // TILE)
    def _(tile):
        place = pl.multiple_of(slot_ref[tile] * TILE, TILE)
        row = pl.multiple_of(tile * TILE, TILE)
        pltpu.make_async_copy(
            grads.at[pl.ds(place, TILE)], out_ref.at[pl.ds(row, TILE)], store_sem
        ).start()

    pltpu.make_async_copy(grads, grads, store_sem).wait()


def attend_back(slots, lengths, parts, column, kept, mixed, lse, tables):
    stream, width = mixed.shape
    heads = width // HD
    block = min(512, stream)
    lanes = min(128, width)
    anywhere = pl.BlockSpec(memory_space=pl.ANY)
    whole = pl.BlockSpec(memory_space=pltpu.VMEM)
    kernel = functools.partial(
        attend_back_kernel, len(parts), column, width, stream, lengths.shape[0], block
    )
    pairs = stream * stream // 3 * heads
    return pl.pallas_call(
        kernel,
        name="attention_backward",
        out_shape=[
            jax.ShapeDtypeStruct((stream, 3 * width), jnp.bfloat16),
            jax.ShapeDtypeStruct((8, 3 * width), jnp.float32),
        ],
        in_specs=[pl.BlockSpec(memory_space=pltpu.SMEM)] * 2
        + [anywhere] * len(parts)
        + [whole] * 5,
        out_specs=[anywhere, whole],
        scratch_shapes=[
            pltpu.VMEM((stream, width), jnp.bfloat16),
            pltpu.VMEM((stream, 3 * width), jnp.bfloat16),
            pltpu.VMEM((stream, lanes), jnp.float32),
            pltpu.VMEM((8, stream), jnp.float32),
            pltpu.SemaphoreType.DMA,
            pltpu.SemaphoreType.DMA,
        ],
        compiler_params=pltpu.CompilerParams(vmem_limit_bytes=VMEM_LIMIT),
        cost_estimate=pl.CostEstimate(
            flops=pairs * 10 * 256, bytes_accessed=stream * width * 20, transcendentals=pairs
        ),
    )(slots, lengths, *parts, kept, mixed, lse, *tables)


def rotary_kernel(lanes, table_ref, cos_ref, sin_ref):
    half_rot = ROT // 2
    lane = lax.broadcasted_iota(jnp.int32, (half_rot, lanes), 1) % HD
    entry = lax.broadcasted_iota(jnp.int32, (half_rot, lanes), 0)
    first, second = lane == entry, lane == entry + half_rot
    pick_cos = (first | second).astype(jnp.float32)
    pick_sin = second.astype(jnp.float32) - first.astype(jnp.float32)

    def spread(values, pick):
        return lax.dot_general(
            values,
            pick,
            (((0,), (0,)), ((), ())),
            precision=lax.Precision.HIGHEST,
            preferred_element_type=jnp.float32,
        )

    still = (lax.broadcasted_iota(jnp.int32, (1, lanes), 1) % HD >= ROT).astype(jnp.float32)
    cos_ref[...] = spread(table_ref[:half_rot, :], pick_cos) + still
    sin_ref[...] = spread(table_ref[half_rot:, :], pick_sin)


def rotary_tables(table, lanes):
    stream = table.shape[1]
    block = min(512, stream)
    return pl.pallas_call(
        functools.partial(rotary_kernel, lanes),
        name="rotary_tables",
        grid=(stream // block,),
        in_specs=[pl.BlockSpec((ROT, block), lambda step: (0, step))],
        out_specs=[pl.BlockSpec((block, lanes), lambda step: (step, 0))] * 2,
        out_shape=[jax.ShapeDtypeStruct((stream, lanes), jnp.float32)] * 2,
        cost_estimate=pl.CostEstimate(
            flops=stream * lanes * 100, bytes_accessed=stream * lanes * 8, transcendentals=0
        ),
    )(table)


def project_kernel(sources, groups, slab, map_ref, *refs):
    inputs = refs[:sources]
    gain_ref, shift_ref, weight_ref, bias_ref = refs[sources : sources + 4]
    outs = refs[len(refs) - groups - 1 :]

    def run(source):
        values = source[...].astype(jnp.float32)
        normed = layer_norm(values, gain_ref[...], shift_ref[...]).astype(jnp.bfloat16)
        outs[0][...] = normed
        result = dot_f32(normed, weight_ref[...], 1, 0) + bias_ref[...]
        for group in range(groups):
            outs[1 + group][...] = result[:, group * slab : (group + 1) * slab].astype(
                jnp.bfloat16
            )

    if sources == 1:
        run(inputs[0])
    else:
        for index in range(sources):

            @pl.when(pl.program_id(0) == index)
            def _(index=index):
                run(inputs[index])


def project(blocks, sources, gain, shift, weight, bias, groups, rows, first, kept):
    features, triple = weight.shape
    slab = triple // groups
    count = len(sources)
    steps = blocks.shape[0] if count == 1 else count
    size = math.gcd(256, sources[0].shape[0])
    kept = [] if kept is None else kept
    fixed = lambda step, order: (0, 0)
    placed = lambda step, order: (first + step, 0)
    if count == 1:
        specs = [pl.BlockSpec((size, features), lambda step, order: (order[step], 0))]
    else:
        specs = [pl.BlockSpec((size, features), fixed)] * count
    specs += [
        pl.BlockSpec((1, features), fixed),
        pl.BlockSpec((1, features), fixed),
        pl.BlockSpec((features, triple), fixed),
        pl.BlockSpec((1, triple), fixed),
    ]
    specs += [pl.BlockSpec(memory_space=pl.ANY)] * len(kept)
    work = steps * size
    return pl.pallas_call(
        functools.partial(project_kernel, count, groups, slab),
        name="norm_project",
        grid_spec=pltpu.PrefetchScalarGridSpec(
            num_scalar_prefetch=1,
            grid=(steps,),
            in_specs=specs,
            out_specs=[pl.BlockSpec((size, features), placed)]
            + [pl.BlockSpec((size, slab), placed)] * groups,
        ),
        out_shape=[jax.ShapeDtypeStruct((rows, features), jnp.bfloat16)]
        + [jax.ShapeDtypeStruct((rows, slab), jnp.bfloat16)] * groups,
        input_output_aliases={count + 5 + index: index for index in range(len(kept))},
        compiler_params=pltpu.CompilerParams(vmem_limit_bytes=VMEM_LIMIT),
        cost_estimate=pl.CostEstimate(
            flops=2 * work * features * triple,
            bytes_accessed=work * features * 4 + features * triple * 2,
            transcendentals=0,
        ),
    )(blocks, *sources, gain, shift, weight, bias, *kept)


def place_kernel(count, at_ref, *refs):
    for index in range(count):

        @pl.when(pl.program_id(0) == index)
        def _(index=index):
            refs[count][...] = refs[index][...]


def place_rows(at, pieces):
    size, features = pieces[0].shape
    count = len(pieces)
    return pl.pallas_call(
        functools.partial(place_kernel, count),
        name="place_rows",
        grid_spec=pltpu.PrefetchScalarGridSpec(
            num_scalar_prefetch=1,
            grid=(count,),
            in_specs=[once((size, features))] * count,
            out_specs=pl.BlockSpec((size, features), lambda step, order: (order[step], 0)),
        ),
        out_shape=jax.ShapeDtypeStruct((size * count, features), pieces[0].dtype),
        compiler_params=pltpu.CompilerParams(vmem_limit_bytes=VMEM_LIMIT),
        cost_estimate=pl.CostEstimate(
            flops=0, bytes_accessed=size * count * features * 4, transcendentals=0
        ),
    )(at, *pieces)


def pick_kernel(at_ref, source, out):
    out[...] = source[...]


def pick_rows(at, values, size):
    rows, features = values.shape
    return pl.pallas_call(
        pick_kernel,
        name="pick_rows",
        grid_spec=pltpu.PrefetchScalarGridSpec(
            num_scalar_prefetch=1,
            grid=(rows // size,),
            in_specs=[pl.BlockSpec((size, features), lambda step, order: (order[step], 0))],
            out_specs=pl.BlockSpec((size, features), lambda step, order: (step, 0)),
        ),
        out_shape=jax.ShapeDtypeStruct((rows, features), values.dtype),
        cost_estimate=pl.CostEstimate(
            flops=0, bytes_accessed=rows * features * 4, transcendentals=0
        ),
    )(at, values)


def once(shape):
    return pl.BlockSpec(shape, lambda *_: (0, 0), pipeline_mode=pl.Buffered(1))


def column_tiles(columns):
    return [(start, min(512, columns - start)) for start in range(0, columns, 512)]


def store_half(step, keep_ref, send_ref, cols, values):
    values = values.astype(jnp.bfloat16)

    @pl.when(step == 0)
    def _():
        send_ref[:, cols] = values

    @pl.when(step == 1)
    def _():
        keep_ref[:, cols] = values


def matmul_call(
    kernel, name, half, in_specs, out_specs, out_shape, scratch, flops, args, aliases=None
):
    bytes_moved = sum(a.size * a.dtype.itemsize for a in args)
    bytes_moved += sum(math.prod(o.shape) * o.dtype.itemsize for o in out_shape)
    return pl.pallas_call(
        kernel,
        name=name,
        grid=(2,),
        in_specs=in_specs,
        out_specs=out_specs,
        out_shape=out_shape,
        scratch_shapes=scratch,
        input_output_aliases=aliases or {},
        compiler_params=pltpu.CompilerParams(vmem_limit_bytes=VMEM_LIMIT),
        cost_estimate=pl.CostEstimate(flops=flops, bytes_accessed=bytes_moved, transcendentals=0),
    )(*args)


def low_shape(*shape):
    return jax.ShapeDtypeStruct(shape, jnp.bfloat16)


def out_kernel(count, groups, lanes, holder_ref, *refs):
    parts = refs[: count * groups]
    weight_ref, keep_ref, send_ref, attended_ref = refs[count * groups :]
    step = pl.program_id(0)
    for s in range(count):
        for c in range(count):

            @pl.when(holder_ref[s] == c)
            def _(s=s, c=c):
                for group in range(groups):
                    first = (c * groups + group) * lanes
                    attended_ref[:, first : first + lanes] = parts[s * groups + group][...]

    for start, size in column_tiles(weight_ref.shape[1]):
        cols = slice(start, start + size)
        result = dot_f32(attended_ref[...], weight_ref[:, cols], 1, 0)
        store_half(step, keep_ref, send_ref, cols, result)


def project_out(holders, parts, count, groups, weight, chunk, half):
    width, features = weight.shape
    lanes = parts[0].shape[1]
    part_spec = pl.BlockSpec((half, lanes), lambda step: (chunk * 2 + 1 - step, 0))
    return matmul_call(
        functools.partial(out_kernel, count, groups, lanes),
        "project_out",
        half,
        [pl.BlockSpec(memory_space=pltpu.SMEM)]
        + [part_spec] * len(parts)
        + [once((width, features))],
        [
            pl.BlockSpec((half, features), lambda step: (0, 0)),
            pl.BlockSpec((half, features), lambda step: (0, 0)),
            pl.BlockSpec((half, width), lambda step: (1 - step, 0)),
        ],
        [low_shape(half, features), low_shape(half, features), low_shape(2 * half, width)],
        [],
        4 * half * features * width,
        (holders, *parts, weight),
    )


def collect(step, pieces, out_ref, first_step):
    half = len(pieces) // 2
    size = pieces[0].shape[0]
    for number in range(2):

        @pl.when(step == number)
        def _(number=number):
            chosen = pieces[half:] if number == first_step else pieces[:half]
            for index, piece in enumerate(chosen):
                out_ref[index * size : (index + 1) * size, :] = piece[...]


def feed_kernel(count, hidden, joined, *refs):
    pieces = refs[:count]
    d_hidden_ref, weight_ref = refs[count : count + 2]
    refs = refs[count + 2 + joined :]
    normed_ref, hidden_ref, grad_ref, keep_ref, send_ref = refs[:5]
    weight, weight_sems, piece_sems = refs[5:]
    step = pl.program_id(0)
    size = pieces[0].shape[0]
    half = count // 2

    def piece_copy(index, number):
        row = index * size
        return pltpu.make_async_copy(
            pieces[half * (1 - number) + index],
            normed_ref.at[pl.ds(row, size)],
            piece_sems.at[index],
        )

    columns = [
        (first, width)
        for start, width in column_tiles(hidden)
        for first in (start, hidden + start)
    ]
    copies = [
        pltpu.make_async_copy(
            weight_ref.at[:, pl.ds(start, width)],
            weight.at[:, pl.ds(start, width)],
            weight_sems.at[number],
        )
        for number, (start, width) in enumerate(columns)
    ]

    @pl.when(step == 0)
    def _():
        for index in range(half):
            piece_copy(index, 0).start()
        for copy in copies:
            copy.start()
        for index in range(half):
            piece_copy(index, 0).wait()

    @pl.when(step == 1)
    def _():
        for index in range(half):
            piece_copy(index, 1).start()
        for index in range(half):
            piece_copy(index, 1).wait()

    for number, (start, width) in enumerate(column_tiles(hidden)):

        @pl.when(step == 0)
        def _(number=number):
            copies[2 * number].wait()
            copies[2 * number + 1].wait()

        gate_cols = slice(start, start + width)
        up_cols = slice(hidden + start, hidden + start + width)
        gate = dot_f32(normed_ref[...], weight[:, gate_cols], 1, 0)
        up = dot_f32(normed_ref[...], weight[:, up_cols], 1, 0)
        sigmoid = 1.0 / (1.0 + jnp.exp(-gate))
        silu = gate * sigmoid
        d_hidden = d_hidden_ref[:, gate_cols]
        hidden_ref[:, gate_cols] = (silu * up).astype(jnp.bfloat16)
        d_gate = d_hidden * up * sigmoid * (1.0 + gate * (1.0 - sigmoid))
        grad_ref[:, gate_cols] = d_gate.astype(jnp.bfloat16)
        grad_ref[:, up_cols] = (d_hidden * silu).astype(jnp.bfloat16)

    for start, width in column_tiles(weight.shape[0]):
        cols = slice(start, start + width)
        result = dot_f32(grad_ref[...], weight[cols, :], 1, 1)
        store_half(step, keep_ref, send_ref, cols, result)


def feed_forward(pieces, d_hidden, weight, rows, chunk, joined):
    share, features = pieces[0].shape
    half = share * len(pieces) // 2
    hidden = d_hidden.shape[1]
    joined_at = lambda step: (chunk * 2 + 1 - step, 0)
    anywhere = pl.BlockSpec(memory_space=pl.ANY)
    copies = 2 * len(column_tiles(hidden))
    joined = [] if joined is None else joined
    args = (*pieces, d_hidden, weight, *joined)
    return matmul_call(
        functools.partial(feed_kernel, len(pieces), hidden, len(joined)),
        "feed_forward",
        half,
        [anywhere] * len(pieces)
        + [pl.BlockSpec((half, hidden), joined_at), anywhere]
        + [anywhere] * len(joined),
        [
            pl.BlockSpec((half, features), joined_at),
            pl.BlockSpec((half, hidden), joined_at),
            pl.BlockSpec((half, 2 * hidden), joined_at),
            pl.BlockSpec((half, features), lambda step: (0, 0)),
            pl.BlockSpec((half, features), lambda step: (0, 0)),
        ],
        [
            low_shape(rows, features),
            low_shape(rows, hidden),
            low_shape(rows, 2 * hidden),
            low_shape(half, features),
            low_shape(half, features),
        ],
        [
            pltpu.VMEM((features, 2 * hidden), jnp.bfloat16),
            pltpu.SemaphoreType.DMA((copies,)),
            pltpu.SemaphoreType.DMA((len(pieces) // 2,)),
        ],
        16 * half * features * hidden,
        args,
        {len(pieces) + 2 + index: index for index in range(len(joined))},
    )


def out_back_kernel(count, pieces, width, holder_ref, *refs):
    sources = refs[:pieces]
    weight_ref, gathered_ref = refs[pieces : pieces + 2]
    outs = refs[pieces + 2 : pieces + 2 + count]
    step = pl.program_id(0)
    collect(step, sources, gathered_ref, 0)
    result = dot_f32(gathered_ref[...], weight_ref[...], 1, 0).astype(jnp.bfloat16)
    for s in range(count):
        for c in range(count):

            @pl.when(holder_ref[s] == c)
            def _(s=s, c=c):
                outs[s][...] = result[:, c * width : (c + 1) * width]


def project_out_back(holders, pieces, weight, count):
    share, features = pieces[0].shape
    half = share * len(pieces) // 2
    total = weight.shape[1]
    width = total // count
    placed = lambda step: (1 - step, 0)
    outs = matmul_call(
        functools.partial(out_back_kernel, count, len(pieces), width),
        "project_out_back",
        half,
        [pl.BlockSpec(memory_space=pltpu.SMEM)]
        + [once((share, features))] * len(pieces)
        + [once((features, total))],
        [pl.BlockSpec((half, features), placed)] + [pl.BlockSpec((half, width), placed)] * count,
        [low_shape(2 * half, features)] + [low_shape(2 * half, width)] * count,
        [],
        4 * half * features * total,
        (holders, *pieces, weight),
    )
    return outs[0], list(outs[1:])


def norm_back_kernel(count, groups, slab, *refs):
    parts = refs[: count * groups]
    weights = refs[count * groups : count * groups + count]
    keep_ref, send_ref, joined = refs[count * groups + count :]
    step = pl.program_id(0)
    if groups > 1:
        for index, part in enumerate(parts):
            joined[:, index * slab : (index + 1) * slab] = part[...]

    for start, size in column_tiles(weights[0].shape[1]):
        cols = slice(start, start + size)
        total = None
        for s in range(count):
            if groups > 1:
                left = joined[:, s * groups * slab : (s + 1) * groups * slab]
            else:
                left = parts[s][...]
            product = dot_f32(left, weights[s][:, cols], 1, 0)
            total = product if total is None else total + product
        store_half(step, keep_ref, send_ref, cols, total)


def project_back(parts, weights, groups, half):
    wide, features = weights[0].shape
    count = len(weights)
    slab = wide // groups

    def spec(first):
        return pl.BlockSpec(
            (half, slab), lambda step: (first // half + 1 - step, 0)
        )

    return matmul_call(
        functools.partial(norm_back_kernel, count, groups, slab),
        "project_back",
        half,
        [spec(first) for _, first in parts] + [once((wide, features))] * count,
        [pl.BlockSpec((half, features), lambda step: (0, 0))] * 2,
        [low_shape(half, features)] * 2,
        [pltpu.VMEM((half, count * wide), jnp.bfloat16)],
        4 * half * features * wide * count,
        (*(array for array, _ in parts), *weights),
    )


def swap_bit(values, axis, bit):
    size = lax.axis_size(axis)
    return lax.ppermute(values, axis, [(i, i ^ (1 << bit)) for i in range(size)])


def sum_over_tensor(keep, send, bits):
    return sum_further(sum_first(keep, send), bits)


def sum_first(keep, send):
    return keep.astype(jnp.float32) + swap_bit(send, "tensor", 0).astype(jnp.float32)


def sum_further(total, bits):
    for bit in range(1, bits):
        half = total.shape[0] // 2
        arrived = swap_bit(total[half:].astype(jnp.bfloat16), "tensor", bit)
        total = total[:half] + arrived.astype(jnp.float32)
    return total


def gather_pieces(own, bits):
    return gather_rest(gather_first(own, bits), bits)


def gather_first(own, bits):
    return [own, swap_bit(own, "tensor", bits - 1)]


def gather_rest(pieces, bits):
    for bit in reversed(range(bits - 1)):
        pieces = pieces + [swap_bit(piece, "tensor", bit) for piece in pieces]
    return pieces


def butterfly(values, after):
    for axis in ("ctx", "dp", "tensor"):
        if axis == "tensor":
            values, _ = lax.optimization_barrier((values, after))
        for bit in range(lax.axis_size(axis).bit_length() - 1):
            values = values + swap_bit(values, axis, bit)
    return values


def shift_over(values, axis, shift):
    size = lax.axis_size(axis)
    return lax.ppermute(values, axis, [(i, (i - shift) % size) for i in range(size)])


def exchange(pieces):
    count = len(pieces)
    arrived = [pieces[0]] + [None] * (count - 1)
    for shift in range(1, count):
        arrived[count - shift] = shift_over(pieces[shift], "ctx", shift)
    return arrived


def take_block(values, index, size, axis):
    return lax.dynamic_slice_in_dim(values, index * size, size, axis=axis)


def body(
    tokens,
    cotangent,
    lengths,
    offsets,
    ln1_gain,
    ln1_bias,
    w_qkv,
    b_qkv,
    w_out,
    ln2_gain,
    ln2_bias,
    w_gate_up,
    w_down,
):
    f32, low = jnp.float32, jnp.bfloat16
    split = ("dp", "ctx")
    n_dp, n_ctx, n_tensor = (lax.axis_size(name) for name in ("dp", "ctx", "tensor"))
    my_dp, me, mine = (lax.axis_index(name) for name in ("dp", "ctx", "tensor"))
    bits = n_tensor.bit_length() - 1
    rows, features = tokens.shape
    quarter = rows // n_tensor
    chunks = 2 if quarter % (2 * TILE) == 0 else 1
    share = quarter // chunks
    block = rows // chunks
    heads_width = w_qkv.shape[2]
    width = heads_width // n_ctx
    lanes = min(128, width)
    groups = width // lanes
    slab = 3 * lanes
    hidden_width = w_down.shape[0]
    stream = rows * n_ctx
    tiles = rows // TILE
    order = [int(format(p, f"0{bits}b")[::-1], 2) for p in range(n_tensor)]
    quarters = [mine ^ item for item in order]
    holders = [(me - s) % n_ctx for s in range(n_ctx)]

    def own_share(values, chunk):
        return lax.dynamic_slice_in_dim(values, mine * quarter + chunk * share, share, axis=0)

    def rotated_chunk(values, chunk):
        return jnp.concatenate(
            [
                lax.dynamic_slice_in_dim(values, q * quarter + chunk * share, share, axis=0)
                for q in quarters
            ],
            axis=0,
        )

    share_at = jnp.stack(
        [quarters[p] * chunks + chunk for chunk in range(chunks) for p in range(n_tensor)]
    ).astype(jnp.int32)

    def unrotate(columns):
        return place_rows(share_at, [piece for pieces in columns for piece in pieces])

    qkv_local = (
        w_qkv.reshape(-1, 3, n_ctx, groups, lanes)
        .transpose(0, 2, 3, 1, 4)
        .reshape(-1, n_ctx, groups * slab)
    )
    depth = qkv_local.shape[0]
    from_ctx = exchange(
        [lax.dynamic_index_in_dim(qkv_local, c, 1, keepdims=False) for c in holders]
    )

    piece_at = jnp.stack(
        [(my_dp + shift) % n_dp * n_ctx + c for c in holders for shift in range(n_dp)]
    ).astype(jnp.int32)

    def ring_rows(arrived):
        pieces = []
        for item in arrived:
            pieces.append(item)
            for _ in range(1, n_dp):
                item = shift_over(item, "dp", 1)
                pieces.append(item)
        return pieces

    qkv_pieces = ring_rows(from_ctx)

    peer_pieces = [[None] * chunks for _ in range(n_ctx)]
    for chunk in range(chunks):
        own = own_share(tokens, chunk)
        for shift in range(1, n_ctx):
            arrived = shift_over(own, "ctx", shift)
            steps = [qkv_pieces[s * n_dp + min(chunk + 1, n_dp - 1)] for s in range(n_ctx)]
            arrived, _ = lax.optimization_barrier((arrived, steps))
            peer_pieces[n_ctx - shift][chunk] = gather_pieces(arrived, bits)

    def scatter_ring(partial, axis, after=()):
        size, index = lax.axis_size(axis), lax.axis_index(axis)
        deep = partial.shape[0] // size
        totals = [take_block(partial, (index + 1) % size, deep, 0)]
        for step in range(1, size):
            arrived = shift_over(totals[-1].astype(low), axis, 1)
            if step <= len(after):
                arrived, _ = lax.optimization_barrier((arrived, after[step - 1]))
            own = take_block(partial, (index + 1 + step) % size, deep, 0)
            totals.append(own.astype(f32) + arrived.astype(f32))
        return totals

    lengths_row = lengths[0]
    offsets_row = offsets[0].reshape(n_ctx, n_tensor, chunks, share // TILE)
    rotated_offsets = jnp.stack(
        [lax.dynamic_index_in_dim(offsets_row, q, 1, keepdims=False) for q in quarters], axis=2
    ).reshape(n_ctx, tiles)
    slots = (
        jnp.concatenate([take_block(rotated_offsets, c, 1, 0) for c in holders], axis=0).reshape(-1)
        // TILE
    )
    place = jnp.arange(stream, dtype=jnp.int32)
    ends = jnp.cumsum(lengths_row)
    begin = jnp.sum(jnp.where(place[None, :] >= ends[:, None], lengths_row[:, None], 0), axis=0)
    half_rot = ROT // 2
    frequency = jnp.exp(jnp.arange(half_rot, dtype=f32) * (-2.0 * math.log(10000.0) / ROT))
    angles = frequency[:, None] * (place - begin).astype(f32)[None, :]
    table = rotary_tables(jnp.concatenate([jnp.cos(angles), jnp.sin(angles)], axis=0), lanes)

    tokens_own = [own_share(tokens, chunk) for chunk in range(chunks)]
    cotangent_rot = pick_rows(share_at, cotangent, share)
    gate_up_local = w_gate_up.reshape(-1, 2 * hidden_width)
    peers_half = [item[: n_tensor // 2] for items in peer_pieces[1:] for item in items]
    qkv_pieces, _ = lax.optimization_barrier(
        (qkv_pieces, (peers_half, table, slots, tokens_own, cotangent_rot, gate_up_local))
    )
    qkv_mine = place_rows(piece_at, qkv_pieces)
    out_full = lax.all_gather(w_out.T, split, axis=0, tiled=True)
    down_local, _ = lax.optimization_barrier((w_down.T, from_ctx))
    down_full = lax.all_gather(down_local, split, axis=0, tiled=True)
    gate_up_local, _ = lax.optimization_barrier((gate_up_local, qkv_mine))
    gate_up_full = lax.all_gather(gate_up_local, split, axis=0, tiled=True)

    gain_one, shift_one = ln1_gain.astype(f32), ln1_bias.astype(f32)
    gain_two, shift_two = ln2_gain.astype(f32), ln2_bias.astype(f32)
    bias_mine = (
        take_block(b_qkv.reshape(3, n_ctx, groups, lanes), me, 1, 1)
        .transpose(1, 2, 0, 3)
        .reshape(1, -1)
        .astype(f32)
    )
    project_args = (gain_one[None], shift_one[None], qkv_mine, bias_mine, groups, stream)
    size = math.gcd(256, rows)
    if share >= size:
        own_blocks = jnp.stack(
            [share_at * (share // size) + i for i in range(share // size)], axis=1
        ).reshape(-1)
        projected = project(own_blocks, [tokens], *project_args, 0, None)
    else:
        own_rows = jnp.concatenate([rotated_chunk(tokens, c) for c in range(chunks)], axis=0)
        projected = project(
            jnp.arange(rows // size, dtype=jnp.int32), [own_rows], *project_args, 0, None
        )
    nothing = jnp.zeros((1,), jnp.int32)
    for s in range(1, n_ctx):
        for chunk in range(chunks):
            first = (s * rows + chunk * block) // share
            projected = project(nothing, peer_pieces[s][chunk], *project_args, first, projected)
    normed1 = projected[0]

    qkv_all = [[qkv_mine]] + [None] * (n_ctx - 1)
    arrived, _ = lax.optimization_barrier((qkv_mine, projected))
    for shift in range(1, n_ctx):
        items = []
        for half in range(2):
            sent = take_block(qkv_mine, half, features // 2, 0)
            arrived = shift_over(lax.optimization_barrier((sent, arrived))[0], "ctx", shift)
            items.append(arrived)
        qkv_all[n_ctx - shift] = items

    kept_attention, arrived_mixed = [], []
    for group in range(groups):
        mixed_parts, *kept = attend(slots, lengths_row, projected[1 + group], table, n_ctx)
        kept_attention.append(kept)
        arrived_mixed.append(exchange(mixed_parts))
    arrived_mixed, _ = lax.optimization_barrier((arrived_mixed, down_full))
    holders_at = jnp.stack(holders).astype(jnp.int32)
    mixed_parts = [arrived_mixed[group][s] for s in range(n_ctx) for group in range(groups)]

    def over_rows(lefts, rights):
        total = None
        for left, right in zip(lefts, rights):
            product = dot_f32(left, right, 0, 0)
            total = product if total is None else total + product
        return total.astype(low)

    tokens_own = [item.astype(f32) for item in tokens_own]
    middle, d_middle, d_middle_low = [], [], []
    attended, arrived_normed2, arrived_middle, d_attended = [], [], [], []
    d_gain_two, d_shift_two = 0.0, 0.0
    out_turned = out_full.T
    d_hidden = dot_f32(cotangent_rot, down_full, 1, 0)
    for chunk in range(chunks):
        keep, send, joined = project_out(
            holders_at, mixed_parts, n_ctx, groups, out_turned, chunk, block // 2
        )
        attended.append(joined)
        total = tokens_own[chunk] + sum_over_tensor(keep, send, bits)
        total, _ = lax.optimization_barrier((total, d_hidden))
        middle.append(total)
        own = layer_norm(middle[chunk], gain_two, shift_two).astype(low)
        arrived_normed2.append(gather_first(own, bits))
    first_normed2 = arrived_normed2
    arrived_normed2 = [gather_rest(item, bits) for item in arrived_normed2]
    joined = None
    d_normed2_all = []
    for chunk in range(chunks):
        *joined, keep, send = feed_forward(
            arrived_normed2[chunk], d_hidden, gate_up_full, rows, chunk, joined
        )
        send, _ = lax.optimization_barrier(
            (
                send,
                (
                    d_normed2_all,
                    first_normed2[chunk + 1 : chunk + 2],
                    [items[chunk] for items in qkv_all[1:]],
                ),
            )
        )
        total = sum_first(keep, send)
        if chunk + 1 < chunks:
            arrived_normed2[chunk + 1], _ = lax.optimization_barrier(
                (arrived_normed2[chunk + 1], total)
            )
        d_normed2_all.append(sum_further(total, bits))
    normed2, hidden, d_gate_up = joined
    ready, _ = lax.optimization_barrier((hidden, total))
    grad_down = dot_f32(cotangent_rot, ready, 0, 0).astype(low)
    for chunk in range(chunks):
        d_normed2 = d_normed2_all[chunk]
        if chunk:
            d_normed2, _ = lax.optimization_barrier(
                (d_normed2, grad_down)
            )
        _, norm_two_back = jax.vjp(layer_norm, middle[chunk], gain_two, shift_two)
        d_middle_norm, d_gain, d_shift = norm_two_back(d_normed2)
        d_gain_two, d_shift_two = d_gain_two + d_gain, d_shift_two + d_shift
        upstream = cotangent_rot[chunk * block : chunk * block + share].astype(f32)
        d_middle.append(upstream + d_middle_norm)
        own = d_middle[chunk].astype(low)
        arrived_middle.append(gather_first(own, bits))
    ready, _ = lax.optimization_barrier(((hidden, d_gate_up), own))
    grad_gate_up = dot_f32(normed2, ready[1], 0, 0).astype(low)
    feed_partial = dot_f32(ready[0], down_full, 1, 1).astype(low)
    arrived_middle[-1], _ = lax.optimization_barrier(
        (arrived_middle[-1], (grad_gate_up, feed_partial, qkv_all))
    )
    arrived_middle = [gather_rest(item, bits) for item in arrived_middle]
    for chunk in range(chunks):
        joined, sent = project_out_back(holders_at, arrived_middle[chunk], out_full, n_ctx)
        d_middle_low.append(joined)
        d_attended.append(sent)
    arrived_back = [exchange(sent) for sent in d_attended]
    back_parts = [arrived_back[chunk][s] for s in range(n_ctx) for chunk in range(chunks)]

    grad_down = lax.psum_scatter(grad_down, split, scatter_dimension=0, tiled=True)
    grad_gate_up = lax.psum_scatter(grad_gate_up, split, scatter_dimension=0, tiled=True)

    late, _ = lax.optimization_barrier((d_middle_low, arrived_back[0]))
    grad_out = over_rows(late, attended)

    kept_feed, arrived_feed = [], []
    for chunk in range(chunks):
        partial = feed_partial[chunk * block : (chunk + 1) * block]
        kept_feed.append(partial[: block // 2])
        send, _ = lax.optimization_barrier((partial[block // 2 :], d_attended))
        arrived_feed.append(sum_first(kept_feed[chunk], send))
    back_parts, arrived_feed, _ = lax.optimization_barrier((back_parts, arrived_feed, grad_out))
    output_shares = [
        (middle[chunk] + sum_further(arrived_feed[chunk], bits)).astype(low)
        for chunk in range(chunks)
    ]

    d_parts, d_groups, bias_sums, output_pieces = [], [], [], []
    for group in range(groups):
        d_group, sums = attend_back(
            slots, lengths_row, back_parts, group * lanes, *kept_attention[group], table
        )
        parts = 1 if group + 1 < groups else chunks
        arrived = []
        for part in range(parts):
            size = rows // parts
            sent = [
                d_group[s * rows + part * size : s * rows + (part + 1) * size]
                for s in range(n_ctx)
            ]
            sent, _ = lax.optimization_barrier((sent, (d_parts, arrived, output_pieces)))
            arrived.append(exchange(sent)[1:])
        d_parts.append(arrived)
        bias_sums.append(jnp.sum(sums, axis=0))
        d_groups.append(d_group)
        if group == 0:
            output_shares, _ = lax.optimization_barrier((output_shares, d_group))
            back_parts, output_shares = lax.optimization_barrier((back_parts, output_shares))
            output_pieces = gather_first(jnp.concatenate(output_shares, axis=0), bits)
    output_pieces, _ = lax.optimization_barrier((output_pieces, d_group))
    output_pieces = gather_rest(output_pieces, bits)
    partials = []
    for group in range(groups):
        after = d_group if group == 0 else d_parts[-1][0]
        late, _ = lax.optimization_barrier((normed1, after))
        partials.append(dot_f32(late, d_groups[group], 0, 0).astype(low))
    qkv_turned = [jnp.concatenate([item.T for item in items], axis=1) for items in qkv_all]
    if groups > 1:
        partials, qkv_turned, _ = lax.optimization_barrier((partials, qkv_turned, d_parts[-1]))
    d_normed1_all = []
    for chunk in range(chunks):
        parts = [(d_group, chunk * block) for d_group in d_groups]
        for s in range(1, n_ctx):
            for arrived in d_parts:
                if len(arrived) == 1:
                    parts.append((arrived[0][s - 1], chunk * block))
                else:
                    parts.append((arrived[chunk][s - 1], 0))
        keep, send = project_back(parts, qkv_turned, groups, block // 2)
        send, _ = lax.optimization_barrier((send, d_normed1_all))
        total = sum_first(keep, send)
        if chunk + 1 < chunks:
            qkv_turned, _ = lax.optimization_barrier((qkv_turned, total))
        d_normed1_all.append(sum_further(total, bits))
    output_pieces, _ = lax.optimization_barrier((output_pieces, total))
    output = place_rows(jnp.stack(quarters).astype(jnp.int32), output_pieces)
    d_normed1_all[-1], _ = lax.optimization_barrier(
        (d_normed1_all[-1], output)
    )
    token_pieces, token_shares = [], []
    d_gain_one, d_shift_one = 0.0, 0.0
    for chunk in range(chunks):
        d_normed1 = d_normed1_all[chunk]
        _, norm_one_back = jax.vjp(layer_norm, tokens_own[chunk], gain_one, shift_one)
        d_input, d_gain, d_shift = norm_one_back(d_normed1)
        d_gain_one, d_shift_one = d_gain_one + d_gain, d_shift_one + d_shift
        token_shares.append((d_middle[chunk] + d_input).astype(low))
        token_pieces.append(gather_pieces(token_shares[chunk], bits))
    after = (d_normed1_all[0], d_normed1_all[-1], token_shares)
    grad_out = scatter_ring(grad_out, "dp", after)[-1]
    grad_qkv = scatter_ring(jnp.concatenate(partials, axis=1), "dp", after)[-1].astype(low)
    grad_down = grad_down.astype(f32).T
    grad_gate_up = grad_gate_up.astype(f32).reshape(-1, 2, hidden_width)
    token_pieces[-1], _ = lax.optimization_barrier((token_pieces[-1], (grad_down, grad_gate_up)))
    grad_tokens = unrotate(token_pieces)

    grad_out = scatter_ring(grad_out, "ctx")[-1]
    grad_qkv = exchange([take_block(grad_qkv, c, depth, 0) for c in holders])
    grad_qkv = jnp.stack(grad_qkv)[(me - jnp.arange(n_ctx)) % n_ctx]
    grad_qkv = (
        grad_qkv.reshape(n_ctx, depth, groups, 3, lanes)
        .transpose(1, 3, 0, 2, 4)
        .reshape(depth, 3, heads_width)
        .astype(f32)
    )

    bias_slots = jnp.zeros((n_tensor, n_ctx, groups * slab), f32)
    bias_slots = lax.dynamic_update_slice(
        bias_slots, jnp.concatenate(bias_sums)[None, None], (mine, me, 0)
    )
    small = [d_gain_one, d_shift_one, d_gain_two, d_shift_two, bias_slots.reshape(-1)]
    small, _ = lax.optimization_barrier(
        (jnp.concatenate(small).reshape(-1, 128), token_pieces[0][: n_tensor // 2])
    )
    small = butterfly(small, token_pieces[-1][: n_tensor // 2]).reshape(-1)
    norms = [small[index * features : (index + 1) * features] for index in range(4)]
    bias_sum = take_block(small[4 * features :].reshape(n_tensor, -1), mine, 1, 0)
    bias_sum = (
        bias_sum.reshape(n_ctx, groups, 3, lanes).transpose(2, 0, 1, 3).reshape(3, heads_width)
    )
    return (
        output,
        grad_tokens,
        norms[0],
        norms[1],
        grad_qkv,
        bias_sum,
        grad_out.T,
        norms[2],
        norms[3],
        grad_gate_up,
        grad_down,
    )


def solution(mesh):
    placed = (
        P(("dp", "ctx"), None),
        P(("dp", "ctx"), None),
        P("dp", None),
        P("dp", None),
        P(),
        P(),
        P(("dp", "ctx"), None, "tensor"),
        P(None, "tensor"),
        P("tensor", ("dp", "ctx")),
        P(),
        P(),
        P(("dp", "ctx"), None, "tensor"),
        P("tensor", ("dp", "ctx")),
    )
    return jax.shard_map(
        body,
        mesh=mesh,
        in_specs=placed,
        out_specs=(
            P(("dp", "ctx"), None),
            P(("dp", "ctx"), None),
            P(),
            P(),
            P(("dp", "ctx"), None, "tensor"),
            P(None, "tensor"),
            P("tensor", ("dp", "ctx")),
            P(),
            P(),
            P(("dp", "ctx"), None, "tensor"),
            P("tensor", ("dp", "ctx")),
        ),
        check_vma=False,
    )
```
